32 devices in a mesh: parts: 2 (over x), types: 8 (over z, y), tm: 2 (over core).
Axes of the slice: x: 2, y: 2, z: 4, core: 2. Of those that a mesh axis runs over, the one named last changes fastest.
Arguments:
- counts: int32 [1024, 8192], P(('parts', 'tm'), 'types'), parts along dimension 0, may hold values from 0 to 3
- mark_value: bfloat16 [1024, 8192], P(('parts', 'tm'), 'types'), parts along dimension 0, may hold values from 0.25 to 4
- base_rate: float32 [8192], P('types'), may hold values from 0.2 to 2
- excite: bfloat16 [4, 64, 6, 128, 128], P(None, 'types'), may hold values from -0.109375 to 0.109375
- block_col: int32 [64, 6], replicated, may hold values from 0 to 63, as said below
- row_fill: int32 [64], replicated, may hold values from 2 to 6, as said below
Outputs:
- grad_excite: bfloat16 [8, 64, 6, 128, 128], P('parts', 'types', None, 'tm'), parts along dimension 0
- grad_rate: float32 [16384], P(('parts', 'types', 'tm')), parts along dimension 0
The draws below stay inside these ranges and needn't reach their ends.
There are 2 independent parts, one for each index of `parts`. The reference program is written for one: setup_inputs(seed, part) draws one part's arguments, and reference() takes and returns one part's arrays. A program takes and returns all parts, laid end to end along the dimension named above; an argument that names none is the same for every part. Nothing has to cross between parts.
Inputs may be any that keep to these rules, and one draw needn't show every extreme that they name: `block_col`: among the live blocks of the 8 block rows of one device, at most 6 name column blocks held by any one device (column block c is held by device c // 8); every device has exactly 6 such blocks from some device in every draw. `row_fill`: the first of each device's 8 block rows has all 6 blocks live.
All inputs are finite; a program needn't handle non-finite values.
Results may differ from the reference program's by a relative error of at most 0.012.
Values may be sent and summed in bfloat16 or wider, within the bound.
No kernel may reach another device: no remote copies, remote signals or barrier semaphores. Data moves between devices by JAX's collectives and lax.ppermute only.
A program may use at most 128 MiB of HBM per device.

```python
import math
import jax
import jax.numpy as jnp
from jax import lax

BLOCK = 128
BROWS_DEV = 8
SLOTS = 6
BASES = 4
K = 8192
BROWS = 64
TIME = 512
N_TYPES = 8


def draw_counts(key, part):
    key = jax.random.fold_in(key, 37)
    subkeys = jax.random.split(key, 6)
    segment_count = (TIME + 63) // 64
    bin_index = jnp.arange(TIME, dtype=jnp.int32)
    segment = bin_index // 64
    segment_shift = jax.random.randint(subkeys[0], (segment_count,), 0, 7).astype(jnp.int32)
    segment_len = jnp.left_shift(jnp.ones((segment_count,), jnp.int32), segment_shift)
    run_index = bin_index % 64 // segment_len[segment]
    market_table = 3 * jax.random.randint(subkeys[1], (segment_count, 64), 0, 2)
    market = market_table[segment, run_index].astype(jnp.int32)
    type_shift = jax.random.randint(subkeys[2], (K,), 0, 7).astype(jnp.int32)
    type_len = jnp.left_shift(jnp.ones((K,), jnp.int32), type_shift)
    offset = jax.random.randint(subkeys[3], (K,), 0, 64).astype(jnp.int32)
    regime = ((bin_index[:, None] + offset[None, :]) // type_len[None, :]).astype(jnp.int32)
    type_table = jax.random.randint(subkeys[4], (TIME + 64, K), 0, 4).astype(jnp.int32)
    own_level = jnp.take_along_axis(type_table, regime, axis=0)
    chooser = jax.random.randint(subkeys[5], (TIME, K), 0, 2)
    return jnp.where(chooser == 0, market[:, None], own_level).astype(jnp.int32)


def draw_block_col(key, part):
    key = jax.random.fold_in(key, 11)
    entries = BROWS_DEV * SLOTS
    capacity = max(2, entries // N_TYPES)
    used = (entries + capacity - 1) // capacity
    extra_reward = jax.random.randint(jax.random.fold_in(key, 1), (N_TYPES,), 0, 4)

    def one_device(dest):
        subkey = jax.random.fold_in(key, dest + 2)
        key_ranking, key_first, key_remainder, key_local = jax.random.split(subkey, 4)
        ranking_value = (jax.random.randint(key_ranking, (N_TYPES,), 0, 4096) + 4096 * extra_reward) * N_TYPES + jnp.arange(N_TYPES)
        chosen = lax.top_k(ranking_value.astype(jnp.int32), used)[1].astype(jnp.int32)
        first = jax.random.permutation(key_first, SLOTS).astype(jnp.int32)
        rest = (SLOTS + jax.random.permutation(key_remainder, entries - SLOTS)).astype(jnp.int32)
        order = jnp.concatenate([first, rest])
        source = chosen[order // capacity]
        local_block = jax.random.randint(key_local, (entries,), 0, BROWS_DEV)
        return (source * BROWS_DEV + local_block).astype(jnp.int32)
    columns = jax.vmap(one_device)(jnp.arange(N_TYPES))
    return columns.reshape(BROWS, SLOTS).astype(jnp.int32)


def draw_row_fill(key, part):
    key = jax.random.fold_in(key, 23)
    fill = jax.random.randint(key, (BROWS,), 2, SLOTS + 1)
    return jnp.where(jnp.arange(BROWS) % BROWS_DEV == 0, SLOTS, fill).astype(jnp.int32)


def block_levels(rng, dims, shards, low, high):
    def one(dim, blocks):
        steps = jax.random.uniform(jax.random.fold_in(jax.random.fold_in(rng, 6), dim), (blocks,), jnp.float32, low / len(shards), high / len(shards))
        return jnp.repeat(jnp.exp(steps), dims[dim] // blocks).reshape((-1,) + (1,) * (len(dims) - dim - 1))

    level = one(*shards[0])
    for cut in shards[1:]:
        level = level * one(*cut)
    return level


def scatter_about(rng, dims, spread, most, shards=(), held_as=jnp.bfloat16):
    result = jax.random.normal(rng, dims, jnp.float32) * spread
    if len(shards) > 0:
        result = block_levels(rng, dims, shards, -0.22, 0.18) * result
    return jnp.clip(result, min=-most, max=most).astype(held_as)


def setup_inputs(seed: int = 0, part: int = 0) -> dict:
    arg_keys = jax.random.split(jax.random.key(seed), 7)
    own_keys = jax.random.split(jax.random.fold_in(arg_keys[6], part), 7)
    counts = draw_counts(jax.random.fold_in(jax.random.fold_in(arg_keys[6], part), 71), part)
    mark_value = jnp.clip(jnp.exp(math.log(4.0) - 2.7725887 * jax.random.uniform(own_keys[1], (TIME, K), jnp.float32) ** block_levels(own_keys[1], (TIME, K), ((0, 2), (1, 8)), -0.2, 0.2)), 0.25, 4.0).astype(jnp.bfloat16)
    base_rate = jnp.clip(jnp.exp(math.log(2.0) - 2.3025851 * jax.random.uniform(arg_keys[2], (K,), jnp.float32) ** block_levels(arg_keys[2], (K,), ((0, 8),), -0.2, 0.2)), 0.2, 2.0)
    excite = scatter_about(arg_keys[3], (BASES, BROWS, SLOTS, BLOCK, BLOCK), (BASES * SLOTS * BLOCK) ** -0.5, 0.109375, ((1, 8),))
    block_col = draw_block_col(jax.random.fold_in(arg_keys[6], 71), part)
    row_fill = draw_row_fill(jax.random.fold_in(arg_keys[6], 71), part)
    return {"counts": counts, "mark_value": mark_value, "base_rate": base_rate, "excite": excite, "block_col": block_col, "row_fill": row_fill}


def reference(counts, mark_value, base_rate, excite, block_col, row_fill):
    tau_scale = 2.0 * TIME / (8.0 ** jnp.arange(BASES, dtype=jnp.float32))
    decay = jnp.exp(-1.0 / tau_scale)
    impact_bf = (counts.astype(jnp.float32) * mark_value.astype(jnp.float32)).astype(jnp.bfloat16)
    impact = lax.optimization_barrier(impact_bf).astype(jnp.float32)

    def advance(carry_state, series):
        next_state = decay[:, None] * carry_state + (1.0 - decay[:, None]) * series[None, :]
        return next_state, carry_state

    start = jnp.zeros((BASES, K), jnp.float32)
    unused, history = lax.scan(advance, start, impact)
    state_bf = jnp.transpose(history, (1, 0, 2)).astype(jnp.bfloat16).reshape(BASES, TIME, BROWS, BLOCK)
    counts_f = counts.astype(jnp.float32).reshape(TIME, BROWS, BLOCK)
    rates = base_rate.reshape(BROWS, BLOCK)

    def one_row(index):
        columns = block_col[index]
        live_mask = jnp.arange(SLOTS) < row_fill[index]
        picked = jnp.take(state_bf, columns, axis=2).astype(jnp.float32)
        picked = jnp.where(live_mask[None, None, :, None], picked, jnp.float32(0.0))
        weights = excite[:, index].astype(jnp.float32)
        excited = jnp.einsum('bspq,btsq->tp', weights, picked)
        intensity = excited + rates[index][None, :]
        weighted = (2.0 / TIME) * (intensity - counts_f[:, index])
        rate_grad = jnp.sum(weighted, axis=0)
        rounded = lax.optimization_barrier(weighted.astype(jnp.bfloat16)).astype(jnp.float32)
        excite_grad = jnp.einsum('tp,btsq->bspq', rounded, picked)
        return excite_grad.astype(jnp.bfloat16), rate_grad

    grads, rate_grads = lax.map(one_row, jnp.arange(BROWS))
    grad_excite = jnp.transpose(grads, (1, 0, 2, 3, 4))
    return grad_excite, rate_grads.reshape(K)
```

```python
import functools
import jax
import jax.numpy as jnp
from jax import lax
from jax.experimental import pallas as pl
from jax.experimental.pallas import tpu as pltpu
from jax.sharding import PartitionSpec as P


def lag_tables(bins, basis_count, overall):
    log_decay = -(8.0 ** jnp.arange(basis_count, dtype=jnp.float32)) / (2.0 * overall)
    t = jnp.arange(bins, dtype=jnp.float32)
    lag = t[:, None] - 1.0 - t[None, :]
    weights = jnp.where(
        lag[None] >= 0.0,
        (1.0 - jnp.exp(log_decay))[:, None, None]
        * jnp.exp(jnp.maximum(lag, 0.0)[None] * log_decay[:, None, None]),
        jnp.float32(0.0),
    )
    power = jnp.exp(t[None, :, None] * log_decay[:, None, None])
    return weights.astype(jnp.bfloat16), jnp.broadcast_to(power, (basis_count, bins, 128))


def prepare_kernel(basis_count, overall, counts_ref, mark_ref, impact_ref, ends_ref):
    bins = counts_ref.shape[0]
    impact = (counts_ref[...].astype(jnp.float32) * mark_ref[...].astype(jnp.float32)).astype(
        jnp.bfloat16
    )
    impact_ref[...] = impact
    impact = impact.astype(jnp.float32)
    back = (bins - 1 - lax.broadcasted_iota(jnp.int32, (bins, 1), 0)).astype(jnp.float32)
    rows = []
    for b in range(basis_count):
        rate = (8.0**b) / (2.0 * overall)
        gain = (1.0 - jnp.exp(jnp.full((bins, 1), -rate, jnp.float32))) * jnp.exp(-rate * back)
        rows.append(jnp.sum(impact * gain, axis=0, keepdims=True))
    ends_ref[...] = jnp.concatenate(rows, axis=0)


def prepare(counts, mark, basis_count, overall):
    bins, types = counts.shape
    lanes = min(types, 256)
    return pl.pallas_call(
        functools.partial(prepare_kernel, basis_count, overall),
        grid=(types // lanes,),
        in_specs=[
            pl.BlockSpec((bins, lanes), lambda i: (0, i)),
            pl.BlockSpec((bins, lanes), lambda i: (0, i)),
        ],
        out_specs=[
            pl.BlockSpec((bins, lanes), lambda i: (0, i)),
            pl.BlockSpec((basis_count, lanes), lambda i: (0, i)),
        ],
        out_shape=[
            jax.ShapeDtypeStruct((bins, types), jnp.bfloat16),
            jax.ShapeDtypeStruct((basis_count, types), jnp.float32),
        ],
        compiler_params=pltpu.CompilerParams(vmem_limit_bytes=32 << 20),
        name="impact",
    )(counts, mark)


def rows_kernel(basis, slots, brows, overall, place_ref, col_ref, fill_ref, *refs):
    blocks = refs[:slots]
    carries = refs[slots : 2 * slots]
    (excite_ref, counts_ref, base_ref, lag_ref, power_ref, mine_ref, other_ref, rate_ref, states) = (
        refs[2 * slots :]
    )
    row = pl.program_id(0)
    own, half = place_ref[0], place_ref[1]
    bins = counts_ref.shape[0]
    tile = excite_ref.shape[-1]
    depth = basis * tile
    fill = fill_ref[own * brows + row]
    excited = jnp.zeros((bins, tile), jnp.float32)

    def build(pair):
        both = jnp.concatenate([blocks[2 * pair][0], blocks[2 * pair + 1][0]], axis=1)
        for b in range(basis):
            state = jnp.dot(lag_ref[b], both, preferred_element_type=jnp.float32)
            for k in range(2):
                s = 2 * pair + k
                carried = power_ref[b] * carries[s][0, b : b + 1, :]
                states[s, :, b * tile : (b + 1) * tile] = (
                    state[:, k * tile : (k + 1) * tile] + carried
                ).astype(jnp.bfloat16)

    total = jnp.zeros((bins, tile), jnp.float32)
    for pair in range(slots // 2):
        if pair == 0:
            build(0)
        else:
            pl.when(2 * pair < fill)(functools.partial(build, pair))
    for s in range(slots):
        weights = jnp.concatenate([excite_ref[b, 0, s] for b in range(basis)], axis=1)
        live = s < fill
        weights = jnp.where(live, weights, jnp.zeros_like(weights))
        state = jnp.where(live, states[s], jnp.zeros_like(states[s]))
        total = total + lax.dot_general(
            state, weights, (((1,), (1,)), ((), ())), preferred_element_type=jnp.float32
        )
    del excited
    intensity = total + base_ref[...]
    weighted = (2.0 / overall) * (intensity - counts_ref[...].astype(jnp.float32))
    rate_ref[0] = jnp.sum(weighted, axis=0, keepdims=True)
    turned = weighted.T.astype(jnp.bfloat16)
    part = tile // 2
    first, last = turned[:part], turned[part:]
    own_first = half == 0
    turned = jnp.concatenate(
        [jnp.where(own_first, first, last), jnp.where(own_first, last, first)], axis=0
    )
    for s in range(slots):
        live = s < fill

        @pl.when(live)
        def _(s=s):
            grad = jnp.dot(turned, states[s], preferred_element_type=jnp.float32).astype(
                jnp.bfloat16
            )
            for b in range(basis):
                piece = grad[:, b * tile : (b + 1) * tile]
                mine_ref[b, 0, s] = piece[:part]
                other_ref[b, 0, s] = piece[part:]

        @pl.when(jnp.logical_not(live))
        def _(s=s):
            for b in range(basis):
                mine_ref[b, 0, s] = jnp.zeros((part, tile), jnp.bfloat16)
                other_ref[b, 0, s] = jnp.zeros((part, tile), jnp.bfloat16)


def rows(place, cols, fill, gathered, entering, excite, counts, base_rate, lag, power, overall):
    basis, brows, slots, tile, _ = excite.shape
    bins = counts.shape[0]
    width = gathered.shape[2] // tile

    def block_at(s):
        def index(i, place, cols, fill):
            c = cols[(place[0] * brows + i) * slots + s]
            return lax.div(c, width), 0, lax.rem(c, width)

        return index

    whole3 = lambda i, *_: (0, 0, 0)
    part = tile // 2
    out_block = pl.BlockSpec((basis, 1, slots, part, tile), lambda i, *_: (0, i, 0, 0, 0))
    out_shape = jax.ShapeDtypeStruct((basis, brows, slots, part, tile), jnp.bfloat16)
    return pl.pallas_call(
        functools.partial(rows_kernel, basis, slots, brows, overall),
        grid_spec=pltpu.PrefetchScalarGridSpec(
            num_scalar_prefetch=3,
            grid=(brows,),
            in_specs=[pl.BlockSpec((1, bins, tile), block_at(s)) for s in range(slots)]
            + [pl.BlockSpec((1, basis, tile), block_at(s)) for s in range(slots)]
            + [
                pl.BlockSpec((basis, 1, slots, tile, tile), lambda i, *_: (0, i, 0, 0, 0)),
                pl.BlockSpec((bins, tile), lambda i, *_: (0, i)),
                pl.BlockSpec((1, tile), lambda i, *_: (0, i)),
                pl.BlockSpec((basis, bins, bins), whole3),
                pl.BlockSpec((basis, bins, tile), whole3),
            ],
            out_specs=[out_block, out_block, pl.BlockSpec((1, 1, tile), lambda i, *_: (i, 0, 0))],
            scratch_shapes=[pltpu.VMEM((slots, bins, basis * tile), jnp.bfloat16)],
        ),
        out_shape=[out_shape, out_shape, jax.ShapeDtypeStruct((brows, 1, tile), jnp.float32)],
        compiler_params=pltpu.CompilerParams(vmem_limit_bytes=40 << 20),
        name="rows",
    )(
        place,
        cols,
        fill,
        *([gathered] * slots),
        *([entering] * slots),
        excite,
        counts,
        base_rate.reshape(1, -1),
        lag,
        power,
    )


def shards(counts, mark_value, base_rate, excite, block_col, row_fill):
    basis, brows, slots, tile, _ = excite.shape
    bins = counts.shape[0]
    overall = bins * lax.axis_size("tm")
    half = lax.axis_index("tm")
    place = jnp.stack([lax.axis_index("types"), half]).astype(jnp.int32)
    impact, ends = prepare(counts, mark_value, basis, overall)
    gathered = lax.all_gather(impact, "types")
    entering = lax.all_gather(lax.ppermute(ends, "tm", [(0, 1)]), "types")
    lag, power = lag_tables(bins, basis, overall)
    mine, other, rate = rows(
        place,
        block_col.reshape(-1),
        row_fill,
        gathered,
        entering,
        excite,
        counts,
        base_rate,
        lag,
        power,
        overall,
    )
    swap = [(0, 1), (1, 0)]
    rate = rate.reshape(2, -1)
    got = lax.ppermute(other, "tm", swap)
    rate_got = lax.ppermute(lax.dynamic_index_in_dim(rate, 1 - half, 0, False), "tm", swap)
    grad = (mine.astype(jnp.float32) + got.astype(jnp.float32)).astype(jnp.bfloat16)
    return grad, lax.dynamic_index_in_dim(rate, half, 0, False) + rate_got


def solution(mesh):
    return jax.shard_map(
        shards,
        mesh=mesh,
        in_specs=(
            P(("parts", "tm"), "types"),
            P(("parts", "tm"), "types"),
            P("types"),
            P(None, "types", None, None, None),
            P(),
            P(),
        ),
        out_specs=(P("parts", "types", None, "tm", None), P(("parts", "types", "tm"))),
        check_vma=False,
    )
```

```python
import functools
import jax
import jax.numpy as jnp
from jax import lax
from jax.experimental import pallas as pl
from jax.experimental.pallas import tpu as pltpu
from jax.sharding import PartitionSpec as P

STREAMS = 4
CARRY_ROWS = 16


def lag_tables(bins, basis_count, overall, lanes):
    log_decay = -(8.0 ** jnp.arange(basis_count, dtype=jnp.float32)) / (2.0 * overall)
    t = jnp.arange(bins, dtype=jnp.float32)
    lag = t[:, None] - 1.0 - t[None, :]
    weights = jnp.where(
        lag[None] >= 0.0,
        (1.0 - jnp.exp(log_decay))[:, None, None]
        * jnp.exp(jnp.maximum(lag, 0.0)[None] * log_decay[:, None, None]),
        jnp.float32(0.0),
    )
    power = jnp.exp(t[None, :, None] * log_decay[:, None, None])
    return weights.astype(jnp.bfloat16), jnp.broadcast_to(power, (basis_count, bins, lanes))


def impact_of(counts_ref, mark_ref, lanes):
    counts = counts_ref[:, lanes].astype(jnp.float32)
    return (counts * mark_ref[:, lanes].astype(jnp.float32)).astype(jnp.bfloat16)


def first_kernel(basis, overall, counts_ref, mark_ref, up_ref, down_ref, ends_ref):
    bins, types = counts_ref.shape
    lanes = types // STREAMS
    back = (bins - 1 - lax.broadcasted_iota(jnp.int32, (bins, 1), 0)).astype(jnp.float32)
    gains = []
    for b in range(basis):
        rate = (8.0**b) / (2.0 * overall)
        gains.append((1.0 - jnp.exp(jnp.full((bins, 1), -rate, jnp.float32))) * jnp.exp(-rate * back))
    for j in range(STREAMS):
        impact = impact_of(counts_ref, mark_ref, slice(j * lanes, (j + 1) * lanes))
        if j == 0:
            up_ref[...] = impact
        if j == 2:
            down_ref[...] = impact
        impact = impact.astype(jnp.float32)
        for b in range(basis):
            ends_ref[b : b + 1, j * lanes : (j + 1) * lanes] = jnp.sum(
                impact * gains[b], axis=0, keepdims=True
            )


def second_kernel(basis, counts_ref, mark_ref, enter_ref, up_ref, down_ref):
    bins, types = counts_ref.shape
    lanes = types // STREAMS
    for j, out_ref in ((1, up_ref), (3, down_ref)):
        out_ref[:bins] = impact_of(counts_ref, mark_ref, slice(j * lanes, (j + 1) * lanes))
        carry = jnp.concatenate(
            [enter_ref[:, (j - 1) * lanes : j * lanes], enter_ref[:, j * lanes : (j + 1) * lanes]],
            axis=0,
        )
        pad = jnp.zeros((CARRY_ROWS - 2 * basis, lanes), jnp.float32)
        out_ref[bins:] = jnp.concatenate([carry, pad], axis=0).astype(jnp.bfloat16)


def first(counts, mark, basis, overall):
    bins, types = counts.shape
    chunk = jax.ShapeDtypeStruct((bins, types // STREAMS), jnp.bfloat16)
    return pl.pallas_call(
        functools.partial(first_kernel, basis, overall),
        out_shape=[chunk, chunk, jax.ShapeDtypeStruct((basis, types), jnp.float32)],
        compiler_params=pltpu.CompilerParams(vmem_limit_bytes=32 << 20),
        name="first_chunks",
    )(counts, mark)


def second(counts, mark, enter, basis):
    bins, types = counts.shape
    chunk = jax.ShapeDtypeStruct((bins + CARRY_ROWS, types // STREAMS), jnp.bfloat16)
    return pl.pallas_call(
        functools.partial(second_kernel, basis),
        out_shape=[chunk, chunk],
        compiler_params=pltpu.CompilerParams(vmem_limit_bytes=32 << 20),
        name="second_chunks",
    )(counts, mark, enter)


def states_kernel(basis, step, tile, *refs):
    chunks = refs[:STREAMS]
    lag_ref, power_ref = refs[STREAMS : STREAMS + 2]
    out_ref, held, sems = refs[-3:]
    bins, lanes = chunks[0].shape
    per = lanes // tile
    copies = []
    for j in range(STREAMS):
        impact = chunks[j][:bins] if j % 2 else chunks[j][...]
        carry = chunks[j | 1][bins:].astype(jnp.float32)
        for b in range(basis):
            state = jnp.dot(lag_ref[b], impact, preferred_element_type=jnp.float32)
            row = (j % 2) * basis + b
            for q in range(per):
                at = slice(q * tile, (q + 1) * tile)
                held[j * per + q, :, b * tile : (b + 1) * tile] = (
                    state[:, at] + power_ref[b] * carry[row : row + 1, at]
                ).astype(jnp.bfloat16)
        copy = pltpu.make_async_copy(
            held.at[pl.ds(j * per, per)],
            out_ref.at[pl.ds((step * STREAMS + j) * per, per)],
            sems.at[j],
        )
        copy.start()
        copies.append(copy)
    for copy in copies:
        copy.wait()


def build_states(states, chunks, lag, power, step, steps, tile):
    basis, bins, _ = lag.shape
    lanes = chunks[0].shape[1]
    width = STREAMS * lanes // tile
    vmem = pl.BlockSpec(memory_space=pltpu.VMEM)
    given = [] if states is None else [states]
    return pl.pallas_call(
        functools.partial(states_kernel, basis, step, tile),
        in_specs=[vmem] * (STREAMS + 2) + [pl.BlockSpec(memory_space=pl.ANY)] * len(given),
        out_specs=pl.BlockSpec(memory_space=pl.ANY),
        out_shape=jax.ShapeDtypeStruct((steps * width, bins, basis * tile), jnp.bfloat16),
        scratch_shapes=[
            pltpu.VMEM((width, bins, basis * tile), jnp.bfloat16),
            pltpu.SemaphoreType.DMA((STREAMS,)),
        ],
        input_output_aliases={STREAMS + 2: 0} if given else {},
        compiler_params=pltpu.CompilerParams(vmem_limit_bytes=32 << 20),
        cost_estimate=pl.CostEstimate(
            flops=2 * basis * bins * bins * lanes * STREAMS,
            bytes_accessed=4 * 1024 * 1024,
            transcendentals=0,
        ),
        name="states",
    )(*chunks, lag, power, *given)


def rows_kernel(basis, slots, brows, overall, place_ref, col_ref, fill_ref, *refs):
    blocks = refs[:slots]
    excite_ref, counts_ref, base_ref, mine_ref, other_ref, rate_ref = refs[slots:]
    row = pl.program_id(0)
    own, half = place_ref[0], place_ref[1]
    tile = excite_ref.shape[-1]
    part = tile // 2
    fill = fill_ref[own * brows + row]
    weights = []
    for s in range(slots):
        weight = jnp.concatenate([excite_ref[b, 0, s] for b in range(basis)], axis=1)
        weights.append(jnp.where(s < fill, weight, jnp.zeros_like(weight)))
    state = jnp.concatenate([blocks[s][0] for s in range(slots)], axis=1)
    excited = lax.dot_general(
        state,
        jnp.concatenate(weights, axis=1),
        (((1,), (1,)), ((), ())),
        preferred_element_type=jnp.float32,
    )
    intensity = excited + base_ref[...]
    weighted = (2.0 / overall) * (intensity - counts_ref[...].astype(jnp.float32))
    rate_ref[0] = jnp.sum(weighted, axis=0, keepdims=True)
    turned = weighted.T.astype(jnp.bfloat16)
    upper, lower = turned[:part], turned[part:]
    turned = jnp.concatenate(
        [jnp.where(half == 0, upper, lower), jnp.where(half == 0, lower, upper)], axis=0
    )
    for s in range(slots):
        grad = jnp.dot(turned, blocks[s][0], preferred_element_type=jnp.float32)
        grad = jnp.where(s < fill, grad, jnp.zeros_like(grad)).astype(jnp.bfloat16)
        for b in range(basis):
            piece = grad[:, b * tile : (b + 1) * tile]
            mine_ref[b, 0, s] = piece[:part]
            other_ref[b, 0, s] = piece[part:]


def ring_place(index, n):
    return jnp.where(index % 2 == 0, index // 2, n - 1 - index // 2)


def rows(place, cols, fill, states, excite, counts, base_rate, overall, n):
    basis, brows, slots, tile, _ = excite.shape
    bins, types = counts.shape
    width = types // tile

    def block_at(s):
        def index(i, place, cols, fill):
            row = place[0] * brows + i
            c = cols[row * slots + s]
            block = lax.rem(c, width)
            ahead = ring_place(lax.div(c, width), n) - ring_place(place[0], n)
            ahead = jnp.where(block < width // 2, -ahead, ahead)
            ahead = jnp.where(ahead < 0, ahead + n, ahead)
            return jnp.where(s < fill[row], ahead * width + block, 0), 0, 0

        return index

    part = tile // 2
    out_block = pl.BlockSpec((basis, 1, slots, part, tile), lambda i, *_: (0, i, 0, 0, 0))
    out_shape = jax.ShapeDtypeStruct((basis, brows, slots, part, tile), jnp.bfloat16)
    return pl.pallas_call(
        functools.partial(rows_kernel, basis, slots, brows, overall),
        grid_spec=pltpu.PrefetchScalarGridSpec(
            num_scalar_prefetch=3,
            grid=(brows,),
            in_specs=[pl.BlockSpec((1, bins, basis * tile), block_at(s)) for s in range(slots)]
            + [
                pl.BlockSpec((basis, 1, slots, tile, tile), lambda i, *_: (0, i, 0, 0, 0)),
                pl.BlockSpec((bins, tile), lambda i, *_: (0, i)),
                pl.BlockSpec((1, tile), lambda i, *_: (0, i)),
            ],
            out_specs=[out_block, out_block, pl.BlockSpec((1, 1, tile), lambda i, *_: (i, 0, 0))],
        ),
        out_shape=[out_shape, out_shape, jax.ShapeDtypeStruct((brows, 1, tile), jnp.float32)],
        compiler_params=pltpu.CompilerParams(vmem_limit_bytes=40 << 20),
        name="rows",
    )(
        place,
        cols,
        fill,
        *([states] * slots),
        excite,
        counts,
        base_rate.reshape(1, -1),
    )


def shards(counts, mark_value, base_rate, excite, block_col, row_fill):
    basis, brows, slots, tile, _ = excite.shape
    bins = counts.shape[0]
    overall = bins * lax.axis_size("tm")
    n = lax.axis_size("types")
    half = lax.axis_index("tm")
    place = jnp.stack([lax.axis_index("types"), half]).astype(jnp.int32)
    order = list(range(0, n, 2)) + list(range(1, n, 2))[::-1]
    up = [(order[i], order[(i + 1) % n]) for i in range(n)]
    down = [(b, a) for a, b in up]
    up_one, down_one, ends = first(counts, mark_value, basis, overall)
    enter = lax.ppermute(ends, "tm", [(0, 1)])
    up_two, down_two = second(counts, mark_value, enter, basis)
    lag, power = lag_tables(bins, basis, overall, tile)
    chunks = [up_one, up_two, down_one, down_two]
    states = None
    for step in range(n):
        ahead = None
        if step < n - 1:
            ahead = [
                lax.ppermute(chunks[j], "types", up if j < STREAMS // 2 else down)
                for j in (0, 2, 1, 3)
            ]
            ahead = [ahead[0], ahead[2], ahead[1], ahead[3]]
        states = build_states(states, chunks, lag, power, step, n, tile)
        chunks = ahead
    mine, other, rate = rows(
        place, block_col.reshape(-1), row_fill, states, excite, counts, base_rate, overall, n
    )
    swap = [(0, 1), (1, 0)]
    rate = rate.reshape(2, -1)
    got = lax.ppermute(other, "tm", swap)
    rate_got = lax.ppermute(lax.dynamic_index_in_dim(rate, 1 - half, 0, False), "tm", swap)
    grad = (mine.astype(jnp.float32) + got.astype(jnp.float32)).astype(jnp.bfloat16)
    return grad, lax.dynamic_index_in_dim(rate, half, 0, False) + rate_got


def solution(mesh):
    return jax.shard_map(
        shards,
        mesh=mesh,
        in_specs=(
            P(("parts", "tm"), "types"),
            P(("parts", "tm"), "types"),
            P("types"),
            P(None, "types", None, None, None),
            P(),
            P(),
        ),
        out_specs=(P("parts", "types", None, "tm", None), P(("parts", "types", "tm"))),
        check_vma=False,
    )
```

```python
import functools
import jax
import jax.numpy as jnp
from jax import lax
from jax.experimental import pallas as pl
from jax.experimental.pallas import tpu as pltpu
from jax.sharding import PartitionSpec as P

STREAMS = 4
CARRY_ROWS = 16
GROUPS = 2


def lag_tables(bins, basis_count, overall, lanes):
    log_decay = -(8.0 ** jnp.arange(basis_count, dtype=jnp.float32)) / (2.0 * overall)
    t = jnp.arange(bins, dtype=jnp.float32)
    lag = t[:, None] - 1.0 - t[None, :]
    weights = jnp.where(
        lag[None] >= 0.0,
        (1.0 - jnp.exp(log_decay))[:, None, None]
        * jnp.exp(jnp.maximum(lag, 0.0)[None] * log_decay[:, None, None]),
        jnp.float32(0.0),
    )
    power = jnp.exp(t[None, :, None] * log_decay[:, None, None])
    return weights.astype(jnp.bfloat16), jnp.broadcast_to(power, (basis_count, bins, lanes))


def impact_of(counts_ref, mark_ref, lanes):
    counts = counts_ref[:, lanes].astype(jnp.float32)
    return (counts * mark_ref[:, lanes].astype(jnp.float32)).astype(jnp.bfloat16)


def first_kernel(basis, overall, counts_ref, mark_ref, up_ref, down_ref, ends_ref):
    bins, types = counts_ref.shape
    lanes = types // STREAMS
    back = (bins - 1 - lax.broadcasted_iota(jnp.int32, (bins, 1), 0)).astype(jnp.float32)
    gains = []
    for b in range(basis):
        rate = (8.0**b) / (2.0 * overall)
        gains.append((1.0 - jnp.exp(jnp.full((bins, 1), -rate, jnp.float32))) * jnp.exp(-rate * back))
    for j in range(STREAMS):
        impact = impact_of(counts_ref, mark_ref, slice(j * lanes, (j + 1) * lanes))
        if j == 0:
            up_ref[...] = impact
        if j == 2:
            down_ref[...] = impact
        impact = impact.astype(jnp.float32)
        for b in range(basis):
            ends_ref[b : b + 1, j * lanes : (j + 1) * lanes] = jnp.sum(
                impact * gains[b], axis=0, keepdims=True
            )


def second_kernel(basis, counts_ref, mark_ref, enter_ref, up_ref, down_ref):
    bins, types = counts_ref.shape
    lanes = types // STREAMS
    for j, out_ref in ((1, up_ref), (3, down_ref)):
        out_ref[:bins] = impact_of(counts_ref, mark_ref, slice(j * lanes, (j + 1) * lanes))
        carry = jnp.concatenate(
            [enter_ref[:, (j - 1) * lanes : j * lanes], enter_ref[:, j * lanes : (j + 1) * lanes]],
            axis=0,
        )
        pad = jnp.zeros((CARRY_ROWS - 2 * basis, lanes), jnp.float32)
        out_ref[bins:] = jnp.concatenate([carry, pad], axis=0).astype(jnp.bfloat16)


def first(counts, mark, basis, overall):
    bins, types = counts.shape
    chunk = jax.ShapeDtypeStruct((bins, types // STREAMS), jnp.bfloat16)
    return pl.pallas_call(
        functools.partial(first_kernel, basis, overall),
        out_shape=[chunk, chunk, jax.ShapeDtypeStruct((basis, types), jnp.float32)],
        compiler_params=pltpu.CompilerParams(vmem_limit_bytes=32 << 20),
        name="first_chunks",
    )(counts, mark)


def second(counts, mark, enter, basis):
    bins, types = counts.shape
    chunk = jax.ShapeDtypeStruct((bins + CARRY_ROWS, types // STREAMS), jnp.bfloat16)
    return pl.pallas_call(
        functools.partial(second_kernel, basis),
        out_shape=[chunk, chunk],
        compiler_params=pltpu.CompilerParams(vmem_limit_bytes=32 << 20),
        name="second_chunks",
    )(counts, mark, enter)


def ring_place(index, n):
    return jnp.where(index % 2 == 0, index // 2, n - 1 - index // 2)


def step_kernel(shape, step, place_ref, col_ref, fill_ref, *refs):
    basis, brows, slots, tile, n = shape
    chunks = refs[:STREAMS]
    lag_ref, power_ref, excite_ref = refs[STREAMS : STREAMS + 3]
    states_ref, total_ref, held = refs[-3:]
    bins, lanes = chunks[0].shape
    per = lanes // tile
    width = STREAMS * per
    own = place_ref[0]
    if step == 0:
        counts_ref, base_ref = refs[STREAMS + 3 : STREAMS + 5]
        for row in range(brows):
            at = slice(row * tile, (row + 1) * tile)
            total_ref[row] = (base_ref[:, at] - counts_ref[:, at].astype(jnp.float32)).T
    for j in range(STREAMS):
        impact = chunks[j][:bins] if j % 2 else chunks[j][...]
        carry = chunks[j | 1][bins:].astype(jnp.float32)
        for b in range(basis):
            state = jnp.dot(lag_ref[b], impact, preferred_element_type=jnp.float32)
            row = (j % 2) * basis + b
            for q in range(per):
                at = slice(q * tile, (q + 1) * tile)
                held[j * per + q, :, b * tile : (b + 1) * tile] = (
                    state[:, at] + power_ref[b] * carry[row : row + 1, at]
                ).astype(jnp.bfloat16)

    @pl.loop(0, brows * slots)
    def _(entry):
        row = entry // slots
        slot = entry - row * slots
        column = col_ref[own * (brows * slots) + entry]
        source = column // width
        block = column - source * width
        ahead = ring_place(source, n) - ring_place(own, n)
        ahead = jnp.where(block < width // 2, -ahead, ahead)
        ahead = jnp.where(ahead < 0, ahead + n, ahead)

        @pl.when((ahead == step) & (slot < fill_ref[own * brows + row]))
        def _():
            state = held[block]
            states_ref[entry] = state
            weight = jnp.concatenate([excite_ref[b, row, slot] for b in range(basis)], axis=1)
            total_ref[row] += lax.dot_general(
                weight, state, (((1,), (1,)), ((), ())), preferred_element_type=jnp.float32
            )


SMEM = pl.BlockSpec(memory_space=pltpu.SMEM)
VMEM = pl.BlockSpec(memory_space=pltpu.VMEM)


def take_step(step, scalars, chunks, lag, power, excite, more, n):
    basis, brows, slots, tile, _ = excite.shape
    bins = lag.shape[1]
    lanes = chunks[0].shape[1]
    before = 3 + STREAMS + 3
    return pl.pallas_call(
        functools.partial(step_kernel, (basis, brows, slots, tile, n), step),
        in_specs=[SMEM] * 3 + [VMEM] * (STREAMS + 5),
        out_specs=[VMEM, VMEM],
        out_shape=[
            jax.ShapeDtypeStruct((brows * slots, bins, basis * tile), jnp.bfloat16),
            jax.ShapeDtypeStruct((brows, tile, bins), jnp.float32),
        ],
        scratch_shapes=[pltpu.VMEM((STREAMS * lanes // tile, bins, basis * tile), jnp.bfloat16)],
        input_output_aliases={} if step == 0 else {before: 0, before + 1: 1},
        compiler_params=pltpu.CompilerParams(vmem_limit_bytes=16 << 20),
        cost_estimate=pl.CostEstimate(
            flops=4 * basis * bins * bins * lanes * STREAMS,
            bytes_accessed=2 * 1024 * 1024,
            transcendentals=0,
        ),
        name="ring_step",
    )(*scalars, *chunks, lag, power, excite, *more)


def products(turned_ref, states_ref, fills, rows, slots, basis, tile, put):
    for r, row in enumerate(rows):
        for s in range(slots):
            grad = jnp.dot(
                turned_ref[row], states_ref[row * slots + s], preferred_element_type=jnp.float32
            )
            grad = jnp.where(s < fills[r], grad, jnp.zeros_like(grad))
            for b in range(basis):
                put(b, r, row, s, grad[:, b * tile : (b + 1) * tile])


def sent_kernel(shape, group, place_ref, fill_ref, *refs):
    basis, brows, slots, tile, overall = shape
    own, half = place_ref[0], place_ref[1]
    part = tile // 2
    if group == 0:
        total_ref, states_ref, out_ref, other_ref, mine_ref, rate_own_ref, rate_sent_ref = refs
        rates = []
        for row in range(brows):
            weighted = (2.0 / overall) * total_ref[row]
            ones = jnp.ones((8, weighted.shape[1]), jnp.float32)
            rates.append(
                lax.dot_general(
                    ones,
                    weighted,
                    (((1,), (1,)), ((), ())),
                    precision=lax.Precision.HIGHEST,
                    preferred_element_type=jnp.float32,
                )[:1]
            )
            weighted = weighted.astype(jnp.bfloat16)
            upper, lower = weighted[:part], weighted[part:]
            mine_ref[row] = jnp.where(half == 0, upper, lower)
            other_ref[row] = jnp.where(half == 0, lower, upper)
        first_half = jnp.concatenate(rates[: brows // 2], axis=0)
        second_half = jnp.concatenate(rates[brows // 2 :], axis=0)
        rate_own_ref[...] = jnp.where(half == 0, first_half, second_half)
        rate_sent_ref[...] = jnp.where(half == 0, second_half, first_half)
    else:
        other_ref, states_ref, out_ref = refs
    count = brows // GROUPS
    rows = range(group * count, (group + 1) * count)
    fills = [fill_ref[own * brows + row] for row in rows]

    def put(b, r, row, s, grad):
        out_ref[b, r, s] = grad.astype(jnp.bfloat16)

    products(other_ref, states_ref, fills, rows, slots, basis, tile, put)


def sent(group, place, fill, given, states, dims, overall):
    basis, brows, slots, tile = dims
    bins = states.shape[1]
    part = tile // 2
    out_shape = [jax.ShapeDtypeStruct((basis, brows // GROUPS, slots, part, tile), jnp.bfloat16)]
    if group == 0:
        out_shape += [jax.ShapeDtypeStruct((brows, part, bins), jnp.bfloat16)] * 2
        out_shape += [jax.ShapeDtypeStruct((brows // 2, tile), jnp.float32)] * 2
    return pl.pallas_call(
        functools.partial(sent_kernel, (basis, brows, slots, tile, overall), group),
        in_specs=[SMEM, SMEM, VMEM, VMEM],
        out_specs=[VMEM] * len(out_shape),
        out_shape=out_shape,
        compiler_params=pltpu.CompilerParams(vmem_limit_bytes=16 << 20),
        name="sent_half",
    )(place, fill, given, states)


def kept_kernel(shape, group, place_ref, fill_ref, mine_ref, states_ref, got_ref, *refs):
    basis, brows, slots, tile = shape
    out_ref, held, sems = refs[-3:]
    own = place_ref[0]
    count = brows // GROUPS
    copies = []
    for r in range(count):
        row = group * count + r

        def put(b, _, row, s, grad, r=r):
            held[b, r, s] = (grad + got_ref[b, r, s].astype(jnp.float32)).astype(jnp.bfloat16)

        products(mine_ref, states_ref, [fill_ref[own * brows + row]], [row], slots, basis, tile, put)
        for b in range(basis):
            copy = pltpu.make_async_copy(held.at[b, r], out_ref.at[b, row], sems.at[b, r])
            copy.start()
            copies.append(copy)
    for copy in copies:
        copy.wait()


def kept(group, place, fill, mine, states, got, out, dims):
    basis, brows, slots, tile = dims
    part = tile // 2
    anywhere = pl.BlockSpec(memory_space=pl.ANY)
    given = [] if out is None else [out]
    return pl.pallas_call(
        functools.partial(kept_kernel, dims, group),
        in_specs=[SMEM, SMEM, VMEM, VMEM, VMEM] + [anywhere] * len(given),
        out_specs=anywhere,
        out_shape=jax.ShapeDtypeStruct((basis, brows, slots, part, tile), jnp.bfloat16),
        scratch_shapes=[
            pltpu.VMEM((basis, brows // GROUPS, slots, part, tile), jnp.bfloat16),
            pltpu.SemaphoreType.DMA((basis, brows // GROUPS)),
        ],
        input_output_aliases={5: 0} if given else {},
        compiler_params=pltpu.CompilerParams(vmem_limit_bytes=16 << 20),
        name="kept_half",
    )(place, fill, mine, states, got, *given)


def shards(counts, mark_value, base_rate, excite, block_col, row_fill):
    basis, brows, slots, tile, _ = excite.shape
    bins = counts.shape[0]
    overall = bins * lax.axis_size("tm")
    n = lax.axis_size("types")
    half = lax.axis_index("tm")
    place = jnp.stack([lax.axis_index("types"), half]).astype(jnp.int32)
    order = list(range(0, n, 2)) + list(range(1, n, 2))[::-1]
    up = [(order[i], order[(i + 1) % n]) for i in range(n)]
    down = [(b, a) for a, b in up]
    up_one, down_one, ends = first(counts, mark_value, basis, overall)
    enter = lax.ppermute(ends, "tm", [(0, 1)])
    up_two, down_two = second(counts, mark_value, enter, basis)
    lag, power = lag_tables(bins, basis, overall, tile)
    chunks = [up_one, up_two, down_one, down_two]
    scalars = (place, block_col.reshape(-1), row_fill)
    more = (counts, base_rate.reshape(1, -1))
    for step in range(n):
        ahead = None
        if step < n - 1:
            ahead = [
                lax.ppermute(chunks[j], "types", up if j < STREAMS // 2 else down)
                for j in (0, 2, 1, 3)
            ]
            ahead = [ahead[0], ahead[2], ahead[1], ahead[3]]
        more = take_step(step, scalars, chunks, lag, power, excite, more, n)
        chunks = ahead
    states, total = more
    dims = (basis, brows, slots, tile)
    swap = [(0, 1), (1, 0)]
    out, other, mine, rate_own, rate_sent = sent(0, place, row_fill, total, states, dims, overall)
    got = [lax.ppermute(out, "tm", swap)]
    rate_got = lax.ppermute(rate_sent, "tm", swap)
    for group in range(1, GROUPS):
        (out,) = sent(group, place, row_fill, other, states, dims, overall)
        got.append(lax.ppermute(out, "tm", swap))
    grad = None
    for group in range(GROUPS):
        grad = kept(group, place, row_fill, mine, states, got[group], grad, dims)
    return grad, (rate_own + rate_got).reshape(-1)


def solution(mesh):
    return jax.shard_map(
        shards,
        mesh=mesh,
        in_specs=(
            P(("parts", "tm"), "types"),
            P(("parts", "tm"), "types"),
            P("types"),
            P(None, "types", None, None, None),
            P(),
            P(),
        ),
        out_specs=(P("parts", "types", None, "tm", None), P(("parts", "types", "tm"))),
        check_vma=False,
    )
```

```python
import functools
import jax
import jax.numpy as jnp
from jax import lax
from jax.experimental import pallas as pl
from jax.experimental.pallas import tpu as pltpu
from jax.sharding import PartitionSpec as P

STREAMS = 4
CARRY_ROWS = 16
GROUPS = 2


def lag_tables(bins, basis_count, overall, lanes):
    log_decay = -(8.0 ** jnp.arange(basis_count, dtype=jnp.float32)) / (2.0 * overall)
    t = jnp.arange(bins, dtype=jnp.float32)
    lag = t[:, None] - 1.0 - t[None, :]
    weights = jnp.where(
        lag[None] >= 0.0,
        (1.0 - jnp.exp(log_decay))[:, None, None]
        * jnp.exp(jnp.maximum(lag, 0.0)[None] * log_decay[:, None, None]),
        jnp.float32(0.0),
    )
    power = jnp.exp(t[None, :, None] * log_decay[:, None, None])
    return weights.astype(jnp.bfloat16), jnp.broadcast_to(power, (basis_count, bins, lanes))


def impact_of(counts_ref, mark_ref, lanes):
    counts = counts_ref[:, lanes].astype(jnp.float32)
    return (counts * mark_ref[:, lanes].astype(jnp.float32)).astype(jnp.bfloat16)


def first_kernel(basis, overall, counts_ref, mark_ref, up_ref, down_ref, ends_ref):
    bins, types = counts_ref.shape
    lanes = types // STREAMS
    back = (bins - 1 - lax.broadcasted_iota(jnp.int32, (bins, 1), 0)).astype(jnp.float32)
    gains = []
    for b in range(basis):
        rate = (8.0**b) / (2.0 * overall)
        gains.append((1.0 - jnp.exp(jnp.full((bins, 1), -rate, jnp.float32))) * jnp.exp(-rate * back))
    for j in range(STREAMS):
        impact = impact_of(counts_ref, mark_ref, slice(j * lanes, (j + 1) * lanes))
        if j == 0:
            up_ref[...] = impact
        if j == 2:
            down_ref[...] = impact
        impact = impact.astype(jnp.float32)
        for b in range(basis):
            ends_ref[b : b + 1, j * lanes : (j + 1) * lanes] = jnp.sum(
                impact * gains[b], axis=0, keepdims=True
            )


def second_kernel(basis, counts_ref, mark_ref, enter_ref, up_ref, down_ref):
    bins, types = counts_ref.shape
    lanes = types // STREAMS
    for j, out_ref in ((1, up_ref), (3, down_ref)):
        out_ref[:bins] = impact_of(counts_ref, mark_ref, slice(j * lanes, (j + 1) * lanes))
        carry = jnp.concatenate(
            [enter_ref[:, (j - 1) * lanes : j * lanes], enter_ref[:, j * lanes : (j + 1) * lanes]],
            axis=0,
        )
        pad = jnp.zeros((CARRY_ROWS - 2 * basis, lanes), jnp.float32)
        out_ref[bins:] = jnp.concatenate([carry, pad], axis=0).astype(jnp.bfloat16)


def first(counts, mark, basis, overall):
    bins, types = counts.shape
    chunk = jax.ShapeDtypeStruct((bins, types // STREAMS), jnp.bfloat16)
    return pl.pallas_call(
        functools.partial(first_kernel, basis, overall),
        out_shape=[chunk, chunk, jax.ShapeDtypeStruct((basis, types), jnp.float32)],
        compiler_params=pltpu.CompilerParams(vmem_limit_bytes=32 << 20),
        name="first_chunks",
    )(counts, mark)


def second(counts, mark, enter, basis):
    bins, types = counts.shape
    chunk = jax.ShapeDtypeStruct((bins + CARRY_ROWS, types // STREAMS), jnp.bfloat16)
    return pl.pallas_call(
        functools.partial(second_kernel, basis),
        out_shape=[chunk, chunk],
        compiler_params=pltpu.CompilerParams(vmem_limit_bytes=32 << 20),
        name="second_chunks",
    )(counts, mark, enter)


def ring_place(index, n):
    return jnp.where(index % 2 == 0, index // 2, n - 1 - index // 2)


SMEM = pl.BlockSpec(memory_space=pltpu.SMEM)
VMEM = pl.BlockSpec(memory_space=pltpu.VMEM)


def plan_kernel(shape, place_ref, col_ref, fill_ref, plan_ref):
    brows, slots, width, n, most = shape
    own = place_ref[0]
    entries = brows * slots
    tail = n * (most + 1)
    plan_ref[tail] = place_ref[1]
    for step in range(n):
        plan_ref[step * (most + 1)] = 0

    @pl.loop(0, brows)
    def _(row):
        fill = fill_ref[own * brows + row]
        plan_ref[tail + 1 + row] = fill

        @pl.loop(0, fill)
        def _(slot):
            column = col_ref[own * entries + row * slots + slot]
            source = lax.div(column, width)
            block = lax.rem(column, width)
            ahead = ring_place(source, n) - ring_place(own, n)
            ahead = jnp.where(block < width // 2, -ahead, ahead)
            ahead = jnp.where(ahead < 0, ahead + n, ahead)
            base = ahead * (most + 1)
            count = plan_ref[base] + 1
            plan_ref[base] = count
            plan_ref[base + count] = (row * 256 + slot) * 256 + block


def make_plan(place, cols, fill, dims, width, n):
    _, brows, slots, _ = dims
    most = 2 * max(2, brows * slots // n)
    return pl.pallas_call(
        functools.partial(plan_kernel, (brows, slots, width, n, most)),
        in_specs=[SMEM] * 3,
        out_specs=SMEM,
        out_shape=jax.ShapeDtypeStruct((n * (most + 1) + 1 + brows,), jnp.int32),
        name="plan",
    )(place, cols, fill)


def step_kernel(shape, step, plan_ref, *refs):
    basis, brows, slots, tile, n = shape
    chunks = refs[:STREAMS]
    lag_ref, power_ref, excite_ref = refs[STREAMS : STREAMS + 3]
    states_ref, total_ref, built_ref, held = refs[-4:]
    bins, lanes = chunks[0].shape
    per = lanes // tile
    built_ref[...] = jnp.zeros_like(built_ref)
    most = (plan_ref.shape[0] - 1 - brows) // n - 1
    if step == 0:
        counts_ref, base_ref = refs[STREAMS + 3 : STREAMS + 5]
        for row in range(brows):
            at = slice(row * tile, (row + 1) * tile)
            total_ref[row] = (base_ref[:, at] - counts_ref[:, at].astype(jnp.float32)).T
    for j in range(STREAMS):
        impact = chunks[j][:bins] if j % 2 else chunks[j][...]
        carry = chunks[j | 1][bins:].astype(jnp.float32)
        for b in range(basis):
            state = jnp.dot(lag_ref[b], impact, preferred_element_type=jnp.float32)
            row = (j % 2) * basis + b
            for q in range(per):
                at = slice(q * tile, (q + 1) * tile)
                held[j * per + q, :, b * tile : (b + 1) * tile] = (
                    state[:, at] + power_ref[b] * carry[row : row + 1, at]
                ).astype(jnp.bfloat16)

    @pl.loop(0, plan_ref[step * (most + 1)])
    def _(k):
        code = plan_ref[step * (most + 1) + 1 + k]
        block = code & 255
        slot = (code >> 8) & 255
        row = code >> 16
        state = held[block]
        states_ref[row * slots + slot] = state
        weight = jnp.concatenate([excite_ref[b, row, slot] for b in range(basis)], axis=1)
        total_ref[row] += lax.dot_general(
            weight, state, (((1,), (1,)), ((), ())), preferred_element_type=jnp.float32
        )


def take_step(step, plan, chunks, lag, power, excite, more, n):
    basis, brows, slots, tile, _ = excite.shape
    bins = lag.shape[1]
    lanes = chunks[0].shape[1]
    before = 1 + STREAMS + 3
    return pl.pallas_call(
        functools.partial(step_kernel, (basis, brows, slots, tile, n), step),
        in_specs=[SMEM] + [VMEM] * (STREAMS + 5),
        out_specs=[VMEM, VMEM, VMEM],
        out_shape=[
            jax.ShapeDtypeStruct((brows * slots, bins, basis * tile), jnp.bfloat16),
            jax.ShapeDtypeStruct((brows, tile, bins), jnp.float32),
            jax.ShapeDtypeStruct((8, tile), jnp.float32),
        ],
        scratch_shapes=[pltpu.VMEM((STREAMS * lanes // tile, bins, basis * tile), jnp.bfloat16)],
        input_output_aliases={} if step == 0 else {before: 0, before + 1: 1},
        compiler_params=pltpu.CompilerParams(vmem_limit_bytes=16 << 20),
        cost_estimate=pl.CostEstimate(
            flops=4 * basis * bins * bins * lanes * STREAMS,
            bytes_accessed=2 * 1024 * 1024,
            transcendentals=0,
        ),
        name="ring_step",
    )(plan, *chunks, lag, power, excite, *more)


def products(turned_ref, states_ref, fills, rows, slots, basis, tile, put):
    for r, row in enumerate(rows):
        for s in range(slots):
            grad = jnp.dot(
                turned_ref[row], states_ref[row * slots + s], preferred_element_type=jnp.float32
            )
            grad = jnp.where(s < fills[r], grad, jnp.zeros_like(grad))
            for b in range(basis):
                put(b, r, row, s, grad[:, b * tile : (b + 1) * tile])


def sent_kernel(shape, group, plan_ref, *refs):
    basis, brows, slots, tile, overall = shape
    tail = plan_ref.shape[0] - 1 - brows
    half = plan_ref[tail]
    part = tile // 2
    if group == 0:
        total_ref, states_ref, out_ref, other_ref, mine_ref, rate_own_ref, rate_sent_ref = refs
        rates = []
        for row in range(brows):
            weighted = (2.0 / overall) * total_ref[row]
            ones = jnp.ones((8, weighted.shape[1]), jnp.float32)
            rates.append(
                lax.dot_general(
                    ones,
                    weighted,
                    (((1,), (1,)), ((), ())),
                    precision=lax.Precision.HIGHEST,
                    preferred_element_type=jnp.float32,
                )[:1]
            )
            weighted = weighted.astype(jnp.bfloat16)
            upper, lower = weighted[:part], weighted[part:]
            mine_ref[row] = jnp.where(half == 0, upper, lower)
            other_ref[row] = jnp.where(half == 0, lower, upper)
        first_half = jnp.concatenate(rates[: brows // 2], axis=0)
        second_half = jnp.concatenate(rates[brows // 2 :], axis=0)
        rate_own_ref[...] = jnp.where(half == 0, first_half, second_half)
        rate_sent_ref[...] = jnp.where(half == 0, second_half, first_half)
    else:
        other_ref, states_ref, out_ref = refs
    count = brows // GROUPS
    rows = range(group * count, (group + 1) * count)
    fills = [plan_ref[tail + 1 + row] for row in rows]

    def put(b, r, row, s, grad):
        out_ref[b, r, s] = grad.astype(jnp.bfloat16)

    products(other_ref, states_ref, fills, rows, slots, basis, tile, put)


def sent(group, plan, given, states, dims, overall):
    basis, brows, slots, tile = dims
    bins = states.shape[1]
    part = tile // 2
    out_shape = [jax.ShapeDtypeStruct((basis, brows // GROUPS, slots, part, tile), jnp.bfloat16)]
    if group == 0:
        out_shape += [jax.ShapeDtypeStruct((brows, part, bins), jnp.bfloat16)] * 2
        out_shape += [jax.ShapeDtypeStruct((brows // 2, tile), jnp.float32)] * 2
    return pl.pallas_call(
        functools.partial(sent_kernel, (basis, brows, slots, tile, overall), group),
        in_specs=[SMEM, VMEM, VMEM],
        out_specs=[VMEM] * len(out_shape),
        out_shape=out_shape,
        compiler_params=pltpu.CompilerParams(vmem_limit_bytes=16 << 20),
        name="sent_half",
    )(plan, given, states)


def kept_kernel(shape, group, plan_ref, mine_ref, states_ref, got_ref, *refs):
    basis, brows, slots, tile = shape
    out_ref, held, sems = refs[-3:]
    tail = plan_ref.shape[0] - 1 - brows
    count = brows // GROUPS
    copies = []
    for r in range(count):
        row = group * count + r

        def put(b, _, row, s, grad, r=r):
            held[b, r, s] = (grad + got_ref[b, r, s].astype(jnp.float32)).astype(jnp.bfloat16)

        products(mine_ref, states_ref, [plan_ref[tail + 1 + row]], [row], slots, basis, tile, put)
        for b in range(basis):
            copy = pltpu.make_async_copy(held.at[b, r], out_ref.at[b, row], sems.at[b, r])
            copy.start()
            copies.append(copy)
    for copy in copies:
        copy.wait()


def kept(group, plan, mine, states, got, out, dims):
    basis, brows, slots, tile = dims
    part = tile // 2
    anywhere = pl.BlockSpec(memory_space=pl.ANY)
    given = [] if out is None else [out]
    return pl.pallas_call(
        functools.partial(kept_kernel, dims, group),
        in_specs=[SMEM, VMEM, VMEM, VMEM] + [anywhere] * len(given),
        out_specs=anywhere,
        out_shape=jax.ShapeDtypeStruct((basis, brows, slots, part, tile), jnp.bfloat16),
        scratch_shapes=[
            pltpu.VMEM((basis, brows // GROUPS, slots, part, tile), jnp.bfloat16),
            pltpu.SemaphoreType.DMA((basis, brows // GROUPS)),
        ],
        input_output_aliases={4: 0} if given else {},
        compiler_params=pltpu.CompilerParams(vmem_limit_bytes=16 << 20),
        name="kept_half",
    )(plan, mine, states, got, *given)


def shards(counts, mark_value, base_rate, excite, block_col, row_fill):
    basis, brows, slots, tile, _ = excite.shape
    bins = counts.shape[0]
    overall = bins * lax.axis_size("tm")
    n = lax.axis_size("types")
    half = lax.axis_index("tm")
    place = jnp.stack([lax.axis_index("types"), half]).astype(jnp.int32)
    order = list(range(0, n, 2)) + list(range(1, n, 2))[::-1]
    up = [(order[i], order[(i + 1) % n]) for i in range(n)]
    down = [(b, a) for a, b in up]
    up_one, down_one, ends = first(counts, mark_value, basis, overall)
    enter = lax.ppermute(ends, "tm", [(0, 1)])
    up_two, down_two = second(counts, mark_value, enter, basis)
    lag, power = lag_tables(bins, basis, overall, tile)
    chunks = [up_one, up_two, down_one, down_two]
    dims = (basis, brows, slots, tile)
    plan = make_plan(place, block_col.reshape(-1), row_fill, dims, counts.shape[1] // tile, n)
    more = (counts, base_rate.reshape(1, -1))
    for step in range(n):
        ahead = None
        if step < n - 1:
            ahead = [
                lax.ppermute(chunks[j], "types", up if j < STREAMS // 2 else down)
                for j in (0, 2, 1, 3)
            ]
            ahead = [ahead[0], ahead[2], ahead[1], ahead[3]]
        *more, built = take_step(step, plan, chunks, lag, power, excite, more, n)
        if step < n - 1:
            ahead = [lax.optimization_barrier((chunk, built))[0] for chunk in ahead]
        chunks = ahead
    states, total = more
    swap = [(0, 1), (1, 0)]
    out, other, mine, rate_own, rate_sent = sent(0, plan, total, states, dims, overall)
    got = [lax.ppermute(out, "tm", swap)]
    rate_got = lax.ppermute(rate_sent, "tm", swap)
    for group in range(1, GROUPS):
        (out,) = sent(group, plan, other, states, dims, overall)
        got.append(lax.ppermute(out, "tm", swap))
    grad = None
    for group in range(GROUPS):
        grad = kept(group, plan, mine, states, got[group], grad, dims)
    return grad, (rate_own + rate_got).reshape(-1)


def solution(mesh):
    return jax.shard_map(
        shards,
        mesh=mesh,
        in_specs=(
            P(("parts", "tm"), "types"),
            P(("parts", "tm"), "types"),
            P("types"),
            P(None, "types", None, None, None),
            P(),
            P(),
        ),
        out_specs=(P("parts", "types", None, "tm", None), P(("parts", "types", "tm"))),
        check_vma=False,
    )
```

```python
import functools
import jax
import jax.numpy as jnp
from jax import lax
from jax.experimental import pallas as pl
from jax.experimental.pallas import tpu as pltpu
from jax.sharding import PartitionSpec as P

GROUPS = 2
LATE = 3
SMEM = pl.BlockSpec(memory_space=pltpu.SMEM)
VMEM = pl.BlockSpec(memory_space=pltpu.VMEM)
ANYWHERE = pl.BlockSpec(memory_space=pl.ANY)
PARAMS = pltpu.CompilerParams(vmem_limit_bytes=16 << 20)


def lag_tables(bins, basis_count, overall, lanes):
    log_decay = -(8.0 ** jnp.arange(basis_count, dtype=jnp.float32)) / (2.0 * overall)
    t = jnp.arange(bins, dtype=jnp.float32)
    lag = t[:, None] - 1.0 - t[None, :]
    weights = jnp.where(
        lag[None] >= 0.0,
        (1.0 - jnp.exp(log_decay))[:, None, None]
        * jnp.exp(jnp.maximum(lag, 0.0)[None] * log_decay[:, None, None]),
        jnp.float32(0.0),
    )
    power = jnp.exp(t[None, :, None] * log_decay[:, None, None])
    return weights.astype(jnp.bfloat16), jnp.broadcast_to(power, (basis_count, bins, lanes))


def impact_kernel(
    basis, tile, overall, counts_hbm, mark_hbm, up_ref, down_ref, ends_ref, counts, mark, sems
):
    bins, types = counts.shape
    parts = sems.shape[1]
    lanes = types // parts
    copies = []
    for j in range(parts):
        at = pl.ds(j * lanes, lanes)
        copies.append(
            (
                pltpu.make_async_copy(counts_hbm.at[:, at], counts.at[:, at], sems.at[0, j]),
                pltpu.make_async_copy(mark_hbm.at[:, at], mark.at[:, at], sems.at[1, j]),
            )
        )
        for copy in copies[-1]:
            copy.start()
    back = (bins - 1 - lax.broadcasted_iota(jnp.int32, (bins, tile), 0)).astype(jnp.float32)
    gains = []
    for b in range(basis):
        rate = (8.0**b) / (2.0 * overall)
        gains.append((1.0 - jnp.exp(jnp.full((bins, tile), -rate, jnp.float32))) * jnp.exp(-rate * back))
    half = types // tile // 2
    for j in range(parts):
        for copy in copies[j]:
            copy.wait()
        for block in range(j * lanes // tile, (j + 1) * lanes // tile):
            at = slice(block * tile, (block + 1) * tile)
            impact = counts[:, at].astype(jnp.float32) * mark[:, at].astype(jnp.float32)
            impact = impact.astype(jnp.bfloat16)
            out_ref = up_ref if block < half else down_ref
            out_ref[block % half * bins : (block % half + 1) * bins] = impact
            impact = impact.astype(jnp.float32)
            for b in range(basis):
                ends_ref[b : b + 1, at] = jnp.sum(impact * gains[b], axis=0, keepdims=True)
    rest = up_ref.shape[0] - half * bins
    for out_ref in (up_ref, down_ref):
        out_ref[half * bins :] = jnp.zeros((rest, tile), jnp.bfloat16)


def impact_chunks(counts, mark, dims, overall):
    basis, _, _, tile = dims
    bins, types = counts.shape
    half = types // tile // 2
    carry = -(-half * basis // 16) * 16
    chunk = jax.ShapeDtypeStruct((half * bins + carry, tile), jnp.bfloat16)
    return pl.pallas_call(
        functools.partial(impact_kernel, basis, tile, overall),
        in_specs=[ANYWHERE, ANYWHERE],
        out_specs=[VMEM, VMEM, VMEM],
        out_shape=[chunk, chunk, jax.ShapeDtypeStruct((basis, types), jnp.float32)],
        scratch_shapes=[
            pltpu.VMEM((bins, types), jnp.int32),
            pltpu.VMEM((bins, types), jnp.bfloat16),
            pltpu.SemaphoreType.DMA((2, 2)),
        ],
        compiler_params=pltpu.CompilerParams(vmem_limit_bytes=56 << 20),
        name="impact_chunks",
    )(counts, mark)


def carry_kernel(basis, bins, enter_ref, _, __, up_ref, down_ref, held, sems):
    rows, tile = up_ref.shape
    half = enter_ref.shape[1] // tile // 2
    rest = rows - half * bins
    copies = []
    for d, out_ref in enumerate((up_ref, down_ref)):
        carry = [
            enter_ref[:, (d * half + q) * tile : (d * half + q + 1) * tile] for q in range(half)
        ]
        if rest > half * basis:
            carry.append(jnp.zeros((rest - half * basis, tile), jnp.float32))
        held[d] = jnp.concatenate(carry, axis=0).astype(jnp.bfloat16)
        copies.append(
            pltpu.make_async_copy(held.at[d], out_ref.at[pl.ds(half * bins, rest)], sems.at[d])
        )
        copies[-1].start()
    for copy in copies:
        copy.wait()


def add_carry(enter, up, down, basis, bins):
    chunk = jax.ShapeDtypeStruct(up.shape, up.dtype)
    rows, tile = up.shape
    return pl.pallas_call(
        functools.partial(carry_kernel, basis, bins),
        in_specs=[VMEM, ANYWHERE, ANYWHERE],
        out_specs=[ANYWHERE, ANYWHERE],
        out_shape=[chunk, chunk],
        scratch_shapes=[
            pltpu.VMEM((2, rows % bins, tile), jnp.bfloat16),
            pltpu.SemaphoreType.DMA((2,)),
        ],
        input_output_aliases={1: 0, 2: 1},
        compiler_params=PARAMS,
        name="carry_rows",
    )(enter, up, down)


def ring_place(index, n):
    return jnp.where(index % 2 == 0, index // 2, n - 1 - index // 2)


def code_of(row, slot, block):
    return (row * 256 + slot) * 256 + block


def plan_kernel(shape, place_ref, col_ref, fill_ref, plan_ref):
    brows, slots, width, n, most = shape
    own = place_ref[0]
    entries = brows * slots
    tail = n * (most + 1)
    plan_ref[tail] = place_ref[1]
    for step in range(n):
        plan_ref[step * (most + 1)] = 0

    @pl.loop(0, brows)
    def _(row):
        fill = fill_ref[own * brows + row]
        plan_ref[tail + 1 + row] = fill

        @pl.loop(0, fill)
        def _(slot):
            column = col_ref[own * entries + row * slots + slot]
            source = lax.div(column, width)
            block = lax.rem(column, width)
            ahead = ring_place(source, n) - ring_place(own, n)
            ahead = jnp.where(block < width // 2, -ahead, ahead)
            ahead = jnp.where(ahead < 0, ahead + n, ahead)
            base = ahead * (most + 1)
            count = plan_ref[base] + 1
            plan_ref[base] = count
            plan_ref[base + count] = code_of(row, slot, block)

    for step in range(n):
        base = step * (most + 1)
        count = plan_ref[base]

        @pl.when(lax.rem(count, 2) == 1)
        def _(base=base, count=count):
            plan_ref[base + count + 1] = code_of(brows, 0, 0)


def make_plan(place, cols, fill, dims, width, n):
    _, brows, slots, _ = dims
    most = 2 * max(2, brows * slots // n)
    return pl.pallas_call(
        functools.partial(plan_kernel, (brows, slots, width, n, most)),
        in_specs=[SMEM] * 3,
        out_specs=SMEM,
        out_shape=jax.ShapeDtypeStruct((n * (most + 1) + 1 + brows,), jnp.int32),
        name="plan",
    )(place, cols, fill)


def start_kernel(tile, counts_ref, base_ref, total_ref):
    for row in range(total_ref.shape[0] - 1):
        at = slice(row * tile, (row + 1) * tile)
        total_ref[row] = (base_ref[:, at] - counts_ref[:, at].astype(jnp.float32)).T
    total_ref[total_ref.shape[0] - 1] = jnp.zeros(total_ref.shape[1:], jnp.float32)


def start_total(counts, base_rate, dims):
    _, brows, _, tile = dims
    return pl.pallas_call(
        functools.partial(start_kernel, tile),
        in_specs=[VMEM, VMEM],
        out_specs=VMEM,
        out_shape=jax.ShapeDtypeStruct((brows + 1, tile, counts.shape[0]), jnp.float32),
        compiler_params=PARAMS,
        name="base_less_counts",
    )(counts, base_rate)


def step_kernel(dims, n, step, plan_ref, up_ref, down_ref, lag_ref, power_ref, excite_ref, *refs):
    basis, brows, slots, tile = dims
    total_in, states_ref, total_ref, built_ref, impact, carry, held, sems = refs[-8:]
    bins = lag_ref.shape[1]
    half = impact.shape[0] // 2
    most = (plan_ref.shape[0] - 1 - brows) // n - 1
    built_ref[...] = jnp.zeros_like(built_ref)
    total_ref[...] = total_in[...]
    pairs = (plan_ref[step * (most + 1)] + 1) // 2

    def entry_at(place):
        code = plan_ref[step * (most + 1) + 1 + place]
        return code >> 16, (code >> 8) & 255, code & 255

    def copy_at(place):
        row, slot, _ = entry_at(place)
        return pltpu.make_async_copy(
            held.at[place], states_ref.at[row * slots + slot], sems.at[place]
        )

    for d, chunk in enumerate((up_ref, down_ref)):
        rows = chunk[half * bins :].astype(jnp.float32)
        for q in range(half):
            impact[d * half + q] = chunk[q * bins : (q + 1) * bins]
            carry[d * half + q, :basis] = rows[q * basis : (q + 1) * basis]

    @pl.loop(0, pairs)
    def _(k):
        found = [entry_at(2 * k + i) for i in range(2)]
        both = jnp.concatenate([impact[block] for _, _, block in found], axis=1)
        enter = [carry[block] for _, _, block in found]
        built = [[], []]
        for b in range(basis):
            state = jnp.dot(lag_ref[b], both, preferred_element_type=jnp.float32)
            for i in range(2):
                built[i].append(
                    (
                        state[:, i * tile : (i + 1) * tile] + power_ref[b] * enter[i][b : b + 1]
                    ).astype(jnp.bfloat16)
                )
        for i, (row, slot, _) in enumerate(found):
            state = jnp.concatenate(built[i], axis=1)
            held[2 * k + i] = state
            copy_at(2 * k + i).start()
            inside = jnp.minimum(row, brows - 1)
            weight = jnp.concatenate([excite_ref[b, inside, slot] for b in range(basis)], axis=1)
            total_ref[row] += lax.dot_general(
                weight, state, (((1,), (1,)), ((), ())), preferred_element_type=jnp.float32
            )

    @pl.loop(0, 2 * pairs)
    def _(place):
        copy_at(place).wait()


def take_step(step, plan, chunks, lag, power, excite, states, total, dims, n):
    basis, brows, slots, tile = dims
    bins = lag.shape[1]
    half = chunks[0].shape[0] // bins
    most = (plan.shape[0] - 1 - brows) // n - 1
    given = [total] if states is None else [states, total]
    return pl.pallas_call(
        functools.partial(step_kernel, dims, n, step),
        in_specs=[SMEM] + [VMEM] * 5 + [ANYWHERE] * (len(given) - 1) + [VMEM],
        out_specs=[ANYWHERE, VMEM, VMEM],
        out_shape=[
            jax.ShapeDtypeStruct((brows * slots + 1, bins, basis * tile), jnp.bfloat16),
            jax.ShapeDtypeStruct(total.shape, total.dtype),
            jax.ShapeDtypeStruct((8, tile), jnp.float32),
        ],
        scratch_shapes=[
            pltpu.VMEM((2 * half, bins, tile), jnp.bfloat16),
            pltpu.VMEM((2 * half, 8, tile), jnp.float32),
            pltpu.VMEM((most, bins, basis * tile), jnp.bfloat16),
            pltpu.SemaphoreType.DMA((most,)),
        ],
        input_output_aliases={} if states is None else {6: 0},
        compiler_params=PARAMS,
        cost_estimate=pl.CostEstimate(
            flops=8 * basis * bins * bins * tile * 4,
            bytes_accessed=4 * 1024 * 1024,
            transcendentals=0,
        ),
        name="ring_step",
    )(plan, *chunks, lag, power, excite, *given)


def products(turned_ref, states_ref, plan_ref, rows, dims, put):
    basis, brows, slots, tile = dims
    tail = plan_ref.shape[0] - 1 - brows
    for r, row in enumerate(rows):
        fill = plan_ref[tail + 1 + row]
        for s in range(slots):
            grad = jnp.dot(
                turned_ref[row], states_ref[row * slots + s], preferred_element_type=jnp.float32
            )
            grad = jnp.where(s < fill, grad, jnp.zeros_like(grad))
            for b in range(basis):
                put(b, r, s, grad[:, b * tile : (b + 1) * tile])


def rows_of(group, dims):
    count = dims[1] // GROUPS
    return range(group * count, (group + 1) * count)


def halves_kernel(dims, overall, plan_ref, total_ref, states_ref, out_ref, *refs):
    _, brows, _, tile = dims
    sent_ref, kept_ref, rate_sent_ref, rate_kept_ref = refs
    half = plan_ref[plan_ref.shape[0] - 1 - brows]
    part = tile // 2
    rates = []
    for row in range(brows):
        weighted = (2.0 / overall) * total_ref[row]
        rates.append(
            lax.dot_general(
                jnp.ones((8, weighted.shape[1]), jnp.float32),
                weighted,
                (((1,), (1,)), ((), ())),
                precision=lax.Precision.HIGHEST,
                preferred_element_type=jnp.float32,
            )[:1]
        )
        weighted = weighted.astype(jnp.bfloat16)
        upper, lower = weighted[:part], weighted[part:]
        kept_ref[row] = jnp.where(half == 0, upper, lower)
        sent_ref[row] = jnp.where(half == 0, lower, upper)
    first_half = jnp.concatenate(rates[: brows // 2], axis=0)
    second_half = jnp.concatenate(rates[brows // 2 :], axis=0)
    rate_kept_ref[...] = jnp.where(half == 0, first_half, second_half)
    rate_sent_ref[...] = jnp.where(half == 0, second_half, first_half)
    store_kernel(dims, 0, plan_ref, sent_ref, states_ref, out_ref)


def store_kernel(dims, group, plan_ref, turned_ref, states_ref, out_ref):
    def put(b, r, s, grad):
        out_ref[b, r, s] = grad.astype(out_ref.dtype)

    products(turned_ref, states_ref, plan_ref, rows_of(group, dims), dims, put)


def group_shape(dims, dtype):
    basis, brows, slots, tile = dims
    return jax.ShapeDtypeStruct((basis, brows // GROUPS, slots, tile // 2, tile), dtype)


def halves(plan, total, states, dims, overall):
    _, brows, _, tile = dims
    turned = jax.ShapeDtypeStruct((brows, tile // 2, total.shape[2]), jnp.bfloat16)
    rate = jax.ShapeDtypeStruct((brows // 2, tile), jnp.float32)
    return pl.pallas_call(
        functools.partial(halves_kernel, dims, overall),
        in_specs=[SMEM, VMEM, VMEM],
        out_specs=[VMEM] * 5,
        out_shape=[group_shape(dims, jnp.bfloat16), turned, turned, rate, rate],
        compiler_params=PARAMS,
        name="weighted_halves",
    )(plan, total, states)


def store_products(group, plan, turned, states, dims, dtype):
    return pl.pallas_call(
        functools.partial(store_kernel, dims, group),
        in_specs=[SMEM, VMEM, VMEM],
        out_specs=VMEM,
        out_shape=group_shape(dims, dtype),
        compiler_params=PARAMS,
        name="products",
    )(plan, turned, states)


def out_copies(dims, group, r, held, out_ref, sems):
    row = rows_of(group, dims)[r]
    return [
        pltpu.make_async_copy(held.at[b, r], out_ref.at[b, row], sems.at[b, r])
        for b in range(dims[0])
    ]


def kept_kernel(dims, group, plan_ref, turned_ref, states_ref, got_ref, out_ref, held, sems):
    copies = []
    for r, row in enumerate(rows_of(group, dims)):

        def put(b, _, s, grad, r=r):
            held[b, r, s] = (grad + got_ref[b, r, s].astype(jnp.float32)).astype(jnp.bfloat16)

        products(turned_ref, states_ref, plan_ref, [row], dims, put)
        for copy in out_copies(dims, group, r, held, out_ref, sems):
            copy.start()
            copies.append(copy)
    for copy in copies:
        copy.wait()


def add_kernel(
    dims, group, own_ref, got_ref, rate_ref, rate_got_ref, _, out_ref, rate_out_ref, held, sems
):
    basis, brows, _, _ = dims
    rate_out_ref[...] = rate_ref[...] + rate_got_ref[...]
    copies = []
    for r in range(brows // GROUPS):
        for b in range(basis):
            held[b, r] = (own_ref[b, r] + got_ref[b, r].astype(jnp.float32)).astype(jnp.bfloat16)
        for copy in out_copies(dims, group, r, held, out_ref, sems):
            copy.start()
            copies.append(copy)
    for copy in copies:
        copy.wait()


def finish(dims, plan, turned, states, own, got, rate, rate_got):
    basis, brows, slots, tile = dims
    whole = jax.ShapeDtypeStruct((basis, brows, slots, tile // 2, tile), jnp.bfloat16)
    scratch = [
        pltpu.VMEM(group_shape(dims, jnp.bfloat16).shape, jnp.bfloat16),
        pltpu.SemaphoreType.DMA((basis, brows // GROUPS)),
    ]
    grad = pl.pallas_call(
        functools.partial(kept_kernel, dims, 0),
        in_specs=[SMEM, VMEM, VMEM, VMEM],
        out_specs=ANYWHERE,
        out_shape=whole,
        scratch_shapes=scratch,
        compiler_params=PARAMS,
        name="kept_half",
    )(plan, turned, states, got[0])
    return pl.pallas_call(
        functools.partial(add_kernel, dims, 1),
        in_specs=[VMEM] * 4 + [ANYWHERE],
        out_specs=[ANYWHERE, VMEM],
        out_shape=[whole, jax.ShapeDtypeStruct(rate.shape, rate.dtype)],
        scratch_shapes=scratch,
        input_output_aliases={4: 0},
        compiler_params=PARAMS,
        name="add_received",
    )(own, got[1], rate, rate_got, grad)


def shards(counts, mark_value, base_rate, excite, block_col, row_fill):
    dims = excite.shape[:4]
    basis, _, _, tile = dims
    bins = counts.shape[0]
    overall = bins * lax.axis_size("tm")
    n = lax.axis_size("types")
    place = jnp.stack([lax.axis_index("types"), lax.axis_index("tm")]).astype(jnp.int32)
    order = list(range(0, n, 2)) + list(range(1, n, 2))[::-1]
    up = [(order[i], order[(i + 1) % n]) for i in range(n)]
    down = [(b, a) for a, b in up]
    swap = [(0, 1), (1, 0)]

    *chunks, ends = impact_chunks(counts, mark_value, dims, overall)
    enter = lax.ppermute(ends, "tm", [(0, 1)])
    chunks = add_carry(enter, *chunks, basis, bins)
    lag, power = lag_tables(bins, basis, overall, tile)
    plan = make_plan(place, block_col.reshape(-1), row_fill, dims, counts.shape[1] // tile, n)
    total = start_total(counts, base_rate.reshape(1, -1), dims)
    states = None
    built = []
    for step in range(n):
        ahead = None
        if step < n - 1:
            if step >= LATE - 1:
                chunks = [
                    lax.optimization_barrier((chunk, built[step - LATE + 1]))[0] for chunk in chunks
                ]
            ahead = [lax.ppermute(chunks[0], "types", up), lax.ppermute(chunks[1], "types", down)]
        states, total, done = take_step(
            step, plan, chunks, lag, power, excite, states, total, dims, n
        )
        built.append(done)
        chunks = ahead
    out, sent, kept, rate_sent, rate_kept = halves(plan, total, states, dims, overall)
    got = [lax.ppermute(out, "tm", swap)]
    rate_got = lax.ppermute(rate_sent, "tm", swap)
    got.append(
        lax.ppermute(store_products(1, plan, sent, states, dims, jnp.bfloat16), "tm", swap)
    )
    own = store_products(1, plan, kept, states, dims, jnp.float32)
    grad, rate = finish(dims, plan, kept, states, own, got, rate_kept, rate_got)
    return grad, rate.reshape(-1)


def solution(mesh):
    return jax.shard_map(
        shards,
        mesh=mesh,
        in_specs=(
            P(("parts", "tm"), "types"),
            P(("parts", "tm"), "types"),
            P("types"),
            P(None, "types", None, None, None),
            P(),
            P(),
        ),
        out_specs=(P("parts", "types", None, "tm", None), P(("parts", "types", "tm"))),
        check_vma=False,
    )
```

```python
import functools
import jax
import jax.numpy as jnp
from jax import lax
from jax.experimental import pallas as pl
from jax.experimental.pallas import tpu as pltpu
from jax.sharding import PartitionSpec as P

GROUPS = 2
SMEM = pl.BlockSpec(memory_space=pltpu.SMEM)
VMEM = pl.BlockSpec(memory_space=pltpu.VMEM)
ANYWHERE = pl.BlockSpec(memory_space=pl.ANY)
PARAMS = pltpu.CompilerParams(vmem_limit_bytes=16 << 20)


def lag_tables(bins, basis_count, overall, lanes):
    log_decay = -(8.0 ** jnp.arange(basis_count, dtype=jnp.float32)) / (2.0 * overall)
    t = jnp.arange(bins, dtype=jnp.float32)
    lag = t[:, None] - 1.0 - t[None, :]
    weights = jnp.where(
        lag[None] >= 0.0,
        (1.0 - jnp.exp(log_decay))[:, None, None]
        * jnp.exp(jnp.maximum(lag, 0.0)[None] * log_decay[:, None, None]),
        jnp.float32(0.0),
    )
    power = jnp.exp(t[None, :, None] * log_decay[:, None, None])
    return weights.astype(jnp.bfloat16), jnp.broadcast_to(power, (basis_count, bins, lanes))


def load_lanes(first, count, parts, counts_hbm, mark_hbm, counts, mark, sems):
    lanes = count // parts
    copies = []
    for j in range(parts):
        at = pl.ds(first + j * lanes, lanes)
        to = pl.ds(j * lanes, lanes)
        copies.append(
            (
                pltpu.make_async_copy(counts_hbm.at[:, at], counts.at[:, to], sems.at[0, j]),
                pltpu.make_async_copy(mark_hbm.at[:, at], mark.at[:, to], sems.at[1, j]),
            )
        )
        for copy in copies[-1]:
            copy.start()
    return copies


def impact_of(counts, mark, at):
    impact = counts[:, at].astype(jnp.float32) * mark[:, at].astype(jnp.float32)
    return impact.astype(jnp.bfloat16)


def first_kernel(counts_hbm, mark_hbm, out_ref, counts, mark, sems):
    bins, lanes = counts.shape
    tile = out_ref.shape[1]
    parts = sems.shape[1]
    copies = load_lanes(0, lanes, parts, counts_hbm, mark_hbm, counts, mark, sems)
    for j in range(parts):
        for copy in copies[j]:
            copy.wait()
        for q in range(j * lanes // parts // tile, (j + 1) * lanes // parts // tile):
            at = slice(q * tile, (q + 1) * tile)
            out_ref[q * bins : (q + 1) * bins] = impact_of(counts, mark, at)


def second_kernel(
    basis, tile, overall, counts_hbm, mark_hbm, out_ref, ends_ref, counts, mark, sems
):
    bins, types = counts.shape
    parts = sems.shape[1]
    lanes = types // parts
    copies = load_lanes(0, types, parts, counts_hbm, mark_hbm, counts, mark, sems)
    back = (bins - 1 - lax.broadcasted_iota(jnp.int32, (bins, tile), 0)).astype(jnp.float32)
    gains = []
    for b in range(basis):
        rate = (8.0**b) / (2.0 * overall)
        gains.append((1.0 - jnp.exp(jnp.full((bins, tile), -rate, jnp.float32))) * jnp.exp(-rate * back))
    half = types // tile // 2
    for j in range(parts):
        for copy in copies[j]:
            copy.wait()
        for block in range(j * lanes // tile, (j + 1) * lanes // tile):
            at = slice(block * tile, (block + 1) * tile)
            impact = impact_of(counts, mark, at)
            if block >= half:
                out_ref[(block - half) * bins : (block - half + 1) * bins] = impact
            impact = impact.astype(jnp.float32)
            for b in range(basis):
                ends_ref[b : b + 1, at] = jnp.sum(impact * gains[b], axis=0, keepdims=True)
    rest = out_ref.shape[0] - half * bins
    out_ref[half * bins :] = jnp.zeros((rest, tile), jnp.bfloat16)


def carry_rows(half, basis):
    return -(-half * basis // 16) * 16


def impact_messages(counts, mark, dims, overall):
    basis, _, _, tile = dims
    bins, types = counts.shape
    half = types // tile // 2
    params = pltpu.CompilerParams(vmem_limit_bytes=56 << 20)
    one = pl.pallas_call(
        first_kernel,
        in_specs=[ANYWHERE, ANYWHERE],
        out_specs=VMEM,
        out_shape=jax.ShapeDtypeStruct((half * bins, tile), jnp.bfloat16),
        scratch_shapes=[
            pltpu.VMEM((bins, types // 2), jnp.int32),
            pltpu.VMEM((bins, types // 2), jnp.bfloat16),
            pltpu.SemaphoreType.DMA((2, 2)),
        ],
        compiler_params=params,
        name="first_message",
    )(counts, mark)
    two, ends = pl.pallas_call(
        functools.partial(second_kernel, basis, tile, overall),
        in_specs=[ANYWHERE, ANYWHERE],
        out_specs=[VMEM, VMEM],
        out_shape=[
            jax.ShapeDtypeStruct((half * bins + 2 * carry_rows(half, basis), tile), jnp.bfloat16),
            jax.ShapeDtypeStruct((basis, types), jnp.float32),
        ],
        scratch_shapes=[
            pltpu.VMEM((bins, types), jnp.int32),
            pltpu.VMEM((bins, types), jnp.bfloat16),
            pltpu.SemaphoreType.DMA((2, 2)),
        ],
        compiler_params=params,
        name="second_message",
    )(counts, mark)
    return one, two, ends


def carry_kernel(basis, bins, enter_ref, _, out_ref, held, sem):
    rows, tile = out_ref.shape
    half = enter_ref.shape[1] // tile // 2
    each = carry_rows(half, basis)
    carry = []
    for d in range(2):
        for q in range(half):
            carry.append(enter_ref[:, (d * half + q) * tile : (d * half + q + 1) * tile])
        if each > half * basis:
            carry.append(jnp.zeros((each - half * basis, tile), jnp.float32))
    held[...] = jnp.concatenate(carry, axis=0).astype(jnp.bfloat16)
    copy = pltpu.make_async_copy(held, out_ref.at[pl.ds(half * bins, 2 * each)], sem)
    copy.start()
    copy.wait()


def add_carry(enter, two, basis, bins):
    rows, tile = two.shape
    return pl.pallas_call(
        functools.partial(carry_kernel, basis, bins),
        in_specs=[VMEM, ANYWHERE],
        out_specs=ANYWHERE,
        out_shape=jax.ShapeDtypeStruct(two.shape, two.dtype),
        scratch_shapes=[
            pltpu.VMEM((rows % bins, tile), jnp.bfloat16),
            pltpu.SemaphoreType.DMA,
        ],
        input_output_aliases={1: 0},
        compiler_params=PARAMS,
        name="carry_rows",
    )(enter, two)


def ring_place(index, n):
    return jnp.where(index % 2 == 0, index // 2, n - 1 - index // 2)


def code_of(row, slot, block):
    return (row * 256 + slot) * 256 + block


def plan_kernel(shape, place_ref, col_ref, fill_ref, plan_ref):
    brows, slots, width, n, most = shape
    own = place_ref[0]
    entries = brows * slots
    tail = n * (most + 1)
    plan_ref[tail] = place_ref[1]
    for step in range(n):
        plan_ref[step * (most + 1)] = 0

    @pl.loop(0, brows)
    def _(row):
        fill = fill_ref[own * brows + row]
        plan_ref[tail + 1 + row] = fill

        @pl.loop(0, fill)
        def _(slot):
            column = col_ref[own * entries + row * slots + slot]
            source = lax.div(column, width)
            block = lax.rem(column, width)
            ahead = ring_place(source, n) - ring_place(own, n)
            ahead = jnp.where(ahead < 0, ahead + n, ahead)
            second = (block >= width // 2).astype(jnp.int32)
            whole = (ahead == 0) | (ahead == n // 2)
            behind = (ahead > n // 2).astype(jnp.int32)
            hops = jnp.where(behind == 1, n - ahead, ahead)
            call = jnp.where(whole, jnp.where(ahead == 0, 0, n - 1), 2 * hops - 1 + second)
            place = block - (width // 2) * (second - 1 + behind)
            base = call * (most + 1)
            count = plan_ref[base] + 1
            plan_ref[base] = count
            plan_ref[base + count] = code_of(row, slot, jnp.where(whole, block, place))

    for step in range(n):
        base = step * (most + 1)
        count = plan_ref[base]

        @pl.when(lax.rem(count, 2) == 1)
        def _(base=base, count=count):
            plan_ref[base + count + 1] = code_of(brows, 0, 0)


def make_plan(place, cols, fill, dims, width, n):
    _, brows, slots, _ = dims
    most = 2 * max(2, brows * slots // n)
    return pl.pallas_call(
        functools.partial(plan_kernel, (brows, slots, width, n, most)),
        in_specs=[SMEM] * 3,
        out_specs=SMEM,
        out_shape=jax.ShapeDtypeStruct((n * (most + 1) + 1 + brows,), jnp.int32),
        name="plan",
    )(place, cols, fill)


def start_kernel(tile, counts_ref, base_ref, total_ref):
    for row in range(total_ref.shape[0] - 1):
        at = slice(row * tile, (row + 1) * tile)
        total_ref[row] = (base_ref[:, at] - counts_ref[:, at].astype(jnp.float32)).T
    total_ref[total_ref.shape[0] - 1] = jnp.zeros(total_ref.shape[1:], jnp.float32)


def start_total(counts, base_rate, dims):
    _, brows, _, tile = dims
    return pl.pallas_call(
        functools.partial(start_kernel, tile),
        in_specs=[VMEM, VMEM],
        out_specs=VMEM,
        out_shape=jax.ShapeDtypeStruct((brows + 1, tile, counts.shape[0]), jnp.float32),
        compiler_params=PARAMS,
        name="base_less_counts",
    )(counts, base_rate)


def step_kernel(dims, n, call, seconds, plan_ref, *refs):
    basis, brows, slots, tile = dims
    lag_ref, power_ref, excite_ref = refs[4:7]
    total_in, states_ref, total_ref, built_ref, held, sems = refs[-6:]
    bins = lag_ref.shape[1]
    half = held.shape[0] // 2
    each = carry_rows(half, basis)
    most = (plan_ref.shape[0] - 1 - brows) // n - 1
    built_ref[...] = jnp.zeros_like(built_ref)
    total_ref[...] = total_in[...]
    for d in range(2):
        impact_ref, carry_ref = refs[2 * d : 2 * d + 2]
        first = half * bins + seconds[d] * each
        carry = carry_ref[first : first + each].astype(jnp.float32)
        for q in range(0, half, 2):
            both = jnp.concatenate(
                [impact_ref[(q + i) * bins : (q + i + 1) * bins] for i in range(2)], axis=1
            )
            for b in range(basis):
                state = jnp.dot(lag_ref[b], both, preferred_element_type=jnp.float32)
                for i in range(2):
                    row = (q + i) * basis + b
                    held[d * half + q + i, :, b * tile : (b + 1) * tile] = (
                        state[:, i * tile : (i + 1) * tile] + power_ref[b] * carry[row : row + 1]
                    ).astype(jnp.bfloat16)

    def entry_at(place):
        code = plan_ref[call * (most + 1) + 1 + place]
        return code >> 16, (code >> 8) & 255, code & 255

    def copy_at(place):
        row, slot, block = entry_at(place)
        return pltpu.make_async_copy(
            held.at[block], states_ref.at[row * slots + slot], sems.at[place]
        )

    pairs = (plan_ref[call * (most + 1)] + 1) // 2

    @pl.loop(0, pairs)
    def _(k):
        terms = []
        for i in range(2):
            row, slot, block = entry_at(2 * k + i)
            copy_at(2 * k + i).start()
            inside = jnp.minimum(row, brows - 1)
            weight = jnp.concatenate([excite_ref[b, inside, slot] for b in range(basis)], axis=1)
            terms.append(
                (
                    row,
                    lax.dot_general(
                        weight,
                        held[block],
                        (((1,), (1,)), ((), ())),
                        preferred_element_type=jnp.float32,
                    ),
                )
            )
        for row, term in terms:
            total_ref[row] += term

    @pl.loop(0, 2 * pairs)
    def _(place):
        copy_at(place).wait()


def take_step(call, seconds, plan, arrived, lag, power, excite, states, total, dims, n):
    basis, brows, slots, tile = dims
    bins = lag.shape[1]
    half = arrived[0].shape[0] // bins
    most = (plan.shape[0] - 1 - brows) // n - 1
    given = [total] if states is None else [states, total]
    return pl.pallas_call(
        functools.partial(step_kernel, dims, n, call, seconds),
        in_specs=[SMEM] + [VMEM] * 7 + [ANYWHERE] * (len(given) - 1) + [VMEM],
        out_specs=[ANYWHERE, VMEM, VMEM],
        out_shape=[
            jax.ShapeDtypeStruct((brows * slots + 1, bins, basis * tile), jnp.bfloat16),
            jax.ShapeDtypeStruct(total.shape, total.dtype),
            jax.ShapeDtypeStruct((8, tile), jnp.float32),
        ],
        scratch_shapes=[
            pltpu.VMEM((2 * half, bins, basis * tile), jnp.bfloat16),
            pltpu.SemaphoreType.DMA((most,)),
        ],
        input_output_aliases={} if states is None else {8: 0},
        compiler_params=PARAMS,
        cost_estimate=pl.CostEstimate(
            flops=8 * basis * bins * bins * tile * 4,
            bytes_accessed=4 * 1024 * 1024,
            transcendentals=0,
        ),
        name="ring_step",
    )(plan, *arrived, lag, power, excite, *given)


def products(turned_ref, states_ref, plan_ref, group, dims, sent_ref, kept_ref):
    basis, brows, slots, tile = dims
    tail = plan_ref.shape[0] - 1 - brows
    part = tile // 2
    for r, row in enumerate(rows_of(group, dims)):
        fill = plan_ref[tail + 1 + row]
        for s in range(slots):
            grad = jnp.dot(
                turned_ref[row], states_ref[row * slots + s], preferred_element_type=jnp.float32
            )
            grad = jnp.where(s < fill, grad, jnp.zeros_like(grad))
            for b in range(basis):
                at = slice(b * tile, (b + 1) * tile)
                kept_ref[b, r, s] = grad[:part, at]
                sent_ref[b, r, s] = grad[part:, at].astype(sent_ref.dtype)


def rows_of(group, dims):
    count = dims[1] // GROUPS
    return range(group * count, (group + 1) * count)


def weighted_kernel(dims, overall, plan_ref, total_ref, states_ref, sent_ref, kept_ref, *refs):
    _, brows, _, tile = dims
    turned_ref, rate_sent_ref, rate_kept_ref = refs
    half = plan_ref[plan_ref.shape[0] - 1 - brows]
    part = tile // 2
    rates = []
    for row in range(brows):
        weighted = (2.0 / overall) * total_ref[row]
        rates.append(
            lax.dot_general(
                jnp.ones((8, weighted.shape[1]), jnp.float32),
                weighted,
                (((1,), (1,)), ((), ())),
                precision=lax.Precision.HIGHEST,
                preferred_element_type=jnp.float32,
            )[:1]
        )
        weighted = weighted.astype(jnp.bfloat16)
        upper, lower = weighted[:part], weighted[part:]
        turned_ref[row, :part] = jnp.where(half == 0, upper, lower)
        turned_ref[row, part:] = jnp.where(half == 0, lower, upper)
    first_half = jnp.concatenate(rates[: brows // 2], axis=0)
    second_half = jnp.concatenate(rates[brows // 2 :], axis=0)
    rate_kept_ref[...] = jnp.where(half == 0, first_half, second_half)
    rate_sent_ref[...] = jnp.where(half == 0, second_half, first_half)
    products(turned_ref, states_ref, plan_ref, 0, dims, sent_ref, kept_ref)


def later_kernel(dims, group, plan_ref, turned_ref, states_ref, sent_ref, kept_ref):
    products(turned_ref, states_ref, plan_ref, group, dims, sent_ref, kept_ref)


def group_shape(dims, dtype):
    basis, brows, slots, tile = dims
    return jax.ShapeDtypeStruct((basis, brows // GROUPS, slots, tile // 2, tile), dtype)


def first_products(plan, total, states, dims, overall):
    _, brows, _, tile = dims
    turned = jax.ShapeDtypeStruct((brows, tile, total.shape[2]), jnp.bfloat16)
    rate = jax.ShapeDtypeStruct((brows // 2, tile), jnp.float32)
    return pl.pallas_call(
        functools.partial(weighted_kernel, dims, overall),
        in_specs=[SMEM, VMEM, VMEM],
        out_specs=[VMEM] * 5,
        out_shape=[
            group_shape(dims, jnp.bfloat16),
            group_shape(dims, jnp.float32),
            turned,
            rate,
            rate,
        ],
        compiler_params=PARAMS,
        name="weighted_products",
    )(plan, total, states)


def later_products(group, plan, turned, states, dims):
    return pl.pallas_call(
        functools.partial(later_kernel, dims, group),
        in_specs=[SMEM, VMEM, VMEM],
        out_specs=[VMEM, VMEM],
        out_shape=[group_shape(dims, jnp.bfloat16), group_shape(dims, jnp.float32)],
        compiler_params=PARAMS,
        name="products",
    )(plan, turned, states)


def add_kernel(dims, group, kept_ref, got_ref, *refs):
    basis, brows, _, _ = dims
    out_ref, held, sems = refs[-3:]
    if group == GROUPS - 1:
        rate_ref, rate_got_ref, rate_out_ref = refs[0], refs[1], refs[-4]
        out_ref, rate_out_ref = rate_out_ref, out_ref
        rate_out_ref[...] = rate_ref[...] + rate_got_ref[...]
    copies = []
    for r, row in enumerate(rows_of(group, dims)):
        for b in range(basis):
            held[b, r] = (kept_ref[b, r] + got_ref[b, r].astype(jnp.float32)).astype(jnp.bfloat16)
            copies.append(
                pltpu.make_async_copy(held.at[b, r], out_ref.at[b, row], sems.at[b, r])
            )
            copies[-1].start()
    for copy in copies:
        copy.wait()


def add_received(group, kept, got, rates, grad, dims):
    basis, brows, slots, tile = dims
    whole = jax.ShapeDtypeStruct((basis, brows, slots, tile // 2, tile), jnp.bfloat16)
    given = [] if grad is None else [grad]
    last = group == GROUPS - 1
    return pl.pallas_call(
        functools.partial(add_kernel, dims, group),
        in_specs=[VMEM] * (2 + len(rates)) + [ANYWHERE] * len(given),
        out_specs=[ANYWHERE, VMEM] if last else [ANYWHERE],
        out_shape=[whole] + ([jax.ShapeDtypeStruct(rates[0].shape, jnp.float32)] if last else []),
        scratch_shapes=[
            pltpu.VMEM(group_shape(dims, jnp.bfloat16).shape, jnp.bfloat16),
            pltpu.SemaphoreType.DMA((basis, brows // GROUPS)),
        ],
        input_output_aliases={2 + len(rates): 0} if given else {},
        compiler_params=PARAMS,
        name="add_received",
    )(kept, got, *rates, *given)


def shards(counts, mark_value, base_rate, excite, block_col, row_fill):
    dims = excite.shape[:4]
    basis, _, _, tile = dims
    bins = counts.shape[0]
    overall = bins * lax.axis_size("tm")
    n = lax.axis_size("types")
    place = jnp.stack([lax.axis_index("types"), lax.axis_index("tm")]).astype(jnp.int32)
    order = list(range(0, n, 2)) + list(range(1, n, 2))[::-1]
    up = [(order[i], order[(i + 1) % n]) for i in range(n)]
    down = [(b, a) for a, b in up]
    swap = [(0, 1), (1, 0)]

    one, two, ends = impact_messages(counts, mark_value, dims, overall)
    enter = lax.ppermute(ends, "tm", [(0, 1)])
    two = add_carry(enter, two, basis, bins)
    lag, power = lag_tables(bins, basis, overall, tile)
    plan = make_plan(place, block_col.reshape(-1), row_fill, dims, counts.shape[1] // tile, n)
    total = start_total(counts, base_rate.reshape(1, -1), dims)

    states = None
    built = []

    def step(call, seconds, arrived):
        nonlocal states, total
        states, total, done = take_step(
            call, seconds, plan, arrived, lag, power, excite, states, total, dims, n
        )
        built.append(done)

    def send(message, way, hop):
        if hop > 2:
            message = lax.optimization_barrier((message, built[2 * hop - 4]))[0]
        return lax.ppermute(message, "types", way)

    hops = n // 2
    at_up, at_down = [one, two], [one, two]
    for hop in range(1, hops + 1):
        if hop < hops:
            next_up, next_down = [None, None], [None, None]
            for second in range(2):
                next_up[second] = send(at_up[second], up, hop)
                next_down[second] = send(at_down[second], down, hop)
        else:
            next_up = [send(at_up[0], up, hop), None]
            next_down = [None, send(at_down[1], down, hop)]
        if hop == 1:
            step(0, (0, 1), [one, two, two, two])
        else:
            for second in range(2):
                step(
                    2 * hop - 3 + second,
                    (second, second),
                    [at_up[second], at_up[1], at_down[second], at_down[1]],
                )
        at_up, at_down = next_up, next_down
    step(n - 1, (0, 1), [at_up[0], at_down[1], at_down[1], at_down[1]])

    out, kept, turned, rate_sent, rate_kept = first_products(plan, total, states, dims, overall)
    kept = [kept]
    got = [lax.ppermute(out, "tm", swap)]
    rate_got = lax.ppermute(rate_sent, "tm", swap)
    for group in range(1, GROUPS):
        out, more = later_products(group, plan, turned, states, dims)
        kept.append(more)
        got.append(lax.ppermute(out, "tm", swap))
    grad = None
    for group in range(GROUPS):
        rates = [rate_kept, rate_got] if group == GROUPS - 1 else []
        grad, *rate = add_received(group, kept[group], got[group], rates, grad, dims)
    return grad, rate[0].reshape(-1)


def solution(mesh):
    return jax.shard_map(
        shards,
        mesh=mesh,
        in_specs=(
            P(("parts", "tm"), "types"),
            P(("parts", "tm"), "types"),
            P("types"),
            P(None, "types", None, None, None),
            P(),
            P(),
        ),
        out_specs=(P("parts", "types", None, "tm", None), P(("parts", "types", "tm"))),
        check_vma=False,
    )
```

```python
import functools
import jax
import jax.numpy as jnp
from jax import lax
from jax.experimental import pallas as pl
from jax.experimental.pallas import tpu as pltpu
from jax.sharding import PartitionSpec as P

GROUPS = 2
SMEM = pl.BlockSpec(memory_space=pltpu.SMEM)
VMEM = pl.BlockSpec(memory_space=pltpu.VMEM)
ANYWHERE = pl.BlockSpec(memory_space=pl.ANY)
PARAMS = pltpu.CompilerParams(vmem_limit_bytes=16 << 20)


def lag_tables(bins, basis_count, overall, lanes):
    log_decay = -(8.0 ** jnp.arange(basis_count, dtype=jnp.float32)) / (2.0 * overall)
    t = jnp.arange(bins, dtype=jnp.float32)
    lag = t[:, None] - 1.0 - t[None, :]
    weights = jnp.where(
        lag[None] >= 0.0,
        (1.0 - jnp.exp(log_decay))[:, None, None]
        * jnp.exp(jnp.maximum(lag, 0.0)[None] * log_decay[:, None, None]),
        jnp.float32(0.0),
    )
    power = jnp.exp(t[None, :, None] * log_decay[:, None, None])
    return weights.astype(jnp.bfloat16), jnp.broadcast_to(power, (basis_count, bins, lanes))


def load_lanes(first, count, parts, counts_hbm, mark_hbm, counts, mark, sems):
    lanes = count // parts
    copies = []
    for j in range(parts):
        at = pl.ds(first + j * lanes, lanes)
        to = pl.ds(j * lanes, lanes)
        copies.append(
            (
                pltpu.make_async_copy(counts_hbm.at[:, at], counts.at[:, to], sems.at[0, j]),
                pltpu.make_async_copy(mark_hbm.at[:, at], mark.at[:, to], sems.at[1, j]),
            )
        )
        for copy in copies[-1]:
            copy.start()
    return copies


def impact_of(counts, mark, at):
    impact = counts[:, at].astype(jnp.float32) * mark[:, at].astype(jnp.float32)
    return impact.astype(jnp.bfloat16)


def first_kernel(counts_hbm, mark_hbm, out_ref, counts, mark, sems):
    bins, lanes = counts.shape
    tile = out_ref.shape[1]
    parts = sems.shape[1]
    copies = load_lanes(0, lanes, parts, counts_hbm, mark_hbm, counts, mark, sems)
    for j in range(parts):
        for copy in copies[j]:
            copy.wait()
        for q in range(j * lanes // parts // tile, (j + 1) * lanes // parts // tile):
            at = slice(q * tile, (q + 1) * tile)
            out_ref[q * bins : (q + 1) * bins] = impact_of(counts, mark, at)


def second_kernel(
    basis, tile, overall, counts_hbm, mark_hbm, out_ref, ends_ref, counts, mark, sems
):
    bins, types = counts.shape
    parts = sems.shape[1]
    lanes = types // parts
    copies = load_lanes(0, types, parts, counts_hbm, mark_hbm, counts, mark, sems)
    back = (bins - 1 - lax.broadcasted_iota(jnp.int32, (bins, tile), 0)).astype(jnp.float32)
    gains = []
    for b in range(basis):
        rate = (8.0**b) / (2.0 * overall)
        gains.append((1.0 - jnp.exp(jnp.full((bins, tile), -rate, jnp.float32))) * jnp.exp(-rate * back))
    half = types // tile // 2
    for j in range(parts):
        for copy in copies[j]:
            copy.wait()
        for block in range(j * lanes // tile, (j + 1) * lanes // tile):
            at = slice(block * tile, (block + 1) * tile)
            impact = impact_of(counts, mark, at)
            if block >= half:
                out_ref[(block - half) * bins : (block - half + 1) * bins] = impact
            impact = impact.astype(jnp.float32)
            for b in range(basis):
                ends_ref[b : b + 1, at] = jnp.sum(impact * gains[b], axis=0, keepdims=True)
    rest = out_ref.shape[0] - half * bins
    out_ref[half * bins :] = jnp.zeros((rest, tile), jnp.bfloat16)


def carry_rows(half, basis):
    return -(-half * basis // 16) * 16


def impact_messages(counts, mark, dims, overall):
    basis, _, _, tile = dims
    bins, types = counts.shape
    half = types // tile // 2
    params = pltpu.CompilerParams(vmem_limit_bytes=56 << 20)
    one = pl.pallas_call(
        first_kernel,
        in_specs=[ANYWHERE, ANYWHERE],
        out_specs=VMEM,
        out_shape=jax.ShapeDtypeStruct((half * bins, tile), jnp.bfloat16),
        scratch_shapes=[
            pltpu.VMEM((bins, types // 2), jnp.int32),
            pltpu.VMEM((bins, types // 2), jnp.bfloat16),
            pltpu.SemaphoreType.DMA((2, 2)),
        ],
        compiler_params=params,
        name="first_message",
    )(counts, mark)
    two, ends = pl.pallas_call(
        functools.partial(second_kernel, basis, tile, overall),
        in_specs=[ANYWHERE, ANYWHERE],
        out_specs=[VMEM, VMEM],
        out_shape=[
            jax.ShapeDtypeStruct((half * bins + 2 * carry_rows(half, basis), tile), jnp.bfloat16),
            jax.ShapeDtypeStruct((basis, types), jnp.float32),
        ],
        scratch_shapes=[
            pltpu.VMEM((bins, types), jnp.int32),
            pltpu.VMEM((bins, types), jnp.bfloat16),
            pltpu.SemaphoreType.DMA((2, 2)),
        ],
        compiler_params=params,
        name="second_message",
    )(counts, mark)
    return one, two, ends


def carry_kernel(basis, bins, enter_ref, _, out_ref, held, sem):
    rows, tile = out_ref.shape
    half = enter_ref.shape[1] // tile // 2
    each = carry_rows(half, basis)
    carry = []
    for d in range(2):
        for q in range(half):
            carry.append(enter_ref[:, (d * half + q) * tile : (d * half + q + 1) * tile])
        if each > half * basis:
            carry.append(jnp.zeros((each - half * basis, tile), jnp.float32))
    held[...] = jnp.concatenate(carry, axis=0).astype(jnp.bfloat16)
    copy = pltpu.make_async_copy(held, out_ref.at[pl.ds(half * bins, 2 * each)], sem)
    copy.start()
    copy.wait()


def add_carry(enter, two, basis, bins):
    rows, tile = two.shape
    return pl.pallas_call(
        functools.partial(carry_kernel, basis, bins),
        in_specs=[VMEM, ANYWHERE],
        out_specs=ANYWHERE,
        out_shape=jax.ShapeDtypeStruct(two.shape, two.dtype),
        scratch_shapes=[
            pltpu.VMEM((rows % bins, tile), jnp.bfloat16),
            pltpu.SemaphoreType.DMA,
        ],
        input_output_aliases={1: 0},
        compiler_params=PARAMS,
        name="carry_rows",
    )(enter, two)


def ring_place(index, n):
    return jnp.where(index % 2 == 0, index // 2, n - 1 - index // 2)


def code_of(row, slot, block):
    return (row * 256 + slot) * 256 + block


def plan_kernel(shape, col_ref, fill_ref, plan_ref):
    brows, slots, width, n, most = shape
    own = lax.axis_index("types")
    tail = n * (most + 1)
    plan_ref[tail] = lax.axis_index("tm")
    for step in range(n):
        plan_ref[step * (most + 1)] = 0

    @pl.loop(0, brows)
    def _(row):
        fill = fill_ref[own * brows + row]
        plan_ref[tail + 1 + row] = fill

        @pl.loop(0, fill)
        def _(slot):
            column = col_ref[own * brows + row, slot]
            source = lax.div(column, width)
            block = lax.rem(column, width)
            ahead = ring_place(source, n) - ring_place(own, n)
            ahead = jnp.where(ahead < 0, ahead + n, ahead)
            second = (block >= width // 2).astype(jnp.int32)
            whole = (ahead == 0) | (ahead == n // 2)
            behind = (ahead > n // 2).astype(jnp.int32)
            hops = jnp.where(behind == 1, n - ahead, ahead)
            call = jnp.where(whole, jnp.where(ahead == 0, 0, n - 1), 2 * hops - 1 + second)
            place = block - (width // 2) * (second - 1 + behind)
            base = call * (most + 1)
            count = plan_ref[base] + 1
            plan_ref[base] = count
            plan_ref[base + count] = code_of(row, slot, jnp.where(whole, block, place))

    for step in range(n):
        base = step * (most + 1)
        count = plan_ref[base]

        @pl.when(lax.rem(count, 2) == 1)
        def _(base=base, count=count):
            plan_ref[base + count + 1] = code_of(brows, 0, 0)


def make_plan(cols, fill, dims, width, n):
    _, brows, slots, _ = dims
    most = 2 * max(2, brows * slots // n)
    return pl.pallas_call(
        functools.partial(plan_kernel, (brows, slots, width, n, most)),
        in_specs=[SMEM] * 2,
        out_specs=SMEM,
        out_shape=jax.ShapeDtypeStruct((n * (most + 1) + 1 + brows,), jnp.int32),
        compiler_params=PARAMS,
        name="plan",
    )(cols, fill)


def start_kernel(tile, counts_ref, base_ref, total_ref):
    for row in range(total_ref.shape[0] - 1):
        at = slice(row * tile, (row + 1) * tile)
        total_ref[row] = base_ref[:, at] - counts_ref[:, at].astype(jnp.float32)
    total_ref[total_ref.shape[0] - 1] = jnp.zeros(total_ref.shape[1:], jnp.float32)


def start_total(counts, base_rate, dims):
    _, brows, _, tile = dims
    return pl.pallas_call(
        functools.partial(start_kernel, tile),
        in_specs=[VMEM, VMEM],
        out_specs=VMEM,
        out_shape=jax.ShapeDtypeStruct((brows + 1, counts.shape[0], tile), jnp.float32),
        compiler_params=PARAMS,
        name="base_less_counts",
    )(counts, base_rate)


def step_kernel(dims, n, call, seconds, plan_ref, *refs):
    basis, brows, slots, tile = dims
    lag_ref, power_ref, excite_ref = refs[4:7]
    total_in, states_ref, total_ref, built_ref, held, weights, sems = refs[-7:]
    bins = lag_ref.shape[1]
    half = held.shape[0] // 2
    each = carry_rows(half, basis)
    most = (plan_ref.shape[0] - 1 - brows) // n - 1
    built_ref[...] = jnp.zeros_like(built_ref)
    pairs = (plan_ref[call * (most + 1)] + 1) // 2

    def entry_at(place):
        code = plan_ref[call * (most + 1) + 1 + place]
        return code >> 16, (code >> 8) & 255, code & 255

    def weight_at(place):
        row, slot, _ = entry_at(place)
        return pltpu.make_async_copy(
            excite_ref.at[:, jnp.minimum(row, brows - 1), slot],
            weights.at[place],
            sems.at[0, place],
        )

    def copy_at(place):
        row, slot, block = entry_at(place)
        return pltpu.make_async_copy(
            held.at[block], states_ref.at[row * slots + slot], sems.at[1, place]
        )

    @pl.loop(0, 2 * pairs)
    def _(place):
        weight_at(place).start()

    total_ref[...] = total_in[...]
    for d in range(2):
        impact_ref, carry_ref = refs[2 * d : 2 * d + 2]
        first = half * bins + seconds[d] * each
        carry = carry_ref[first : first + each].astype(jnp.float32)
        for q in range(0, half, 2):
            both = jnp.concatenate(
                [impact_ref[(q + i) * bins : (q + i + 1) * bins] for i in range(2)], axis=1
            )
            for b in range(basis):
                state = jnp.dot(lag_ref[b], both, preferred_element_type=jnp.float32)
                for i in range(2):
                    row = (q + i) * basis + b
                    held[d * half + q + i, :, b * tile : (b + 1) * tile] = (
                        state[:, i * tile : (i + 1) * tile] + power_ref[b] * carry[row : row + 1]
                    ).astype(jnp.bfloat16)

    @pl.loop(0, pairs)
    def _(k):
        terms = []
        for i in range(2):
            row, _, block = entry_at(2 * k + i)
            copy_at(2 * k + i).start()
            weight_at(2 * k + i).wait()
            weight = jnp.concatenate([weights[2 * k + i, b] for b in range(basis)], axis=1)
            term = lax.dot_general(
                held[block], weight, (((1,), (1,)), ((), ())), preferred_element_type=jnp.float32
            )
            terms.append((row, term))
        for row, term in terms:
            total_ref[row] += term

    @pl.loop(0, 2 * pairs)
    def _(place):
        copy_at(place).wait()


def take_step(call, seconds, plan, arrived, lag, power, excite, states, total, dims, n):
    basis, brows, slots, tile = dims
    bins = lag.shape[1]
    half = arrived[0].shape[0] // bins
    most = (plan.shape[0] - 1 - brows) // n - 1
    given = [total] if states is None else [states, total]
    return pl.pallas_call(
        functools.partial(step_kernel, dims, n, call, seconds),
        in_specs=[SMEM] + [VMEM] * 6 + [ANYWHERE] * len(given) + [VMEM],
        out_specs=[ANYWHERE, VMEM, VMEM],
        out_shape=[
            jax.ShapeDtypeStruct((brows * slots + 1, bins, basis * tile), jnp.bfloat16),
            jax.ShapeDtypeStruct(total.shape, total.dtype),
            jax.ShapeDtypeStruct((8, tile), jnp.float32),
        ],
        scratch_shapes=[
            pltpu.VMEM((2 * half, bins, basis * tile), jnp.bfloat16),
            pltpu.VMEM((most, basis, tile, tile), jnp.bfloat16),
            pltpu.SemaphoreType.DMA((2, most)),
        ],
        input_output_aliases={} if states is None else {8: 0},
        compiler_params=PARAMS,
        cost_estimate=pl.CostEstimate(
            flops=8 * basis * bins * bins * tile * 4,
            bytes_accessed=4 * 1024 * 1024,
            transcendentals=0,
        ),
        name="ring_step",
    )(plan, *arrived, lag, power, excite, *given)


def products(turned_ref, states_ref, plan_ref, group, dims, sent_ref, kept_ref):
    basis, brows, slots, tile = dims
    tail = plan_ref.shape[0] - 1 - brows
    part = tile // 2
    for r, row in enumerate(rows_of(group, dims)):
        fill = plan_ref[tail + 1 + row]
        for s in range(slots):
            grad = jnp.dot(
                turned_ref[row], states_ref[row * slots + s], preferred_element_type=jnp.float32
            )
            grad = jnp.where(s < fill, grad, jnp.zeros_like(grad))
            for b in range(basis):
                at = slice(b * tile, (b + 1) * tile)
                kept_ref[b, r, s] = grad[:part, at]
                sent_ref[b, r, s] = grad[part:, at].astype(sent_ref.dtype)


def rows_of(group, dims):
    count = dims[1] // GROUPS
    return range(group * count, (group + 1) * count)


def weighted_kernel(dims, overall, plan_ref, total_ref, states_ref, sent_ref, kept_ref, *refs):
    _, brows, _, tile = dims
    turned_ref, rate_sent_ref, rate_kept_ref = refs
    half = plan_ref[plan_ref.shape[0] - 1 - brows]
    part = tile // 2
    rates = []
    for row in range(brows):
        weighted = (2.0 / overall) * total_ref[row]
        rates.append(jnp.sum(weighted, axis=0, keepdims=True))
        weighted = weighted.T.astype(jnp.bfloat16)
        upper, lower = weighted[:part], weighted[part:]
        turned_ref[row, :part] = jnp.where(half == 0, upper, lower)
        turned_ref[row, part:] = jnp.where(half == 0, lower, upper)
    first_half = jnp.concatenate(rates[: brows // 2], axis=0)
    second_half = jnp.concatenate(rates[brows // 2 :], axis=0)
    rate_kept_ref[...] = jnp.where(half == 0, first_half, second_half)
    rate_sent_ref[...] = jnp.where(half == 0, second_half, first_half)
    products(turned_ref, states_ref, plan_ref, 0, dims, sent_ref, kept_ref)


def later_kernel(dims, group, plan_ref, turned_ref, states_ref, sent_ref, kept_ref):
    products(turned_ref, states_ref, plan_ref, group, dims, sent_ref, kept_ref)


def group_shape(dims, dtype):
    basis, brows, slots, tile = dims
    return jax.ShapeDtypeStruct((basis, brows // GROUPS, slots, tile // 2, tile), dtype)


def first_products(plan, total, states, dims, overall):
    _, brows, _, tile = dims
    turned = jax.ShapeDtypeStruct((brows, tile, total.shape[1]), jnp.bfloat16)
    rate = jax.ShapeDtypeStruct((brows // 2, tile), jnp.float32)
    return pl.pallas_call(
        functools.partial(weighted_kernel, dims, overall),
        in_specs=[SMEM, VMEM, VMEM],
        out_specs=[VMEM] * 5,
        out_shape=[
            group_shape(dims, jnp.bfloat16),
            group_shape(dims, jnp.float32),
            turned,
            rate,
            rate,
        ],
        compiler_params=PARAMS,
        name="weighted_products",
    )(plan, total, states)


def later_products(group, plan, turned, states, dims):
    return pl.pallas_call(
        functools.partial(later_kernel, dims, group),
        in_specs=[SMEM, VMEM, VMEM],
        out_specs=[VMEM, VMEM],
        out_shape=[group_shape(dims, jnp.bfloat16), group_shape(dims, jnp.float32)],
        compiler_params=PARAMS,
        name="products",
    )(plan, turned, states)


def add_kernel(dims, group, kept_ref, got_ref, *refs):
    basis, brows, _, _ = dims
    out_ref, held, sems = refs[-3:]
    if group == GROUPS - 1:
        rate_ref, rate_got_ref, rate_out_ref = refs[0], refs[1], refs[-4]
        out_ref, rate_out_ref = rate_out_ref, out_ref
        rate_out_ref[...] = rate_ref[...] + rate_got_ref[...]
    copies = []
    for r, row in enumerate(rows_of(group, dims)):
        for b in range(basis):
            held[b, r] = (kept_ref[b, r] + got_ref[b, r].astype(jnp.float32)).astype(jnp.bfloat16)
            copies.append(
                pltpu.make_async_copy(held.at[b, r], out_ref.at[b, row], sems.at[b, r])
            )
            copies[-1].start()
    for copy in copies:
        copy.wait()


def add_received(group, kept, got, rates, grad, dims):
    basis, brows, slots, tile = dims
    whole = jax.ShapeDtypeStruct((basis, brows, slots, tile // 2, tile), jnp.bfloat16)
    given = [] if grad is None else [grad]
    last = group == GROUPS - 1
    return pl.pallas_call(
        functools.partial(add_kernel, dims, group),
        in_specs=[VMEM] * (2 + len(rates)) + [ANYWHERE] * len(given),
        out_specs=[ANYWHERE, VMEM] if last else [ANYWHERE],
        out_shape=[whole] + ([jax.ShapeDtypeStruct(rates[0].shape, jnp.float32)] if last else []),
        scratch_shapes=[
            pltpu.VMEM(group_shape(dims, jnp.bfloat16).shape, jnp.bfloat16),
            pltpu.SemaphoreType.DMA((basis, brows // GROUPS)),
        ],
        input_output_aliases={2 + len(rates): 0} if given else {},
        compiler_params=PARAMS,
        name="add_received",
    )(kept, got, *rates, *given)


def shards(counts, mark_value, base_rate, excite, block_col, row_fill):
    dims = excite.shape[:4]
    basis, _, _, tile = dims
    bins = counts.shape[0]
    overall = bins * lax.axis_size("tm")
    n = lax.axis_size("types")
    order = list(range(0, n, 2)) + list(range(1, n, 2))[::-1]
    up = [(order[i], order[(i + 1) % n]) for i in range(n)]
    down = [(b, a) for a, b in up]
    swap = [(0, 1), (1, 0)]

    one, two, ends = impact_messages(counts, mark_value, dims, overall)
    enter = lax.ppermute(ends, "tm", [(0, 1)])
    two = add_carry(enter, two, basis, bins)
    lag, power = lag_tables(bins, basis, overall, tile)
    plan = make_plan(block_col, row_fill, dims, counts.shape[1] // tile, n)
    total = start_total(counts, base_rate.reshape(1, -1), dims)

    states = None
    built = []

    def step(call, seconds, arrived):
        nonlocal states, total
        states, total, done = take_step(
            call, seconds, plan, arrived, lag, power, excite, states, total, dims, n
        )
        built.append(done)

    def send(message, way, hop):
        if hop > 2:
            message = lax.optimization_barrier((message, built[2 * hop - 4]))[0]
        return lax.ppermute(message, "types", way)

    hops = n // 2
    at_up, at_down = [one, two], [one, two]
    for hop in range(1, hops + 1):
        if hop < hops:
            next_up, next_down = [None, None], [None, None]
            for second in range(2):
                next_up[second] = send(at_up[second], up, hop)
                next_down[second] = send(at_down[second], down, hop)
        else:
            next_up = [send(at_up[0], up, hop), None]
            next_down = [None, send(at_down[1], down, hop)]
        if hop == 1:
            step(0, (0, 1), [one, two, two, two])
        else:
            for second in range(2):
                step(
                    2 * hop - 3 + second,
                    (second, second),
                    [at_up[second], at_up[1], at_down[second], at_down[1]],
                )
        at_up, at_down = next_up, next_down
    step(n - 1, (0, 1), [at_up[0], at_down[1], at_down[1], at_down[1]])

    out, kept, turned, rate_sent, rate_kept = first_products(plan, total, states, dims, overall)
    kept = [kept]
    got = [lax.ppermute(out, "tm", swap)]
    rate_got = lax.ppermute(rate_sent, "tm", swap)
    for group in range(1, GROUPS):
        out, more = later_products(group, plan, turned, states, dims)
        kept.append(more)
        got.append(lax.ppermute(out, "tm", swap))
    grad = None
    for group in range(GROUPS):
        rates = [rate_kept, rate_got] if group == GROUPS - 1 else []
        grad, *rate = add_received(group, kept[group], got[group], rates, grad, dims)
    return grad, rate[0].reshape(-1)


def solution(mesh):
    return jax.shard_map(
        shards,
        mesh=mesh,
        in_specs=(
            P(("parts", "tm"), "types"),
            P(("parts", "tm"), "types"),
            P("types"),
            P(None, "types", None, None, None),
            P(),
            P(),
        ),
        out_specs=(P("parts", "types", None, "tm", None), P(("parts", "types", "tm"))),
        check_vma=False,
    )
```

```python
import functools
import jax
import jax.numpy as jnp
from jax import lax
from jax.experimental import pallas as pl
from jax.experimental.pallas import tpu as pltpu
from jax.sharding import PartitionSpec as P

GROUPS = 2
SMEM = pl.BlockSpec(memory_space=pltpu.SMEM)
VMEM = pl.BlockSpec(memory_space=pltpu.VMEM)
ANYWHERE = pl.BlockSpec(memory_space=pl.ANY)
PARAMS = pltpu.CompilerParams(vmem_limit_bytes=16 << 20)


def lag_tables(bins, basis_count, overall, lanes):
    log_decay = -(8.0 ** jnp.arange(basis_count, dtype=jnp.float32)) / (2.0 * overall)
    t = jnp.arange(bins, dtype=jnp.float32)
    lag = t[:, None] - 1.0 - t[None, :]
    weights = jnp.where(
        lag[None] >= 0.0,
        (1.0 - jnp.exp(log_decay))[:, None, None]
        * jnp.exp(jnp.maximum(lag, 0.0)[None] * log_decay[:, None, None]),
        jnp.float32(0.0),
    )
    power = jnp.exp(t[None, :, None] * log_decay[:, None, None])
    return weights.astype(jnp.bfloat16), jnp.broadcast_to(power, (basis_count, bins, lanes))


def load_lanes(first, count, parts, counts_hbm, mark_hbm, counts, mark, sems):
    lanes = count // parts
    copies = []
    for j in range(parts):
        at = pl.ds(first + j * lanes, lanes)
        to = pl.ds(j * lanes, lanes)
        copies.append(
            (
                pltpu.make_async_copy(counts_hbm.at[:, at], counts.at[:, to], sems.at[0, j]),
                pltpu.make_async_copy(mark_hbm.at[:, at], mark.at[:, to], sems.at[1, j]),
            )
        )
        for copy in copies[-1]:
            copy.start()
    return copies


def impact_of(counts, mark, at):
    impact = counts[:, at].astype(jnp.float32) * mark[:, at].astype(jnp.float32)
    return impact.astype(jnp.bfloat16)


def first_kernel(counts_hbm, mark_hbm, out_ref, counts, mark, sems):
    bins, lanes = counts.shape
    tile = out_ref.shape[1]
    parts = sems.shape[1]
    copies = load_lanes(0, lanes, parts, counts_hbm, mark_hbm, counts, mark, sems)
    for j in range(parts):
        for copy in copies[j]:
            copy.wait()
        for q in range(j * lanes // parts // tile, (j + 1) * lanes // parts // tile):
            at = slice(q * tile, (q + 1) * tile)
            out_ref[q * bins : (q + 1) * bins] = impact_of(counts, mark, at)


def second_kernel(
    basis, tile, overall, counts_hbm, mark_hbm, out_ref, ends_ref, counts, mark, sems
):
    bins, types = counts.shape
    parts = sems.shape[1]
    lanes = types // parts
    copies = load_lanes(0, types, parts, counts_hbm, mark_hbm, counts, mark, sems)
    back = (bins - 1 - lax.broadcasted_iota(jnp.int32, (bins, tile), 0)).astype(jnp.float32)
    gains = []
    for b in range(basis):
        rate = (8.0**b) / (2.0 * overall)
        gains.append((1.0 - jnp.exp(jnp.full((bins, tile), -rate, jnp.float32))) * jnp.exp(-rate * back))
    half = types // tile // 2
    for j in range(parts):
        for copy in copies[j]:
            copy.wait()
        for block in range(j * lanes // tile, (j + 1) * lanes // tile):
            at = slice(block * tile, (block + 1) * tile)
            impact = impact_of(counts, mark, at)
            if block >= half:
                out_ref[(block - half) * bins : (block - half + 1) * bins] = impact
            impact = impact.astype(jnp.float32)
            for b in range(basis):
                ends_ref[b : b + 1, at] = jnp.sum(impact * gains[b], axis=0, keepdims=True)
    rest = out_ref.shape[0] - half * bins
    out_ref[half * bins :] = jnp.zeros((rest, tile), jnp.bfloat16)


def carry_rows(half, basis):
    return -(-half * basis // 16) * 16


def impact_messages(counts, mark, dims, overall):
    basis, _, _, tile = dims
    bins, types = counts.shape
    half = types // tile // 2
    params = pltpu.CompilerParams(vmem_limit_bytes=56 << 20)
    one = pl.pallas_call(
        first_kernel,
        in_specs=[ANYWHERE, ANYWHERE],
        out_specs=VMEM,
        out_shape=jax.ShapeDtypeStruct((half * bins, tile), jnp.bfloat16),
        scratch_shapes=[
            pltpu.VMEM((bins, types // 2), jnp.int32),
            pltpu.VMEM((bins, types // 2), jnp.bfloat16),
            pltpu.SemaphoreType.DMA((2, 2)),
        ],
        compiler_params=params,
        name="first_message",
    )(counts, mark)
    two, ends = pl.pallas_call(
        functools.partial(second_kernel, basis, tile, overall),
        in_specs=[ANYWHERE, ANYWHERE],
        out_specs=[VMEM, VMEM],
        out_shape=[
            jax.ShapeDtypeStruct((half * bins + 2 * carry_rows(half, basis), tile), jnp.bfloat16),
            jax.ShapeDtypeStruct((basis, types), jnp.float32),
        ],
        scratch_shapes=[
            pltpu.VMEM((bins, types), jnp.int32),
            pltpu.VMEM((bins, types), jnp.bfloat16),
            pltpu.SemaphoreType.DMA((2, 2)),
        ],
        compiler_params=params,
        name="second_message",
    )(counts, mark)
    return one, two, ends


def carry_kernel(basis, bins, enter_ref, _, out_ref, held, sem):
    rows, tile = out_ref.shape
    half = enter_ref.shape[1] // tile // 2
    each = carry_rows(half, basis)
    carry = []
    for d in range(2):
        for q in range(half):
            carry.append(enter_ref[:, (d * half + q) * tile : (d * half + q + 1) * tile])
        if each > half * basis:
            carry.append(jnp.zeros((each - half * basis, tile), jnp.float32))
    held[...] = jnp.concatenate(carry, axis=0).astype(jnp.bfloat16)
    copy = pltpu.make_async_copy(held, out_ref.at[pl.ds(half * bins, 2 * each)], sem)
    copy.start()
    copy.wait()


def add_carry(enter, two, basis, bins):
    rows, tile = two.shape
    return pl.pallas_call(
        functools.partial(carry_kernel, basis, bins),
        in_specs=[VMEM, ANYWHERE],
        out_specs=ANYWHERE,
        out_shape=jax.ShapeDtypeStruct(two.shape, two.dtype),
        scratch_shapes=[
            pltpu.VMEM((rows % bins, tile), jnp.bfloat16),
            pltpu.SemaphoreType.DMA,
        ],
        input_output_aliases={1: 0},
        compiler_params=PARAMS,
        name="carry_rows",
    )(enter, two)


def ring_place(index, n):
    return jnp.where(index % 2 == 0, index // 2, n - 1 - index // 2)


def code_of(row, slot, block):
    return (row * 256 + slot) * 256 + block


def plan_kernel(shape, col_ref, fill_ref, plan_ref):
    brows, slots, width, n, most = shape
    own = lax.axis_index("types")
    calls = n // 2 + 1
    tail = calls * (most + 1)
    plan_ref[tail] = lax.axis_index("tm")
    for step in range(calls):
        plan_ref[step * (most + 1)] = 0

    @pl.loop(0, brows)
    def _(row):
        fill = fill_ref[own * brows + row]
        plan_ref[tail + 1 + row] = fill

        @pl.loop(0, fill)
        def _(slot):
            column = col_ref[own * brows + row, slot]
            source = lax.div(column, width)
            block = lax.rem(column, width)
            ahead = ring_place(source, n) - ring_place(own, n)
            ahead = jnp.where(ahead < 0, ahead + n, ahead)
            call = jnp.minimum(ahead, n - ahead)
            down = (ahead > 0) & (ahead < n // 2)
            base = call * (most + 1)
            count = plan_ref[base] + 1
            plan_ref[base] = count
            plan_ref[base + count] = code_of(row, slot, jnp.where(down, width + block, block))

    for step in range(calls):
        base = step * (most + 1)
        count = plan_ref[base]

        @pl.when(lax.rem(count, 2) == 1)
        def _(base=base, count=count):
            plan_ref[base + count + 1] = code_of(brows, 0, 0)


def make_plan(cols, fill, dims, width, n):
    _, brows, slots, _ = dims
    most = 2 * max(2, brows * slots // n)
    return pl.pallas_call(
        functools.partial(plan_kernel, (brows, slots, width, n, most)),
        in_specs=[SMEM] * 2,
        out_specs=SMEM,
        out_shape=jax.ShapeDtypeStruct(((n // 2 + 1) * (most + 1) + 1 + brows,), jnp.int32),
        compiler_params=PARAMS,
        name="plan",
    )(cols, fill)


def start_kernel(tile, counts_ref, base_ref, total_ref):
    for row in range(total_ref.shape[0] - 1):
        at = slice(row * tile, (row + 1) * tile)
        total_ref[row] = base_ref[:, at] - counts_ref[:, at].astype(jnp.float32)
    total_ref[total_ref.shape[0] - 1] = jnp.zeros(total_ref.shape[1:], jnp.float32)


def start_total(counts, base_rate, dims):
    _, brows, _, tile = dims
    return pl.pallas_call(
        functools.partial(start_kernel, tile),
        in_specs=[VMEM, VMEM],
        out_specs=VMEM,
        out_shape=jax.ShapeDtypeStruct((brows + 1, counts.shape[0], tile), jnp.float32),
        compiler_params=PARAMS,
        name="base_less_counts",
    )(counts, base_rate)


def step_kernel(dims, n, call, groups, plan_ref, *refs):
    basis, brows, slots, tile = dims
    lag_ref, power_ref, excite_ref = refs[len(groups) : len(groups) + 3]
    total_in, states_ref, total_ref, built_ref, held, weights, sems = refs[-7:]
    bins = lag_ref.shape[1]
    half = held.shape[0] // len(groups)
    each = carry_rows(half, basis)
    most = (plan_ref.shape[0] - 1 - brows) // (n // 2 + 1) - 1
    built_ref[...] = jnp.zeros_like(built_ref)
    pairs = (plan_ref[call * (most + 1)] + 1) // 2

    def entry_at(place):
        code = plan_ref[call * (most + 1) + 1 + place]
        return code >> 16, (code >> 8) & 255, code & 255

    def weight_at(place):
        row, slot, _ = entry_at(place)
        return pltpu.make_async_copy(
            excite_ref.at[:, jnp.minimum(row, brows - 1), slot],
            weights.at[place],
            sems.at[0, place],
        )

    def copy_at(place):
        row, slot, block = entry_at(place)
        return pltpu.make_async_copy(
            held.at[block], states_ref.at[row * slots + slot], sems.at[1, place]
        )

    @pl.loop(0, 2 * pairs)
    def _(place):
        weight_at(place).start()

    total_ref[...] = total_in[...]
    for d, (carried_by, second) in enumerate(groups):
        impact_ref, carry_ref = refs[d], refs[carried_by]
        first = half * bins + second * each
        carry = carry_ref[first : first + each].astype(jnp.float32)
        for q in range(0, half, 2):
            both = jnp.concatenate(
                [impact_ref[(q + i) * bins : (q + i + 1) * bins] for i in range(2)], axis=1
            )
            for b in range(basis):
                state = jnp.dot(lag_ref[b], both, preferred_element_type=jnp.float32)
                for i in range(2):
                    row = (q + i) * basis + b
                    held[d * half + q + i, :, b * tile : (b + 1) * tile] = (
                        state[:, i * tile : (i + 1) * tile] + power_ref[b] * carry[row : row + 1]
                    ).astype(jnp.bfloat16)

    @pl.loop(0, pairs)
    def _(k):
        terms = []
        for i in range(2):
            row, _, block = entry_at(2 * k + i)
            copy_at(2 * k + i).start()
            weight_at(2 * k + i).wait()
            weight = jnp.concatenate([weights[2 * k + i, b] for b in range(basis)], axis=1)
            term = lax.dot_general(
                held[block], weight, (((1,), (1,)), ((), ())), preferred_element_type=jnp.float32
            )
            terms.append((row, term))
        for row, term in terms:
            total_ref[row] += term

    @pl.loop(0, 2 * pairs)
    def _(place):
        copy_at(place).wait()


def take_step(call, groups, plan, arrived, lag, power, excite, states, total, dims, n):
    basis, brows, slots, tile = dims
    bins = lag.shape[1]
    half = arrived[0].shape[0] // bins
    most = (plan.shape[0] - 1 - brows) // (n // 2 + 1) - 1
    given = [total] if states is None else [states, total]
    return pl.pallas_call(
        functools.partial(step_kernel, dims, n, call, groups),
        in_specs=[SMEM] + [VMEM] * (len(groups) + 2) + [ANYWHERE] * len(given) + [VMEM],
        out_specs=[ANYWHERE, VMEM, VMEM],
        out_shape=[
            jax.ShapeDtypeStruct((brows * slots + 1, bins, basis * tile), jnp.bfloat16),
            jax.ShapeDtypeStruct(total.shape, total.dtype),
            jax.ShapeDtypeStruct((8, tile), jnp.float32),
        ],
        scratch_shapes=[
            pltpu.VMEM((len(groups) * half, bins, basis * tile), jnp.bfloat16),
            pltpu.VMEM((most, basis, tile, tile), jnp.bfloat16),
            pltpu.SemaphoreType.DMA((2, most)),
        ],
        input_output_aliases={} if states is None else {len(groups) + 4: 0},
        compiler_params=PARAMS,
        cost_estimate=pl.CostEstimate(
            flops=8 * basis * bins * bins * tile * 4,
            bytes_accessed=4 * 1024 * 1024,
            transcendentals=0,
        ),
        name="ring_step",
    )(plan, *arrived, lag, power, excite, *given)


def products(turned_ref, states_ref, plan_ref, group, dims, sent_ref, kept_ref):
    basis, brows, slots, tile = dims
    tail = plan_ref.shape[0] - 1 - brows
    part = tile // 2
    for r, row in enumerate(rows_of(group, dims)):
        fill = plan_ref[tail + 1 + row]
        for s in range(slots):
            grad = jnp.dot(
                turned_ref[row], states_ref[row * slots + s], preferred_element_type=jnp.float32
            )
            grad = jnp.where(s < fill, grad, jnp.zeros_like(grad))
            for b in range(basis):
                at = slice(b * tile, (b + 1) * tile)
                kept_ref[b, r, s] = grad[:part, at]
                sent_ref[b, r, s] = grad[part:, at].astype(sent_ref.dtype)


def rows_of(group, dims):
    count = dims[1] // GROUPS
    return range(group * count, (group + 1) * count)


def weighted_kernel(dims, overall, plan_ref, total_ref, states_ref, sent_ref, kept_ref, *refs):
    _, brows, _, tile = dims
    turned_ref, rate_sent_ref, rate_kept_ref = refs
    half = plan_ref[plan_ref.shape[0] - 1 - brows]
    part = tile // 2
    rates = []
    for row in range(brows):
        weighted = (2.0 / overall) * total_ref[row]
        rates.append(jnp.sum(weighted, axis=0, keepdims=True))
        weighted = weighted.T.astype(jnp.bfloat16)
        upper, lower = weighted[:part], weighted[part:]
        turned_ref[row, :part] = jnp.where(half == 0, upper, lower)
        turned_ref[row, part:] = jnp.where(half == 0, lower, upper)
    first_half = jnp.concatenate(rates[: brows // 2], axis=0)
    second_half = jnp.concatenate(rates[brows // 2 :], axis=0)
    rate_kept_ref[...] = jnp.where(half == 0, first_half, second_half)
    rate_sent_ref[...] = jnp.where(half == 0, second_half, first_half)
    products(turned_ref, states_ref, plan_ref, 0, dims, sent_ref, kept_ref)


def later_kernel(dims, group, plan_ref, turned_ref, states_ref, sent_ref, kept_ref):
    products(turned_ref, states_ref, plan_ref, group, dims, sent_ref, kept_ref)


def group_shape(dims, dtype):
    basis, brows, slots, tile = dims
    return jax.ShapeDtypeStruct((basis, brows // GROUPS, slots, tile // 2, tile), dtype)


def first_products(plan, total, states, dims, overall):
    _, brows, _, tile = dims
    turned = jax.ShapeDtypeStruct((brows, tile, total.shape[1]), jnp.bfloat16)
    rate = jax.ShapeDtypeStruct((brows // 2, tile), jnp.float32)
    return pl.pallas_call(
        functools.partial(weighted_kernel, dims, overall),
        in_specs=[SMEM, VMEM, VMEM],
        out_specs=[VMEM] * 5,
        out_shape=[
            group_shape(dims, jnp.bfloat16),
            group_shape(dims, jnp.float32),
            turned,
            rate,
            rate,
        ],
        compiler_params=PARAMS,
        name="weighted_products",
    )(plan, total, states)


def later_products(group, plan, turned, states, dims):
    return pl.pallas_call(
        functools.partial(later_kernel, dims, group),
        in_specs=[SMEM, VMEM, VMEM],
        out_specs=[VMEM, VMEM],
        out_shape=[group_shape(dims, jnp.bfloat16), group_shape(dims, jnp.float32)],
        compiler_params=PARAMS,
        name="products",
    )(plan, turned, states)


def add_kernel(dims, group, kept_ref, got_ref, *refs):
    basis, brows, _, _ = dims
    out_ref, held, sems = refs[-3:]
    if group == GROUPS - 1:
        rate_ref, rate_got_ref, rate_out_ref = refs[0], refs[1], refs[-4]
        out_ref, rate_out_ref = rate_out_ref, out_ref
        rate_out_ref[...] = rate_ref[...] + rate_got_ref[...]
    copies = []
    for r, row in enumerate(rows_of(group, dims)):
        for b in range(basis):
            held[b, r] = (kept_ref[b, r] + got_ref[b, r].astype(jnp.float32)).astype(jnp.bfloat16)
            copies.append(
                pltpu.make_async_copy(held.at[b, r], out_ref.at[b, row], sems.at[b, r])
            )
            copies[-1].start()
    for copy in copies:
        copy.wait()


def add_received(group, kept, got, rates, grad, dims):
    basis, brows, slots, tile = dims
    whole = jax.ShapeDtypeStruct((basis, brows, slots, tile // 2, tile), jnp.bfloat16)
    given = [] if grad is None else [grad]
    last = group == GROUPS - 1
    return pl.pallas_call(
        functools.partial(add_kernel, dims, group),
        in_specs=[VMEM] * (2 + len(rates)) + [ANYWHERE] * len(given),
        out_specs=[ANYWHERE, VMEM] if last else [ANYWHERE],
        out_shape=[whole] + ([jax.ShapeDtypeStruct(rates[0].shape, jnp.float32)] if last else []),
        scratch_shapes=[
            pltpu.VMEM(group_shape(dims, jnp.bfloat16).shape, jnp.bfloat16),
            pltpu.SemaphoreType.DMA((basis, brows // GROUPS)),
        ],
        input_output_aliases={2 + len(rates): 0} if given else {},
        compiler_params=PARAMS,
        name="add_received",
    )(kept, got, *rates, *given)


def shards(counts, mark_value, base_rate, excite, block_col, row_fill):
    dims = excite.shape[:4]
    basis, _, _, tile = dims
    bins = counts.shape[0]
    overall = bins * lax.axis_size("tm")
    n = lax.axis_size("types")
    order = list(range(0, n, 2)) + list(range(1, n, 2))[::-1]
    up = [(order[i], order[(i + 1) % n]) for i in range(n)]
    down = [(b, a) for a, b in up]
    swap = [(0, 1), (1, 0)]

    one, two, ends = impact_messages(counts, mark_value, dims, overall)
    enter = lax.ppermute(ends, "tm", [(0, 1)])
    two = add_carry(enter, two, basis, bins)
    lag, power = lag_tables(bins, basis, overall, tile)

    states = None
    built = []

    def after(value, message):
        return lax.optimization_barrier((value, message))[0]

    def step(groups, arrived):
        nonlocal states, total
        states, total, done = take_step(
            len(built), groups, plan, arrived, lag, power, excite, states, total, dims, n
        )
        built.append(done)

    def send(message, way, hop):
        if hop > 2:
            message = after(message, built[hop - 2])
        return lax.ppermute(message, "types", way)

    two_groups = ((1, 0), (1, 1))
    hops = n // 2
    at_up, at_down = [one, two], [one, two]
    for hop in range(1, hops + 1):
        if hop < hops:
            next_up, next_down = [None, None], [None, None]
            for second in range(2):
                next_up[second] = send(at_up[second], up, hop)
                next_down[second] = send(at_down[second], down, hop)
        else:
            next_up = [send(at_up[0], up, hop), None]
            next_down = [None, send(at_down[1], down, hop)]
        if hop == 1:
            cols = after(block_col, next_up[0])
            plan = make_plan(cols, row_fill, dims, counts.shape[1] // tile, n)
            total = start_total(counts, base_rate.reshape(1, -1), dims)
            total = after(total, next_up[1])
            step(two_groups, [one, two])
        else:
            step(((1, 0), (1, 1), (3, 0), (3, 1)), [*at_up, *at_down])
        at_up, at_down = next_up, next_down
    step(two_groups, [at_up[0], at_down[1]])

    out, kept, turned, rate_sent, rate_kept = first_products(plan, total, states, dims, overall)
    kept = [kept]
    got = [lax.ppermute(out, "tm", swap)]
    rate_got = lax.ppermute(rate_sent, "tm", swap)
    for group in range(1, GROUPS):
        out, more = later_products(group, plan, turned, states, dims)
        kept.append(more)
        got.append(lax.ppermute(out, "tm", swap))
    grad = None
    for group in range(GROUPS):
        rates = [rate_kept, rate_got] if group == GROUPS - 1 else []
        grad, *rate = add_received(group, kept[group], got[group], rates, grad, dims)
    return grad, rate[0].reshape(-1)


def solution(mesh):
    return jax.shard_map(
        shards,
        mesh=mesh,
        in_specs=(
            P(("parts", "tm"), "types"),
            P(("parts", "tm"), "types"),
            P("types"),
            P(None, "types", None, None, None),
            P(),
            P(),
        ),
        out_specs=(P("parts", "types", None, "tm", None), P(("parts", "types", "tm"))),
        check_vma=False,
    )
```

```python
import functools
import jax
import jax.numpy as jnp
from jax import lax
from jax.experimental import pallas as pl
from jax.experimental.pallas import tpu as pltpu
from jax.sharding import PartitionSpec as P

GROUPS = 2
SMEM = pl.BlockSpec(memory_space=pltpu.SMEM)
VMEM = pl.BlockSpec(memory_space=pltpu.VMEM)
ANYWHERE = pl.BlockSpec(memory_space=pl.ANY)
PARAMS = pltpu.CompilerParams(vmem_limit_bytes=16 << 20)


def lag_tables(bins, basis_count, overall, lanes):
    log_decay = -(8.0 ** jnp.arange(basis_count, dtype=jnp.float32)) / (2.0 * overall)
    t = jnp.arange(bins, dtype=jnp.float32)
    lag = t[:, None] - 1.0 - t[None, :]
    weights = jnp.where(
        lag[None] >= 0.0,
        (1.0 - jnp.exp(log_decay))[:, None, None]
        * jnp.exp(jnp.maximum(lag, 0.0)[None] * log_decay[:, None, None]),
        jnp.float32(0.0),
    )
    power = jnp.exp(t[None, :, None] * log_decay[:, None, None])
    return weights.astype(jnp.bfloat16), jnp.broadcast_to(power, (basis_count, bins, lanes))


def load_lanes(first, count, parts, counts_hbm, mark_hbm, counts, mark, sems):
    lanes = count // parts
    copies = []
    for j in range(parts):
        at = pl.ds(first + j * lanes, lanes)
        to = pl.ds(j * lanes, lanes)
        copies.append(
            (
                pltpu.make_async_copy(counts_hbm.at[:, at], counts.at[:, to], sems.at[0, j]),
                pltpu.make_async_copy(mark_hbm.at[:, at], mark.at[:, to], sems.at[1, j]),
            )
        )
        for copy in copies[-1]:
            copy.start()
    return copies


def impact_of(counts, mark, at):
    impact = counts[:, at].astype(jnp.float32) * mark[:, at].astype(jnp.float32)
    return impact.astype(jnp.bfloat16)


def first_kernel(counts_hbm, mark_hbm, out_ref, counts, mark, sems):
    bins, lanes = counts.shape
    tile = out_ref.shape[1]
    parts = sems.shape[1]
    copies = load_lanes(0, lanes, parts, counts_hbm, mark_hbm, counts, mark, sems)
    for j in range(parts):
        for copy in copies[j]:
            copy.wait()
        for q in range(j * lanes // parts // tile, (j + 1) * lanes // parts // tile):
            at = slice(q * tile, (q + 1) * tile)
            out_ref[q * bins : (q + 1) * bins] = impact_of(counts, mark, at)


def second_kernel(
    basis, tile, overall, counts_hbm, mark_hbm, out_ref, ends_ref, counts, mark, sems
):
    bins, types = counts.shape
    parts = sems.shape[1]
    lanes = types // parts
    copies = load_lanes(0, types, parts, counts_hbm, mark_hbm, counts, mark, sems)
    back = (bins - 1 - lax.broadcasted_iota(jnp.int32, (bins, tile), 0)).astype(jnp.float32)
    gains = []
    for b in range(basis):
        rate = (8.0**b) / (2.0 * overall)
        gains.append((1.0 - jnp.exp(jnp.full((bins, tile), -rate, jnp.float32))) * jnp.exp(-rate * back))
    half = types // tile // 2
    for j in range(parts):
        for copy in copies[j]:
            copy.wait()
        for block in range(j * lanes // tile, (j + 1) * lanes // tile):
            at = slice(block * tile, (block + 1) * tile)
            impact = impact_of(counts, mark, at)
            if block >= half:
                out_ref[(block - half) * bins : (block - half + 1) * bins] = impact
            impact = impact.astype(jnp.float32)
            for b in range(basis):
                ends_ref[b : b + 1, at] = jnp.sum(impact * gains[b], axis=0, keepdims=True)
    rest = out_ref.shape[0] - half * bins
    out_ref[half * bins :] = jnp.zeros((rest, tile), jnp.bfloat16)


def carry_rows(half, basis):
    return -(-half * basis // 16) * 16


def impact_messages(counts, mark, dims, overall):
    basis, _, _, tile = dims
    bins, types = counts.shape
    half = types // tile // 2
    params = pltpu.CompilerParams(vmem_limit_bytes=56 << 20)
    one = pl.pallas_call(
        first_kernel,
        in_specs=[ANYWHERE, ANYWHERE],
        out_specs=VMEM,
        out_shape=jax.ShapeDtypeStruct((half * bins, tile), jnp.bfloat16),
        scratch_shapes=[
            pltpu.VMEM((bins, types // 2), jnp.int32),
            pltpu.VMEM((bins, types // 2), jnp.bfloat16),
            pltpu.SemaphoreType.DMA((2, 2)),
        ],
        compiler_params=params,
        name="first_message",
    )(counts, mark)
    two, ends = pl.pallas_call(
        functools.partial(second_kernel, basis, tile, overall),
        in_specs=[ANYWHERE, ANYWHERE],
        out_specs=[VMEM, VMEM],
        out_shape=[
            jax.ShapeDtypeStruct((half * bins + 2 * carry_rows(half, basis), tile), jnp.bfloat16),
            jax.ShapeDtypeStruct((basis, types), jnp.float32),
        ],
        scratch_shapes=[
            pltpu.VMEM((bins, types), jnp.int32),
            pltpu.VMEM((bins, types), jnp.bfloat16),
            pltpu.SemaphoreType.DMA((2, 2)),
        ],
        compiler_params=params,
        name="second_message",
    )(counts, mark)
    return one, two, ends


def carry_kernel(basis, bins, enter_ref, _, out_ref, held, sem):
    rows, tile = out_ref.shape
    half = enter_ref.shape[1] // tile // 2
    each = carry_rows(half, basis)
    carry = []
    for d in range(2):
        for q in range(half):
            carry.append(enter_ref[:, (d * half + q) * tile : (d * half + q + 1) * tile])
        if each > half * basis:
            carry.append(jnp.zeros((each - half * basis, tile), jnp.float32))
    held[...] = jnp.concatenate(carry, axis=0).astype(jnp.bfloat16)
    copy = pltpu.make_async_copy(held, out_ref.at[pl.ds(half * bins, 2 * each)], sem)
    copy.start()
    copy.wait()


def add_carry(enter, two, basis, bins):
    rows, tile = two.shape
    return pl.pallas_call(
        functools.partial(carry_kernel, basis, bins),
        in_specs=[VMEM, ANYWHERE],
        out_specs=ANYWHERE,
        out_shape=jax.ShapeDtypeStruct(two.shape, two.dtype),
        scratch_shapes=[
            pltpu.VMEM((rows % bins, tile), jnp.bfloat16),
            pltpu.SemaphoreType.DMA,
        ],
        input_output_aliases={1: 0},
        compiler_params=PARAMS,
        name="carry_rows",
    )(enter, two)


def ring_place(index, n):
    return jnp.where((index & 1) == 0, index >> 1, n - 1 - (index >> 1))


def code_of(row, slot, block):
    return (row * 256 + slot) * 256 + block


def plan_kernel(shape, col_ref, fill_ref, plan_ref):
    brows, slots, width, n, most = shape
    own = lax.axis_index("types")
    calls = n // 2 + 1
    tail = calls * (most + 1)
    plan_ref[tail] = lax.axis_index("tm")
    for step in range(calls):
        plan_ref[step * (most + 1)] = 0

    @pl.loop(0, brows)
    def _(row):
        fill = fill_ref[own * brows + row]
        plan_ref[tail + 1 + row] = fill

        @pl.loop(0, fill)
        def _(slot):
            column = col_ref[own * brows + row, slot]
            shift = width.bit_length() - 1
            even = width == 1 << shift
            source = column >> shift if even else lax.div(column, width)
            block = column & (width - 1) if even else lax.rem(column, width)
            ahead = ring_place(source, n) - ring_place(own, n)
            ahead = jnp.where(ahead < 0, ahead + n, ahead)
            call = jnp.minimum(ahead, n - ahead)
            down = (ahead > 0) & (ahead < n // 2)
            base = call * (most + 1)
            count = plan_ref[base] + 1
            plan_ref[base] = count
            plan_ref[base + count] = code_of(row, slot, jnp.where(down, width + block, block))

    for step in range(calls):
        base = step * (most + 1)
        count = plan_ref[base]

        @pl.when(lax.rem(count, 2) == 1)
        def _(base=base, count=count):
            plan_ref[base + count + 1] = code_of(brows, 0, 0)


def make_plan(cols, fill, dims, width, n):
    _, brows, slots, _ = dims
    most = 2 * max(2, brows * slots // n)
    return pl.pallas_call(
        functools.partial(plan_kernel, (brows, slots, width, n, most)),
        in_specs=[SMEM] * 2,
        out_specs=SMEM,
        out_shape=jax.ShapeDtypeStruct(((n // 2 + 1) * (most + 1) + 1 + brows,), jnp.int32),
        compiler_params=PARAMS,
        name="plan",
    )(cols, fill)


def start_kernel(tile, counts_ref, base_ref, total_ref):
    for row in range(total_ref.shape[0] - 1):
        at = slice(row * tile, (row + 1) * tile)
        total_ref[row] = base_ref[:, at] - counts_ref[:, at].astype(jnp.float32)
    total_ref[total_ref.shape[0] - 1] = jnp.zeros(total_ref.shape[1:], jnp.float32)


def start_total(counts, base_rate, dims):
    _, brows, _, tile = dims
    return pl.pallas_call(
        functools.partial(start_kernel, tile),
        in_specs=[VMEM, VMEM],
        out_specs=VMEM,
        out_shape=jax.ShapeDtypeStruct((brows + 1, counts.shape[0], tile), jnp.float32),
        compiler_params=PARAMS,
        name="base_less_counts",
    )(counts, base_rate)


def step_kernel(dims, n, call, groups, plan_ref, *refs):
    basis, brows, slots, tile = dims
    lag_ref, power_ref, excite_ref = refs[len(groups) : len(groups) + 3]
    total_in, states_ref, total_ref, built_ref, held, weights, sems = refs[-7:]
    bins = lag_ref.shape[1]
    half = held.shape[0] // len(groups)
    each = carry_rows(half, basis)
    most = (plan_ref.shape[0] - 1 - brows) // (n // 2 + 1) - 1
    built_ref[...] = jnp.zeros_like(built_ref)
    pairs = (plan_ref[call * (most + 1)] + 1) // 2

    def entry_at(place):
        code = plan_ref[call * (most + 1) + 1 + place]
        return code >> 16, (code >> 8) & 255, code & 255

    def weight_at(place):
        row, slot, _ = entry_at(place)
        return pltpu.make_async_copy(
            excite_ref.at[:, jnp.minimum(row, brows - 1), slot],
            weights.at[place],
            sems.at[0, place],
        )

    def copy_at(place):
        row, slot, block = entry_at(place)
        return pltpu.make_async_copy(
            held.at[block], states_ref.at[row * slots + slot], sems.at[1, place]
        )

    @pl.loop(0, 2 * pairs)
    def _(place):
        weight_at(place).start()

    total_ref[...] = total_in[...]
    for d, (carried_by, second) in enumerate(groups):
        impact_ref, carry_ref = refs[d], refs[carried_by]
        first = half * bins + second * each
        carry = carry_ref[first : first + each].astype(jnp.float32)
        for q in range(0, half, 2):
            both = jnp.concatenate(
                [impact_ref[(q + i) * bins : (q + i + 1) * bins] for i in range(2)], axis=1
            )
            for b in range(basis):
                state = jnp.dot(lag_ref[b], both, preferred_element_type=jnp.float32)
                for i in range(2):
                    row = (q + i) * basis + b
                    held[d * half + q + i, :, b * tile : (b + 1) * tile] = (
                        state[:, i * tile : (i + 1) * tile] + power_ref[b] * carry[row : row + 1]
                    ).astype(jnp.bfloat16)

    @pl.loop(0, pairs)
    def _(k):
        terms = []
        for i in range(2):
            row, _, block = entry_at(2 * k + i)
            copy_at(2 * k + i).start()
            weight_at(2 * k + i).wait()
            weight = jnp.concatenate([weights[2 * k + i, b] for b in range(basis)], axis=1)
            term = lax.dot_general(
                held[block], weight, (((1,), (1,)), ((), ())), preferred_element_type=jnp.float32
            )
            terms.append((row, term))
        for row, term in terms:
            total_ref[row] += term

    @pl.loop(0, 2 * pairs)
    def _(place):
        copy_at(place).wait()


def take_step(call, groups, plan, arrived, lag, power, excite, states, total, dims, n):
    basis, brows, slots, tile = dims
    bins = lag.shape[1]
    half = arrived[0].shape[0] // bins
    most = (plan.shape[0] - 1 - brows) // (n // 2 + 1) - 1
    given = [total] if states is None else [states, total]
    return pl.pallas_call(
        functools.partial(step_kernel, dims, n, call, groups),
        in_specs=[SMEM] + [VMEM] * (len(groups) + 2) + [ANYWHERE] * len(given) + [VMEM],
        out_specs=[ANYWHERE, VMEM, VMEM],
        out_shape=[
            jax.ShapeDtypeStruct((brows * slots + 1, bins, basis * tile), jnp.bfloat16),
            jax.ShapeDtypeStruct(total.shape, total.dtype),
            jax.ShapeDtypeStruct((8, tile), jnp.float32),
        ],
        scratch_shapes=[
            pltpu.VMEM((len(groups) * half, bins, basis * tile), jnp.bfloat16),
            pltpu.VMEM((most, basis, tile, tile), jnp.bfloat16),
            pltpu.SemaphoreType.DMA((2, most)),
        ],
        input_output_aliases={} if states is None else {len(groups) + 4: 0},
        compiler_params=PARAMS,
        cost_estimate=pl.CostEstimate(
            flops=8 * basis * bins * bins * tile * 4,
            bytes_accessed=4 * 1024 * 1024,
            transcendentals=0,
        ),
        name="ring_step",
    )(plan, *arrived, lag, power, excite, *given)


def products(turned_ref, states_ref, plan_ref, group, dims, sent_ref, kept_ref):
    basis, brows, slots, tile = dims
    tail = plan_ref.shape[0] - 1 - brows
    part = tile // 2
    for r, row in enumerate(rows_of(group, dims)):
        fill = plan_ref[tail + 1 + row]
        for s in range(slots):
            grad = jnp.dot(
                turned_ref[row], states_ref[row * slots + s], preferred_element_type=jnp.float32
            )
            grad = jnp.where(s < fill, grad, jnp.zeros_like(grad))
            for b in range(basis):
                at = slice(b * tile, (b + 1) * tile)
                kept_ref[b, r, s] = grad[:part, at]
                sent_ref[b, r, s] = grad[part:, at].astype(sent_ref.dtype)


def rows_of(group, dims):
    count = dims[1] // GROUPS
    return range(group * count, (group + 1) * count)


def weighted_kernel(dims, overall, plan_ref, total_ref, states_ref, sent_ref, kept_ref, *refs):
    _, brows, _, tile = dims
    turned_ref, rate_sent_ref, rate_kept_ref = refs
    half = plan_ref[plan_ref.shape[0] - 1 - brows]
    part = tile // 2
    rates = []
    for row in range(brows):
        weighted = (2.0 / overall) * total_ref[row]
        rates.append(jnp.sum(weighted, axis=0, keepdims=True))
        weighted = weighted.T.astype(jnp.bfloat16)
        upper, lower = weighted[:part], weighted[part:]
        turned_ref[row, :part] = jnp.where(half == 0, upper, lower)
        turned_ref[row, part:] = jnp.where(half == 0, lower, upper)
    first_half = jnp.concatenate(rates[: brows // 2], axis=0)
    second_half = jnp.concatenate(rates[brows // 2 :], axis=0)
    rate_kept_ref[...] = jnp.where(half == 0, first_half, second_half)
    rate_sent_ref[...] = jnp.where(half == 0, second_half, first_half)
    products(turned_ref, states_ref, plan_ref, 0, dims, sent_ref, kept_ref)


def later_kernel(dims, group, plan_ref, turned_ref, states_ref, sent_ref, kept_ref):
    products(turned_ref, states_ref, plan_ref, group, dims, sent_ref, kept_ref)


def group_shape(dims, dtype):
    basis, brows, slots, tile = dims
    return jax.ShapeDtypeStruct((basis, brows // GROUPS, slots, tile // 2, tile), dtype)


def first_products(plan, total, states, dims, overall):
    _, brows, _, tile = dims
    turned = jax.ShapeDtypeStruct((brows, tile, total.shape[1]), jnp.bfloat16)
    rate = jax.ShapeDtypeStruct((brows // 2, tile), jnp.float32)
    return pl.pallas_call(
        functools.partial(weighted_kernel, dims, overall),
        in_specs=[SMEM, VMEM, VMEM],
        out_specs=[VMEM] * 5,
        out_shape=[
            group_shape(dims, jnp.bfloat16),
            group_shape(dims, jnp.float32),
            turned,
            rate,
            rate,
        ],
        compiler_params=PARAMS,
        name="weighted_products",
    )(plan, total, states)


def later_products(group, plan, turned, states, dims):
    return pl.pallas_call(
        functools.partial(later_kernel, dims, group),
        in_specs=[SMEM, VMEM, VMEM],
        out_specs=[VMEM, VMEM],
        out_shape=[group_shape(dims, jnp.bfloat16), group_shape(dims, jnp.float32)],
        compiler_params=PARAMS,
        name="products",
    )(plan, turned, states)


def add_kernel(dims, group, kept_ref, got_ref, *refs):
    basis, brows, _, _ = dims
    out_ref, held, sems = refs[-3:]
    if group == GROUPS - 1:
        rate_ref, rate_got_ref, rate_out_ref = refs[0], refs[1], refs[-4]
        out_ref, rate_out_ref = rate_out_ref, out_ref
        rate_out_ref[...] = rate_ref[...] + rate_got_ref[...]
    copies = []
    for r, row in enumerate(rows_of(group, dims)):
        for b in range(basis):
            held[b, r] = (kept_ref[b, r] + got_ref[b, r].astype(jnp.float32)).astype(jnp.bfloat16)
            copies.append(
                pltpu.make_async_copy(held.at[b, r], out_ref.at[b, row], sems.at[b, r])
            )
            copies[-1].start()
    for copy in copies:
        copy.wait()


def add_received(group, kept, got, rates, grad, dims):
    basis, brows, slots, tile = dims
    whole = jax.ShapeDtypeStruct((basis, brows, slots, tile // 2, tile), jnp.bfloat16)
    given = [] if grad is None else [grad]
    last = group == GROUPS - 1
    return pl.pallas_call(
        functools.partial(add_kernel, dims, group),
        in_specs=[VMEM] * (2 + len(rates)) + [ANYWHERE] * len(given),
        out_specs=[ANYWHERE, VMEM] if last else [ANYWHERE],
        out_shape=[whole] + ([jax.ShapeDtypeStruct(rates[0].shape, jnp.float32)] if last else []),
        scratch_shapes=[
            pltpu.VMEM(group_shape(dims, jnp.bfloat16).shape, jnp.bfloat16),
            pltpu.SemaphoreType.DMA((basis, brows // GROUPS)),
        ],
        input_output_aliases={2 + len(rates): 0} if given else {},
        compiler_params=PARAMS,
        name="add_received",
    )(kept, got, *rates, *given)


def shards(counts, mark_value, base_rate, excite, block_col, row_fill):
    dims = excite.shape[:4]
    basis, _, _, tile = dims
    bins = counts.shape[0]
    overall = bins * lax.axis_size("tm")
    n = lax.axis_size("types")
    order = list(range(0, n, 2)) + list(range(1, n, 2))[::-1]
    up = [(order[i], order[(i + 1) % n]) for i in range(n)]
    down = [(b, a) for a, b in up]
    swap = [(0, 1), (1, 0)]

    one, two, ends = impact_messages(counts, mark_value, dims, overall)
    enter = lax.ppermute(ends, "tm", [(0, 1)])
    two = add_carry(enter, two, basis, bins)
    lag, power = lag_tables(bins, basis, overall, tile)

    states = None
    built = []

    def after(value, message):
        return lax.optimization_barrier((value, message))[0]

    def step(groups, arrived):
        nonlocal states, total
        states, total, done = take_step(
            len(built), groups, plan, arrived, lag, power, excite, states, total, dims, n
        )
        built.append(done)

    def send(message, way, hop):
        if hop > 2:
            message = after(message, built[hop - 3])
        return lax.ppermute(message, "types", way)

    two_groups = ((1, 0), (1, 1))
    hops = n // 2
    at_up, at_down = [one, two], [one, two]
    for hop in range(1, hops + 1):
        if 1 < hop < hops:
            ready = (at_up[0], at_down[0])
            at_up = [at_up[0], after(at_up[1], ready)]
            at_down = [at_down[0], after(at_down[1], ready)]
        if hop < hops:
            next_up, next_down = [None, None], [None, None]
            for second in range(2):
                next_up[second] = send(at_up[second], up, hop)
                next_down[second] = send(at_down[second], down, hop)
        else:
            next_up = [send(at_up[0], up, hop), None]
            next_down = [None, send(at_down[1], down, hop)]
        if hop == 1:
            cols = after(block_col, next_up[1])
            plan = make_plan(cols, row_fill, dims, counts.shape[1] // tile, n)
            total = start_total(counts, base_rate.reshape(1, -1), dims)
            total = after(total, next_up[1])
            step(two_groups, [one, two])
        else:
            step(((1, 0), (1, 1), (3, 0), (3, 1)), [*at_up, *at_down])
        at_up, at_down = next_up, next_down
    step(two_groups, [at_up[0], at_down[1]])

    out, kept, turned, rate_sent, rate_kept = first_products(plan, total, states, dims, overall)
    kept = [kept]
    got = [lax.ppermute(out, "tm", swap)]
    rate_got = lax.ppermute(rate_sent, "tm", swap)
    for group in range(1, GROUPS):
        out, more = later_products(group, plan, turned, states, dims)
        kept.append(more)
        got.append(lax.ppermute(out, "tm", swap))
    grad = None
    for group in range(GROUPS):
        rates = [rate_kept, rate_got] if group == GROUPS - 1 else []
        grad, *rate = add_received(group, kept[group], got[group], rates, grad, dims)
    return grad, rate[0].reshape(-1)


def solution(mesh):
    return jax.shard_map(
        shards,
        mesh=mesh,
        in_specs=(
            P(("parts", "tm"), "types"),
            P(("parts", "tm"), "types"),
            P("types"),
            P(None, "types", None, None, None),
            P(),
            P(),
        ),
        out_specs=(P("parts", "types", None, "tm", None), P(("parts", "types", "tm"))),
        check_vma=False,
    )
```

```python
import functools
import jax
import jax.numpy as jnp
from jax import lax
from jax.experimental import pallas as pl
from jax.experimental.pallas import tpu as pltpu
from jax.sharding import PartitionSpec as P

GROUPS = 2
SMEM = pl.BlockSpec(memory_space=pltpu.SMEM)
VMEM = pl.BlockSpec(memory_space=pltpu.VMEM)
ANYWHERE = pl.BlockSpec(memory_space=pl.ANY)
PARAMS = pltpu.CompilerParams(vmem_limit_bytes=16 << 20)


def lag_tables(bins, basis_count, overall, lanes):
    log_decay = -(8.0 ** jnp.arange(basis_count, dtype=jnp.float32)) / (2.0 * overall)
    t = jnp.arange(bins, dtype=jnp.float32)
    lag = t[:, None] - 1.0 - t[None, :]
    weights = jnp.where(
        lag[None] >= 0.0,
        (1.0 - jnp.exp(log_decay))[:, None, None]
        * jnp.exp(jnp.maximum(lag, 0.0)[None] * log_decay[:, None, None]),
        jnp.float32(0.0),
    )
    power = jnp.exp(t[None, :, None] * log_decay[:, None, None])
    return weights.astype(jnp.bfloat16), jnp.broadcast_to(power, (basis_count, bins, lanes))


def load_lanes(first, count, parts, counts_hbm, mark_hbm, counts, mark, sems):
    lanes = count // parts
    copies = []
    for j in range(parts):
        at = pl.ds(first + j * lanes, lanes)
        to = pl.ds(j * lanes, lanes)
        copies.append(
            (
                pltpu.make_async_copy(counts_hbm.at[:, at], counts.at[:, to], sems.at[0, j]),
                pltpu.make_async_copy(mark_hbm.at[:, at], mark.at[:, to], sems.at[1, j]),
            )
        )
        for copy in copies[-1]:
            copy.start()
    return copies


def impact_of(counts, mark, at):
    impact = counts[:, at].astype(jnp.float32) * mark[:, at].astype(jnp.float32)
    return impact.astype(jnp.bfloat16)


def first_kernel(counts_hbm, mark_hbm, out_ref, counts, mark, sems):
    bins, lanes = counts.shape
    tile = out_ref.shape[1]
    parts = sems.shape[1]
    copies = load_lanes(0, lanes, parts, counts_hbm, mark_hbm, counts, mark, sems)
    for j in range(parts):
        for copy in copies[j]:
            copy.wait()
        for q in range(j * lanes // parts // tile, (j + 1) * lanes // parts // tile):
            at = slice(q * tile, (q + 1) * tile)
            out_ref[q * bins : (q + 1) * bins] = impact_of(counts, mark, at)


def second_kernel(
    basis, tile, overall, counts_hbm, mark_hbm, out_ref, ends_ref, counts, mark, sems
):
    bins, types = counts.shape
    parts = sems.shape[1]
    lanes = types // parts
    copies = load_lanes(0, types, parts, counts_hbm, mark_hbm, counts, mark, sems)
    back = (bins - 1 - lax.broadcasted_iota(jnp.int32, (bins, tile), 0)).astype(jnp.float32)
    gains = []
    for b in range(basis):
        rate = (8.0**b) / (2.0 * overall)
        gains.append((1.0 - jnp.exp(jnp.full((bins, tile), -rate, jnp.float32))) * jnp.exp(-rate * back))
    half = types // tile // 2
    for j in range(parts):
        for copy in copies[j]:
            copy.wait()
        for block in range(j * lanes // tile, (j + 1) * lanes // tile):
            at = slice(block * tile, (block + 1) * tile)
            impact = impact_of(counts, mark, at)
            if block >= half:
                out_ref[(block - half) * bins : (block - half + 1) * bins] = impact
            impact = impact.astype(jnp.float32)
            for b in range(basis):
                ends_ref[b : b + 1, at] = jnp.sum(impact * gains[b], axis=0, keepdims=True)
    rest = out_ref.shape[0] - half * bins
    out_ref[half * bins :] = jnp.zeros((rest, tile), jnp.bfloat16)


def carry_rows(half, basis):
    return -(-half * basis // 16) * 16


def impact_messages(counts, mark, dims, overall):
    basis, _, _, tile = dims
    bins, types = counts.shape
    half = types // tile // 2
    params = pltpu.CompilerParams(vmem_limit_bytes=56 << 20)
    one = pl.pallas_call(
        first_kernel,
        in_specs=[ANYWHERE, ANYWHERE],
        out_specs=VMEM,
        out_shape=jax.ShapeDtypeStruct((half * bins, tile), jnp.bfloat16),
        scratch_shapes=[
            pltpu.VMEM((bins, types // 2), jnp.int32),
            pltpu.VMEM((bins, types // 2), jnp.bfloat16),
            pltpu.SemaphoreType.DMA((2, 2)),
        ],
        compiler_params=params,
        name="first_message",
    )(counts, mark)
    two, ends = pl.pallas_call(
        functools.partial(second_kernel, basis, tile, overall),
        in_specs=[ANYWHERE, ANYWHERE],
        out_specs=[VMEM, VMEM],
        out_shape=[
            jax.ShapeDtypeStruct((half * bins + 2 * carry_rows(half, basis), tile), jnp.bfloat16),
            jax.ShapeDtypeStruct((basis, types), jnp.float32),
        ],
        scratch_shapes=[
            pltpu.VMEM((bins, types), jnp.int32),
            pltpu.VMEM((bins, types), jnp.bfloat16),
            pltpu.SemaphoreType.DMA((2, 2)),
        ],
        compiler_params=params,
        name="second_message",
    )(counts, mark)
    return one, two, ends


def carry_kernel(basis, bins, enter_ref, _, out_ref, held, sem):
    rows, tile = out_ref.shape
    half = enter_ref.shape[1] // tile // 2
    each = carry_rows(half, basis)
    carry = []
    for d in range(2):
        for q in range(half):
            carry.append(enter_ref[:, (d * half + q) * tile : (d * half + q + 1) * tile])
        if each > half * basis:
            carry.append(jnp.zeros((each - half * basis, tile), jnp.float32))
    held[...] = jnp.concatenate(carry, axis=0).astype(jnp.bfloat16)
    copy = pltpu.make_async_copy(held, out_ref.at[pl.ds(half * bins, 2 * each)], sem)
    copy.start()
    copy.wait()


def add_carry(enter, two, basis, bins):
    rows, tile = two.shape
    return pl.pallas_call(
        functools.partial(carry_kernel, basis, bins),
        in_specs=[VMEM, ANYWHERE],
        out_specs=ANYWHERE,
        out_shape=jax.ShapeDtypeStruct(two.shape, two.dtype),
        scratch_shapes=[
            pltpu.VMEM((rows % bins, tile), jnp.bfloat16),
            pltpu.SemaphoreType.DMA,
        ],
        input_output_aliases={1: 0},
        compiler_params=PARAMS,
        name="carry_rows",
    )(enter, two)


def ring_place(index, n):
    return jnp.where((index & 1) == 0, index >> 1, n - 1 - (index >> 1))


def code_of(row, slot, block):
    return (row * 256 + slot) * 256 + block


def plan_kernel(shape, col_ref, fill_ref, plan_ref):
    brows, slots, width, n, most = shape
    own = lax.axis_index("types")
    calls = n // 2 + 1
    tail = calls * (most + 1)
    plan_ref[tail] = lax.axis_index("tm")
    for step in range(calls):
        plan_ref[step * (most + 1)] = 0

    @pl.loop(0, brows)
    def _(row):
        fill = fill_ref[own * brows + row]
        plan_ref[tail + 1 + row] = fill

        @pl.loop(0, fill)
        def _(slot):
            column = col_ref[own * brows + row, slot]
            shift = width.bit_length() - 1
            even = width == 1 << shift
            source = column >> shift if even else lax.div(column, width)
            block = column & (width - 1) if even else lax.rem(column, width)
            ahead = ring_place(source, n) - ring_place(own, n)
            ahead = jnp.where(ahead < 0, ahead + n, ahead)
            call = jnp.minimum(ahead, n - ahead)
            down = (ahead > 0) & (ahead < n // 2)
            base = call * (most + 1)
            count = plan_ref[base] + 1
            plan_ref[base] = count
            plan_ref[base + count] = code_of(row, slot, jnp.where(down, width + block, block))

    for step in range(calls):
        base = step * (most + 1)
        count = plan_ref[base]

        @pl.when(lax.rem(count, 2) == 1)
        def _(base=base, count=count):
            plan_ref[base + count + 1] = code_of(brows, 0, 0)


def make_plan(cols, fill, dims, width, n):
    _, brows, slots, _ = dims
    most = 2 * max(2, brows * slots // n)
    return pl.pallas_call(
        functools.partial(plan_kernel, (brows, slots, width, n, most)),
        in_specs=[SMEM] * 2,
        out_specs=SMEM,
        out_shape=jax.ShapeDtypeStruct(((n // 2 + 1) * (most + 1) + 1 + brows,), jnp.int32),
        compiler_params=PARAMS,
        name="plan",
    )(cols, fill)


def start_kernel(tile, counts_ref, base_ref, total_ref):
    for row in range(total_ref.shape[0] - 1):
        at = slice(row * tile, (row + 1) * tile)
        total_ref[row] = base_ref[:, at] - counts_ref[:, at].astype(jnp.float32)
    total_ref[total_ref.shape[0] - 1] = jnp.zeros(total_ref.shape[1:], jnp.float32)


def start_total(counts, base_rate, dims):
    _, brows, _, tile = dims
    return pl.pallas_call(
        functools.partial(start_kernel, tile),
        in_specs=[VMEM, VMEM],
        out_specs=VMEM,
        out_shape=jax.ShapeDtypeStruct((brows + 1, counts.shape[0], tile), jnp.float32),
        compiler_params=PARAMS,
        name="base_less_counts",
    )(counts, base_rate)


def step_kernel(dims, n, call, groups, plan_ref, *refs):
    basis, brows, slots, tile = dims
    lag_ref, power_ref, excite_ref = refs[len(groups) : len(groups) + 3]
    total_in, states_ref, total_ref, built_ref, held, weights, sems = refs[-7:]
    bins = lag_ref.shape[1]
    half = held.shape[0] // len(groups)
    each = carry_rows(half, basis)
    most = (plan_ref.shape[0] - 1 - brows) // (n // 2 + 1) - 1
    built_ref[...] = jnp.zeros_like(built_ref)
    pairs = (plan_ref[call * (most + 1)] + 1) // 2

    def entry_at(place):
        code = plan_ref[call * (most + 1) + 1 + place]
        return code >> 16, (code >> 8) & 255, code & 255

    def weight_at(place):
        row, slot, _ = entry_at(place)
        return pltpu.make_async_copy(
            excite_ref.at[:, jnp.minimum(row, brows - 1), slot],
            weights.at[place],
            sems.at[0, place],
        )

    def copy_at(place):
        row, slot, block = entry_at(place)
        return pltpu.make_async_copy(
            held.at[block], states_ref.at[row * slots + slot], sems.at[1, place]
        )

    @pl.loop(0, 2 * pairs)
    def _(place):
        weight_at(place).start()

    total_ref[...] = total_in[...]
    for d, (carried_by, second) in enumerate(groups):
        impact_ref, carry_ref = refs[d], refs[carried_by]
        first = half * bins + second * each
        carry = carry_ref[first : first + each].astype(jnp.float32)
        for q in range(0, half, 2):
            both = jnp.concatenate(
                [impact_ref[(q + i) * bins : (q + i + 1) * bins] for i in range(2)], axis=1
            )
            for b in range(basis):
                state = jnp.dot(lag_ref[b], both, preferred_element_type=jnp.float32)
                for i in range(2):
                    row = (q + i) * basis + b
                    held[d * half + q + i, :, b * tile : (b + 1) * tile] = (
                        state[:, i * tile : (i + 1) * tile] + power_ref[b] * carry[row : row + 1]
                    ).astype(jnp.bfloat16)

    @pl.loop(0, pairs)
    def _(k):
        terms = []
        for i in range(2):
            row, _, block = entry_at(2 * k + i)
            copy_at(2 * k + i).start()
            weight_at(2 * k + i).wait()
            weight = jnp.concatenate([weights[2 * k + i, b] for b in range(basis)], axis=1)
            term = lax.dot_general(
                held[block], weight, (((1,), (1,)), ((), ())), preferred_element_type=jnp.float32
            )
            terms.append((row, term))
        for row, term in terms:
            total_ref[row] += term

    @pl.loop(0, 2 * pairs)
    def _(place):
        copy_at(place).wait()


def take_step(call, groups, plan, arrived, lag, power, excite, states, total, dims, n):
    basis, brows, slots, tile = dims
    bins = lag.shape[1]
    half = arrived[0].shape[0] // bins
    most = (plan.shape[0] - 1 - brows) // (n // 2 + 1) - 1
    given = [total] if states is None else [states, total]
    return pl.pallas_call(
        functools.partial(step_kernel, dims, n, call, groups),
        in_specs=[SMEM] + [VMEM] * (len(groups) + 2) + [ANYWHERE] * len(given) + [VMEM],
        out_specs=[ANYWHERE, VMEM, VMEM],
        out_shape=[
            jax.ShapeDtypeStruct((brows * slots + 1, bins, basis * tile), jnp.bfloat16),
            jax.ShapeDtypeStruct(total.shape, total.dtype),
            jax.ShapeDtypeStruct((8, tile), jnp.float32),
        ],
        scratch_shapes=[
            pltpu.VMEM((len(groups) * half, bins, basis * tile), jnp.bfloat16),
            pltpu.VMEM((most, basis, tile, tile), jnp.bfloat16),
            pltpu.SemaphoreType.DMA((2, most)),
        ],
        input_output_aliases={} if states is None else {len(groups) + 4: 0},
        compiler_params=PARAMS,
        cost_estimate=pl.CostEstimate(
            flops=8 * basis * bins * bins * tile * 4,
            bytes_accessed=4 * 1024 * 1024,
            transcendentals=0,
        ),
        name="ring_step",
    )(plan, *arrived, lag, power, excite, *given)


def products(turned_ref, states_ref, plan_ref, group, dims, sent_ref, kept_ref):
    basis, brows, slots, tile = dims
    tail = plan_ref.shape[0] - 1 - brows
    part = tile // 2
    for r, row in enumerate(rows_of(group, dims)):
        fill = plan_ref[tail + 1 + row]
        for s in range(slots):
            grad = jnp.dot(
                turned_ref[row], states_ref[row * slots + s], preferred_element_type=jnp.float32
            )
            grad = jnp.where(s < fill, grad, jnp.zeros_like(grad))
            for b in range(basis):
                at = slice(b * tile, (b + 1) * tile)
                kept_ref[b, r, s] = grad[:part, at]
                sent_ref[b, r, s] = grad[part:, at].astype(sent_ref.dtype)


def rows_of(group, dims):
    count = dims[1] // GROUPS
    return range(group * count, (group + 1) * count)


def weighted_kernel(dims, overall, plan_ref, total_ref, states_ref, sent_ref, kept_ref, *refs):
    _, brows, _, tile = dims
    turned_ref, rate_sent_ref, rate_kept_ref = refs
    half = plan_ref[plan_ref.shape[0] - 1 - brows]
    part = tile // 2
    rates = []
    for row in range(brows):
        weighted = (2.0 / overall) * total_ref[row]
        rates.append(jnp.sum(weighted, axis=0, keepdims=True))
        weighted = weighted.T.astype(jnp.bfloat16)
        upper, lower = weighted[:part], weighted[part:]
        turned_ref[row, :part] = jnp.where(half == 0, upper, lower)
        turned_ref[row, part:] = jnp.where(half == 0, lower, upper)
    first_half = jnp.concatenate(rates[: brows // 2], axis=0)
    second_half = jnp.concatenate(rates[brows // 2 :], axis=0)
    rate_kept_ref[...] = jnp.where(half == 0, first_half, second_half)
    rate_sent_ref[...] = jnp.where(half == 0, second_half, first_half)
    products(turned_ref, states_ref, plan_ref, 0, dims, sent_ref, kept_ref)


def later_kernel(dims, group, plan_ref, turned_ref, states_ref, sent_ref, kept_ref):
    products(turned_ref, states_ref, plan_ref, group, dims, sent_ref, kept_ref)


def group_shape(dims, dtype):
    basis, brows, slots, tile = dims
    return jax.ShapeDtypeStruct((basis, brows // GROUPS, slots, tile // 2, tile), dtype)


def first_products(plan, total, states, dims, overall):
    _, brows, _, tile = dims
    turned = jax.ShapeDtypeStruct((brows, tile, total.shape[1]), jnp.bfloat16)
    rate = jax.ShapeDtypeStruct((brows // 2, tile), jnp.float32)
    return pl.pallas_call(
        functools.partial(weighted_kernel, dims, overall),
        in_specs=[SMEM, VMEM, VMEM],
        out_specs=[VMEM] * 5,
        out_shape=[
            group_shape(dims, jnp.bfloat16),
            group_shape(dims, jnp.float32),
            turned,
            rate,
            rate,
        ],
        compiler_params=PARAMS,
        name="weighted_products",
    )(plan, total, states)


def later_products(group, plan, turned, states, dims):
    return pl.pallas_call(
        functools.partial(later_kernel, dims, group),
        in_specs=[SMEM, VMEM, VMEM],
        out_specs=[VMEM, VMEM],
        out_shape=[group_shape(dims, jnp.bfloat16), group_shape(dims, jnp.float32)],
        compiler_params=PARAMS,
        name="products",
    )(plan, turned, states)


def add_kernel(dims, group, kept_ref, got_ref, *refs):
    basis, brows, _, _ = dims
    out_ref, held, sems = refs[-3:]
    if group == GROUPS - 1:
        rate_ref, rate_got_ref, rate_out_ref = refs[0], refs[1], refs[-4]
        out_ref, rate_out_ref = rate_out_ref, out_ref
        rate_out_ref[...] = rate_ref[...] + rate_got_ref[...]
    copies = []
    for r, row in enumerate(rows_of(group, dims)):
        for b in range(basis):
            held[b, r] = (kept_ref[b, r] + got_ref[b, r].astype(jnp.float32)).astype(jnp.bfloat16)
            copies.append(
                pltpu.make_async_copy(held.at[b, r], out_ref.at[b, row], sems.at[b, r])
            )
            copies[-1].start()
    for copy in copies:
        copy.wait()


def add_received(group, kept, got, rates, grad, dims):
    basis, brows, slots, tile = dims
    whole = jax.ShapeDtypeStruct((basis, brows, slots, tile // 2, tile), jnp.bfloat16)
    given = [] if grad is None else [grad]
    last = group == GROUPS - 1
    return pl.pallas_call(
        functools.partial(add_kernel, dims, group),
        in_specs=[VMEM] * (2 + len(rates)) + [ANYWHERE] * len(given),
        out_specs=[ANYWHERE, VMEM] if last else [ANYWHERE],
        out_shape=[whole] + ([jax.ShapeDtypeStruct(rates[0].shape, jnp.float32)] if last else []),
        scratch_shapes=[
            pltpu.VMEM(group_shape(dims, jnp.bfloat16).shape, jnp.bfloat16),
            pltpu.SemaphoreType.DMA((basis, brows // GROUPS)),
        ],
        input_output_aliases={2 + len(rates): 0} if given else {},
        compiler_params=PARAMS,
        name="add_received",
    )(kept, got, *rates, *given)


def shards(counts, mark_value, base_rate, excite, block_col, row_fill):
    dims = excite.shape[:4]
    basis, _, _, tile = dims
    bins = counts.shape[0]
    overall = bins * lax.axis_size("tm")
    n = lax.axis_size("types")
    order = list(range(0, n, 2)) + list(range(1, n, 2))[::-1]
    up = [(order[i], order[(i + 1) % n]) for i in range(n)]
    down = [(b, a) for a, b in up]
    swap = [(0, 1), (1, 0)]

    one, two, ends = impact_messages(counts, mark_value, dims, overall)
    enter = lax.ppermute(ends, "tm", [(0, 1)])
    two = add_carry(enter, two, basis, bins)
    lag, power = lag_tables(bins, basis, overall, tile)

    states = None
    built = []

    def after(value, message):
        return lax.optimization_barrier((value, message))[0]

    def step(groups, arrived):
        nonlocal states, total
        states, total, done = take_step(
            len(built), groups, plan, arrived, lag, power, excite, states, total, dims, n
        )
        built.append(done)

    def send(message, way, hop):
        if hop > 2:
            message = after(message, built[hop - 3])
        return lax.ppermute(message, "types", way)

    two_groups = ((1, 0), (1, 1))
    hops = n // 2
    at_up, at_down = [one, two], [one, two]
    for hop in range(1, hops + 1):
        if 1 < hop < hops:
            ready = (at_up[0], at_down[0]) + ((plan,) if hop == 2 else ())
            at_up = [at_up[0], after(at_up[1], ready)]
            at_down = [at_down[0], after(at_down[1], ready)]
        if hop < hops:
            next_up, next_down = [None, None], [None, None]
            for second in range(2):
                next_up[second] = send(at_up[second], up, hop)
                next_down[second] = send(at_down[second], down, hop)
        else:
            next_up = [send(at_up[0], up, hop), None]
            next_down = [None, send(at_down[1], down, hop)]
        if hop == 1:
            cols = after(block_col, (next_up[0], next_down[0]))
            plan = make_plan(cols, row_fill, dims, counts.shape[1] // tile, n)
            total = start_total(counts, base_rate.reshape(1, -1), dims)
            total = after(total, next_up[1])
            step(two_groups, [one, two])
        else:
            step(((1, 0), (1, 1), (3, 0), (3, 1)), [*at_up, *at_down])
        at_up, at_down = next_up, next_down
    step(two_groups, [at_up[0], at_down[1]])

    out, kept, turned, rate_sent, rate_kept = first_products(plan, total, states, dims, overall)
    kept = [kept]
    got = [lax.ppermute(out, "tm", swap)]
    rate_got = lax.ppermute(rate_sent, "tm", swap)
    for group in range(1, GROUPS):
        out, more = later_products(group, plan, turned, states, dims)
        kept.append(more)
        got.append(lax.ppermute(out, "tm", swap))
    grad = None
    for group in range(GROUPS):
        rates = [rate_kept, rate_got] if group == GROUPS - 1 else []
        grad, *rate = add_received(group, kept[group], got[group], rates, grad, dims)
    return grad, rate[0].reshape(-1)


def solution(mesh):
    return jax.shard_map(
        shards,
        mesh=mesh,
        in_specs=(
            P(("parts", "tm"), "types"),
            P(("parts", "tm"), "types"),
            P("types"),
            P(None, "types", None, None, None),
            P(),
            P(),
        ),
        out_specs=(P("parts", "types", None, "tm", None), P(("parts", "types", "tm"))),
        check_vma=False,
    )
```

```python
import functools
import jax
import jax.numpy as jnp
from jax import lax
from jax.experimental import pallas as pl
from jax.experimental.pallas import tpu as pltpu
from jax.sharding import PartitionSpec as P

GROUPS = 2
SMEM = pl.BlockSpec(memory_space=pltpu.SMEM)
VMEM = pl.BlockSpec(memory_space=pltpu.VMEM)
ANYWHERE = pl.BlockSpec(memory_space=pl.ANY)
PARAMS = pltpu.CompilerParams(vmem_limit_bytes=16 << 20)


def lag_tables(bins, basis_count, overall, lanes):
    log_decay = -(8.0 ** jnp.arange(basis_count, dtype=jnp.float32)) / (2.0 * overall)
    t = jnp.arange(bins, dtype=jnp.float32)
    lag = t[:, None] - 1.0 - t[None, :]
    weights = jnp.where(
        lag[None] >= 0.0,
        (1.0 - jnp.exp(log_decay))[:, None, None]
        * jnp.exp(jnp.maximum(lag, 0.0)[None] * log_decay[:, None, None]),
        jnp.float32(0.0),
    )
    power = jnp.exp(t[None, :, None] * log_decay[:, None, None])
    return weights.astype(jnp.bfloat16), jnp.broadcast_to(power, (basis_count, bins, lanes))


def load_lanes(first, count, parts, counts_hbm, mark_hbm, counts, mark, sems):
    lanes = count // parts
    copies = []
    for j in range(parts):
        at = pl.ds(first + j * lanes, lanes)
        to = pl.ds(j * lanes, lanes)
        copies.append(
            (
                pltpu.make_async_copy(counts_hbm.at[:, at], counts.at[:, to], sems.at[0, j]),
                pltpu.make_async_copy(mark_hbm.at[:, at], mark.at[:, to], sems.at[1, j]),
            )
        )
        for copy in copies[-1]:
            copy.start()
    return copies


def impact_of(counts, mark, at):
    impact = counts[:, at].astype(jnp.float32) * mark[:, at].astype(jnp.float32)
    return impact.astype(jnp.bfloat16)


def first_kernel(counts_hbm, mark_hbm, out_ref, counts, mark, sems):
    bins, lanes = counts.shape
    tile = out_ref.shape[1]
    parts = sems.shape[1]
    copies = load_lanes(0, lanes, parts, counts_hbm, mark_hbm, counts, mark, sems)
    for j in range(parts):
        for copy in copies[j]:
            copy.wait()
        for q in range(j * lanes // parts // tile, (j + 1) * lanes // parts // tile):
            at = slice(q * tile, (q + 1) * tile)
            out_ref[q * bins : (q + 1) * bins] = impact_of(counts, mark, at)


def second_kernel(
    basis, tile, overall, counts_hbm, mark_hbm, out_ref, ends_ref, counts, mark, sems
):
    bins, types = counts.shape
    parts = sems.shape[1]
    lanes = types // parts
    copies = load_lanes(0, types, parts, counts_hbm, mark_hbm, counts, mark, sems)
    back = (bins - 1 - lax.broadcasted_iota(jnp.int32, (bins, tile), 0)).astype(jnp.float32)
    gains = []
    for b in range(basis):
        rate = (8.0**b) / (2.0 * overall)
        gains.append((1.0 - jnp.exp(jnp.full((bins, tile), -rate, jnp.float32))) * jnp.exp(-rate * back))
    half = types // tile // 2
    for j in range(parts):
        for copy in copies[j]:
            copy.wait()
        for block in range(j * lanes // tile, (j + 1) * lanes // tile):
            at = slice(block * tile, (block + 1) * tile)
            impact = impact_of(counts, mark, at)
            if block >= half:
                out_ref[(block - half) * bins : (block - half + 1) * bins] = impact
            impact = impact.astype(jnp.float32)
            for b in range(basis):
                ends_ref[b : b + 1, at] = jnp.sum(impact * gains[b], axis=0, keepdims=True)
    rest = out_ref.shape[0] - half * bins
    out_ref[half * bins :] = jnp.zeros((rest, tile), jnp.bfloat16)


def carry_rows(half, basis):
    return -(-half * basis // 16) * 16


def impact_messages(counts, mark, dims, overall):
    basis, _, _, tile = dims
    bins, types = counts.shape
    half = types // tile // 2
    params = pltpu.CompilerParams(vmem_limit_bytes=56 << 20)
    one = pl.pallas_call(
        first_kernel,
        in_specs=[ANYWHERE, ANYWHERE],
        out_specs=VMEM,
        out_shape=jax.ShapeDtypeStruct((half * bins, tile), jnp.bfloat16),
        scratch_shapes=[
            pltpu.VMEM((bins, types // 2), jnp.int32),
            pltpu.VMEM((bins, types // 2), jnp.bfloat16),
            pltpu.SemaphoreType.DMA((2, 2)),
        ],
        compiler_params=params,
        name="first_message",
    )(counts, mark)
    two, ends = pl.pallas_call(
        functools.partial(second_kernel, basis, tile, overall),
        in_specs=[ANYWHERE, ANYWHERE],
        out_specs=[VMEM, VMEM],
        out_shape=[
            jax.ShapeDtypeStruct((half * bins + 2 * carry_rows(half, basis), tile), jnp.bfloat16),
            jax.ShapeDtypeStruct((basis, types), jnp.float32),
        ],
        scratch_shapes=[
            pltpu.VMEM((bins, types), jnp.int32),
            pltpu.VMEM((bins, types), jnp.bfloat16),
            pltpu.SemaphoreType.DMA((2, 2)),
        ],
        compiler_params=params,
        name="second_message",
    )(counts, mark)
    return one, two, ends


def carry_kernel(basis, bins, enter_ref, _, out_ref, held, sem):
    rows, tile = out_ref.shape
    half = enter_ref.shape[1] // tile // 2
    each = carry_rows(half, basis)
    carry = []
    for d in range(2):
        for q in range(half):
            carry.append(enter_ref[:, (d * half + q) * tile : (d * half + q + 1) * tile])
        if each > half * basis:
            carry.append(jnp.zeros((each - half * basis, tile), jnp.float32))
    held[...] = jnp.concatenate(carry, axis=0).astype(jnp.bfloat16)
    copy = pltpu.make_async_copy(held, out_ref.at[pl.ds(half * bins, 2 * each)], sem)
    copy.start()
    copy.wait()


def add_carry(enter, two, basis, bins):
    rows, tile = two.shape
    return pl.pallas_call(
        functools.partial(carry_kernel, basis, bins),
        in_specs=[VMEM, ANYWHERE],
        out_specs=ANYWHERE,
        out_shape=jax.ShapeDtypeStruct(two.shape, two.dtype),
        scratch_shapes=[
            pltpu.VMEM((rows % bins, tile), jnp.bfloat16),
            pltpu.SemaphoreType.DMA,
        ],
        input_output_aliases={1: 0},
        compiler_params=PARAMS,
        name="carry_rows",
    )(enter, two)


def ring_place(index, n):
    return jnp.where((index & 1) == 0, index >> 1, n - 1 - (index >> 1))


def code_of(row, slot, block):
    return (row * 256 + slot) * 256 + block


def plan_kernel(shape, col_ref, fill_ref, plan_ref):
    brows, slots, width, n, most = shape
    own = lax.axis_index("types")
    calls = n // 2 + 1
    tail = calls * (most + 1)
    plan_ref[tail] = lax.axis_index("tm")
    for step in range(calls):
        plan_ref[step * (most + 1)] = 0

    @pl.loop(0, brows)
    def _(row):
        fill = fill_ref[own * brows + row]
        plan_ref[tail + 1 + row] = fill

        @pl.loop(0, fill)
        def _(slot):
            column = col_ref[own * brows + row, slot]
            shift = width.bit_length() - 1
            even = width == 1 << shift
            source = column >> shift if even else lax.div(column, width)
            block = column & (width - 1) if even else lax.rem(column, width)
            ahead = ring_place(source, n) - ring_place(own, n)
            ahead = jnp.where(ahead < 0, ahead + n, ahead)
            call = jnp.minimum(ahead, n - ahead)
            down = (ahead > 0) & (ahead < n // 2)
            base = call * (most + 1)
            count = plan_ref[base] + 1
            plan_ref[base] = count
            plan_ref[base + count] = code_of(row, slot, jnp.where(down, width + block, block))

    for step in range(calls):
        base = step * (most + 1)
        count = plan_ref[base]

        @pl.when(lax.rem(count, 2) == 1)
        def _(base=base, count=count):
            plan_ref[base + count + 1] = code_of(brows, 0, 0)


def make_plan(cols, fill, dims, width, n):
    _, brows, slots, _ = dims
    most = 2 * max(2, brows * slots // n)
    return pl.pallas_call(
        functools.partial(plan_kernel, (brows, slots, width, n, most)),
        in_specs=[SMEM] * 2,
        out_specs=SMEM,
        out_shape=jax.ShapeDtypeStruct(((n // 2 + 1) * (most + 1) + 1 + brows,), jnp.int32),
        compiler_params=PARAMS,
        name="plan",
    )(cols, fill)


def start_kernel(tile, counts_ref, base_ref, total_ref):
    for row in range(total_ref.shape[0] - 1):
        at = slice(row * tile, (row + 1) * tile)
        total_ref[row] = base_ref[:, at] - counts_ref[:, at].astype(jnp.float32)
    total_ref[total_ref.shape[0] - 1] = jnp.zeros(total_ref.shape[1:], jnp.float32)


def start_total(counts, base_rate, dims):
    _, brows, _, tile = dims
    return pl.pallas_call(
        functools.partial(start_kernel, tile),
        in_specs=[VMEM, VMEM],
        out_specs=VMEM,
        out_shape=jax.ShapeDtypeStruct((brows + 1, counts.shape[0], tile), jnp.float32),
        compiler_params=PARAMS,
        name="base_less_counts",
    )(counts, base_rate)


def step_kernel(dims, n, call, groups, plan_ref, *refs):
    basis, brows, slots, tile = dims
    lag_ref, power_ref, excite_ref = refs[len(groups) : len(groups) + 3]
    total_in, states_ref, total_ref, built_ref, held, weights, sems = refs[-7:]
    bins = lag_ref.shape[1]
    half = held.shape[0] // len(groups)
    each = carry_rows(half, basis)
    most = (plan_ref.shape[0] - 1 - brows) // (n // 2 + 1) - 1
    built_ref[...] = jnp.zeros_like(built_ref)
    pairs = (plan_ref[call * (most + 1)] + 1) // 2

    def entry_at(place):
        code = plan_ref[call * (most + 1) + 1 + place]
        return code >> 16, (code >> 8) & 255, code & 255

    def weight_at(place):
        row, slot, _ = entry_at(place)
        return pltpu.make_async_copy(
            excite_ref.at[:, jnp.minimum(row, brows - 1), slot],
            weights.at[place],
            sems.at[0, place],
        )

    def copy_at(place):
        row, slot, block = entry_at(place)
        return pltpu.make_async_copy(
            held.at[block], states_ref.at[row * slots + slot], sems.at[1, place]
        )

    @pl.loop(0, 2 * pairs)
    def _(place):
        weight_at(place).start()

    total_ref[...] = total_in[...]
    for d, (carried_by, second) in enumerate(groups):
        impact_ref, carry_ref = refs[d], refs[carried_by]
        first = half * bins + second * each
        carry = carry_ref[first : first + each].astype(jnp.float32)
        for q in range(0, half, 2):
            both = jnp.concatenate(
                [impact_ref[(q + i) * bins : (q + i + 1) * bins] for i in range(2)], axis=1
            )
            for b in range(basis):
                state = jnp.dot(lag_ref[b], both, preferred_element_type=jnp.float32)
                for i in range(2):
                    row = (q + i) * basis + b
                    held[d * half + q + i, :, b * tile : (b + 1) * tile] = (
                        state[:, i * tile : (i + 1) * tile] + power_ref[b] * carry[row : row + 1]
                    ).astype(jnp.bfloat16)

    @pl.loop(0, 2 * pairs)
    def _(place):
        copy_at(place).start()

    @pl.loop(0, pairs)
    def _(k):
        terms = []
        for i in range(2):
            row, _, block = entry_at(2 * k + i)
            weight_at(2 * k + i).wait()
            weight = jnp.concatenate([weights[2 * k + i, b] for b in range(basis)], axis=1)
            term = lax.dot_general(
                held[block], weight, (((1,), (1,)), ((), ())), preferred_element_type=jnp.float32
            )
            terms.append((row, term))
        for row, term in terms:
            total_ref[row] += term

    @pl.loop(0, 2 * pairs)
    def _(place):
        copy_at(place).wait()


def take_step(call, groups, plan, arrived, lag, power, excite, states, total, dims, n):
    basis, brows, slots, tile = dims
    bins = lag.shape[1]
    half = arrived[0].shape[0] // bins
    most = (plan.shape[0] - 1 - brows) // (n // 2 + 1) - 1
    given = [total] if states is None else [states, total]
    return pl.pallas_call(
        functools.partial(step_kernel, dims, n, call, groups),
        in_specs=[SMEM] + [VMEM] * (len(groups) + 2) + [ANYWHERE] * len(given) + [VMEM],
        out_specs=[ANYWHERE, VMEM, VMEM],
        out_shape=[
            jax.ShapeDtypeStruct((brows * slots + 1, bins, basis * tile), jnp.bfloat16),
            jax.ShapeDtypeStruct(total.shape, total.dtype),
            jax.ShapeDtypeStruct((8, tile), jnp.float32),
        ],
        scratch_shapes=[
            pltpu.VMEM((len(groups) * half, bins, basis * tile), jnp.bfloat16),
            pltpu.VMEM((most, basis, tile, tile), jnp.bfloat16),
            pltpu.SemaphoreType.DMA((2, most)),
        ],
        input_output_aliases={} if states is None else {len(groups) + 4: 0},
        compiler_params=PARAMS,
        cost_estimate=pl.CostEstimate(
            flops=8 * basis * bins * bins * tile * 4,
            bytes_accessed=4 * 1024 * 1024,
            transcendentals=0,
        ),
        name="ring_step",
    )(plan, *arrived, lag, power, excite, *given)


def products(turned_ref, states_ref, plan_ref, group, dims, sent_ref, kept_ref):
    basis, brows, slots, tile = dims
    tail = plan_ref.shape[0] - 1 - brows
    part = tile // 2
    for r, row in enumerate(rows_of(group, dims)):
        fill = plan_ref[tail + 1 + row]
        for s in range(slots):
            grad = jnp.dot(
                turned_ref[row], states_ref[row * slots + s], preferred_element_type=jnp.float32
            )
            grad = jnp.where(s < fill, grad, jnp.zeros_like(grad))
            for b in range(basis):
                at = slice(b * tile, (b + 1) * tile)
                kept_ref[b, r, s] = grad[:part, at]
                sent_ref[b, r, s] = grad[part:, at].astype(sent_ref.dtype)


def rows_of(group, dims):
    count = dims[1] // GROUPS
    return range(group * count, (group + 1) * count)


def weighted_kernel(dims, overall, plan_ref, total_ref, states_ref, sent_ref, kept_ref, *refs):
    _, brows, _, tile = dims
    turned_ref, rate_sent_ref, rate_kept_ref = refs
    half = plan_ref[plan_ref.shape[0] - 1 - brows]
    part = tile // 2
    rates = []
    for row in range(brows):
        weighted = (2.0 / overall) * total_ref[row]
        rates.append(jnp.sum(weighted, axis=0, keepdims=True))
        weighted = weighted.T.astype(jnp.bfloat16)
        upper, lower = weighted[:part], weighted[part:]
        turned_ref[row, :part] = jnp.where(half == 0, upper, lower)
        turned_ref[row, part:] = jnp.where(half == 0, lower, upper)
    first_half = jnp.concatenate(rates[: brows // 2], axis=0)
    second_half = jnp.concatenate(rates[brows // 2 :], axis=0)
    rate_kept_ref[...] = jnp.where(half == 0, first_half, second_half)
    rate_sent_ref[...] = jnp.where(half == 0, second_half, first_half)
    products(turned_ref, states_ref, plan_ref, 0, dims, sent_ref, kept_ref)


def later_kernel(dims, group, plan_ref, turned_ref, states_ref, sent_ref, kept_ref):
    products(turned_ref, states_ref, plan_ref, group, dims, sent_ref, kept_ref)


def group_shape(dims, dtype):
    basis, brows, slots, tile = dims
    return jax.ShapeDtypeStruct((basis, brows // GROUPS, slots, tile // 2, tile), dtype)


def first_products(plan, total, states, dims, overall):
    _, brows, _, tile = dims
    turned = jax.ShapeDtypeStruct((brows, tile, total.shape[1]), jnp.bfloat16)
    rate = jax.ShapeDtypeStruct((brows // 2, tile), jnp.float32)
    return pl.pallas_call(
        functools.partial(weighted_kernel, dims, overall),
        in_specs=[SMEM, VMEM, VMEM],
        out_specs=[VMEM] * 5,
        out_shape=[
            group_shape(dims, jnp.bfloat16),
            group_shape(dims, jnp.float32),
            turned,
            rate,
            rate,
        ],
        compiler_params=PARAMS,
        name="weighted_products",
    )(plan, total, states)


def later_products(group, plan, turned, states, dims):
    return pl.pallas_call(
        functools.partial(later_kernel, dims, group),
        in_specs=[SMEM, VMEM, VMEM],
        out_specs=[VMEM, VMEM],
        out_shape=[group_shape(dims, jnp.bfloat16), group_shape(dims, jnp.float32)],
        compiler_params=PARAMS,
        name="products",
    )(plan, turned, states)


def add_kernel(dims, group, kept_ref, got_ref, *refs):
    basis, brows, _, _ = dims
    out_ref, held, sems = refs[-3:]
    if group == GROUPS - 1:
        rate_ref, rate_got_ref, rate_out_ref = refs[0], refs[1], refs[-4]
        out_ref, rate_out_ref = rate_out_ref, out_ref
        rate_out_ref[...] = rate_ref[...] + rate_got_ref[...]
    copies = []
    for r, row in enumerate(rows_of(group, dims)):
        for b in range(basis):
            held[b, r] = (kept_ref[b, r] + got_ref[b, r].astype(jnp.float32)).astype(jnp.bfloat16)
            copies.append(
                pltpu.make_async_copy(held.at[b, r], out_ref.at[b, row], sems.at[b, r])
            )
            copies[-1].start()
    for copy in copies:
        copy.wait()


def add_received(group, kept, got, rates, grad, dims):
    basis, brows, slots, tile = dims
    whole = jax.ShapeDtypeStruct((basis, brows, slots, tile // 2, tile), jnp.bfloat16)
    given = [] if grad is None else [grad]
    last = group == GROUPS - 1
    return pl.pallas_call(
        functools.partial(add_kernel, dims, group),
        in_specs=[VMEM] * (2 + len(rates)) + [ANYWHERE] * len(given),
        out_specs=[ANYWHERE, VMEM] if last else [ANYWHERE],
        out_shape=[whole] + ([jax.ShapeDtypeStruct(rates[0].shape, jnp.float32)] if last else []),
        scratch_shapes=[
            pltpu.VMEM(group_shape(dims, jnp.bfloat16).shape, jnp.bfloat16),
            pltpu.SemaphoreType.DMA((basis, brows // GROUPS)),
        ],
        input_output_aliases={2 + len(rates): 0} if given else {},
        compiler_params=PARAMS,
        name="add_received",
    )(kept, got, *rates, *given)


def shards(counts, mark_value, base_rate, excite, block_col, row_fill):
    dims = excite.shape[:4]
    basis, _, _, tile = dims
    bins = counts.shape[0]
    overall = bins * lax.axis_size("tm")
    n = lax.axis_size("types")
    order = list(range(0, n, 2)) + list(range(1, n, 2))[::-1]
    up = [(order[i], order[(i + 1) % n]) for i in range(n)]
    down = [(b, a) for a, b in up]
    swap = [(0, 1), (1, 0)]

    one, two, ends = impact_messages(counts, mark_value, dims, overall)
    enter = lax.ppermute(ends, "tm", [(0, 1)])
    two = add_carry(enter, two, basis, bins)
    lag, power = lag_tables(bins, basis, overall, tile)

    states = None
    built = []

    def after(value, message):
        return lax.optimization_barrier((value, message))[0]

    def step(groups, arrived):
        nonlocal states, total
        states, total, done = take_step(
            len(built), groups, plan, arrived, lag, power, excite, states, total, dims, n
        )
        built.append(done)

    def send(message, way, hop):
        if hop > 2:
            message = after(message, built[hop - 3])
        return lax.ppermute(message, "types", way)

    two_groups = ((1, 0), (1, 1))
    hops = n // 2
    at_up, at_down = [one, two], [one, two]
    for hop in range(1, hops + 1):
        if 1 < hop < hops:
            ready = (at_up[0], at_down[0]) + ((plan,) if hop == 2 else ())
            at_up = [at_up[0], after(at_up[1], ready)]
            at_down = [at_down[0], after(at_down[1], ready)]
        if hop < hops:
            next_up, next_down = [None, None], [None, None]
            for second in range(2):
                next_up[second] = send(at_up[second], up, hop)
                next_down[second] = send(at_down[second], down, hop)
        else:
            next_up = [send(at_up[0], up, hop), None]
            next_down = [None, send(at_down[1], down, hop)]
        if hop == 1:
            cols = after(block_col, (next_up[0], next_down[0]))
            plan = make_plan(cols, row_fill, dims, counts.shape[1] // tile, n)
            total = start_total(counts, base_rate.reshape(1, -1), dims)
            total = after(total, next_up[1])
            step(two_groups, [one, two])
        else:
            step(((1, 0), (1, 1), (3, 0), (3, 1)), [*at_up, *at_down])
        at_up, at_down = next_up, next_down
    step(two_groups, [at_up[0], at_down[1]])

    out, kept, turned, rate_sent, rate_kept = first_products(plan, total, states, dims, overall)
    kept = [kept]
    got = [lax.ppermute(out, "tm", swap)]
    rate_got = lax.ppermute(rate_sent, "tm", swap)
    for group in range(1, GROUPS):
        out, more = later_products(group, plan, turned, states, dims)
        kept.append(more)
        got.append(lax.ppermute(out, "tm", swap))
    grad = None
    for group in range(GROUPS):
        rates = [rate_kept, rate_got] if group == GROUPS - 1 else []
        grad, *rate = add_received(group, kept[group], got[group], rates, grad, dims)
    return grad, rate[0].reshape(-1)


def solution(mesh):
    return jax.shard_map(
        shards,
        mesh=mesh,
        in_specs=(
            P(("parts", "tm"), "types"),
            P(("parts", "tm"), "types"),
            P("types"),
            P(None, "types", None, None, None),
            P(),
            P(),
        ),
        out_specs=(P("parts", "types", None, "tm", None), P(("parts", "types", "tm"))),
        check_vma=False,
    )
```

```python
import functools
import jax
import jax.numpy as jnp
from jax import lax
from jax.experimental import pallas as pl
from jax.experimental.pallas import tpu as pltpu
from jax.sharding import PartitionSpec as P

GROUPS = 2
SMEM = pl.BlockSpec(memory_space=pltpu.SMEM)
VMEM = pl.BlockSpec(memory_space=pltpu.VMEM)
ANYWHERE = pl.BlockSpec(memory_space=pl.ANY)
PARAMS = pltpu.CompilerParams(vmem_limit_bytes=16 << 20)


def lag_tables(bins, basis_count, overall, lanes):
    log_decay = -(8.0 ** jnp.arange(basis_count, dtype=jnp.float32)) / (2.0 * overall)
    t = jnp.arange(bins, dtype=jnp.float32)
    lag = t[:, None] - 1.0 - t[None, :]
    weights = jnp.where(
        lag[None] >= 0.0,
        (1.0 - jnp.exp(log_decay))[:, None, None]
        * jnp.exp(jnp.maximum(lag, 0.0)[None] * log_decay[:, None, None]),
        jnp.float32(0.0),
    )
    power = jnp.exp(t[None, :, None] * log_decay[:, None, None])
    return weights.astype(jnp.bfloat16), jnp.broadcast_to(power, (basis_count, bins, lanes))


def load_lanes(first, count, parts, counts_hbm, mark_hbm, counts, mark, sems):
    lanes = count // parts
    copies = []
    for j in range(parts):
        at = pl.ds(first + j * lanes, lanes)
        to = pl.ds(j * lanes, lanes)
        copies.append(
            (
                pltpu.make_async_copy(counts_hbm.at[:, at], counts.at[:, to], sems.at[0, j]),
                pltpu.make_async_copy(mark_hbm.at[:, at], mark.at[:, to], sems.at[1, j]),
            )
        )
        for copy in copies[-1]:
            copy.start()
    return copies


def impact_of(counts, mark, at):
    impact = counts[:, at].astype(jnp.float32) * mark[:, at].astype(jnp.float32)
    return impact.astype(jnp.bfloat16)


def first_kernel(counts_hbm, mark_hbm, out_ref, counts, mark, sems):
    bins, lanes = counts.shape
    tile = out_ref.shape[1]
    parts = sems.shape[1]
    copies = load_lanes(0, lanes, parts, counts_hbm, mark_hbm, counts, mark, sems)
    for j in range(parts):
        for copy in copies[j]:
            copy.wait()
        for q in range(j * lanes // parts // tile, (j + 1) * lanes // parts // tile):
            at = slice(q * tile, (q + 1) * tile)
            out_ref[q * bins : (q + 1) * bins] = impact_of(counts, mark, at)


def second_kernel(
    basis, tile, overall, counts_hbm, mark_hbm, out_ref, ends_ref, counts, mark, sems
):
    bins, types = counts.shape
    parts = sems.shape[1]
    lanes = types // parts
    copies = load_lanes(0, types, parts, counts_hbm, mark_hbm, counts, mark, sems)
    back = (bins - 1 - lax.broadcasted_iota(jnp.int32, (bins, tile), 0)).astype(jnp.float32)
    gains = []
    for b in range(basis):
        rate = (8.0**b) / (2.0 * overall)
        gains.append((1.0 - jnp.exp(jnp.full((bins, tile), -rate, jnp.float32))) * jnp.exp(-rate * back))
    half = types // tile // 2
    for j in range(parts):
        for copy in copies[j]:
            copy.wait()
        for block in range(j * lanes // tile, (j + 1) * lanes // tile):
            at = slice(block * tile, (block + 1) * tile)
            impact = impact_of(counts, mark, at)
            if block >= half:
                out_ref[(block - half) * bins : (block - half + 1) * bins] = impact
            impact = impact.astype(jnp.float32)
            for b in range(basis):
                ends_ref[b : b + 1, at] = jnp.sum(impact * gains[b], axis=0, keepdims=True)
    rest = out_ref.shape[0] - half * bins
    out_ref[half * bins :] = jnp.zeros((rest, tile), jnp.bfloat16)


def carry_rows(half, basis):
    return -(-half * basis // 16) * 16


def impact_messages(counts, mark, dims, overall):
    basis, _, _, tile = dims
    bins, types = counts.shape
    half = types // tile // 2
    params = pltpu.CompilerParams(vmem_limit_bytes=56 << 20)
    one = pl.pallas_call(
        first_kernel,
        in_specs=[ANYWHERE, ANYWHERE],
        out_specs=VMEM,
        out_shape=jax.ShapeDtypeStruct((half * bins, tile), jnp.bfloat16),
        scratch_shapes=[
            pltpu.VMEM((bins, types // 2), jnp.int32),
            pltpu.VMEM((bins, types // 2), jnp.bfloat16),
            pltpu.SemaphoreType.DMA((2, 2)),
        ],
        compiler_params=params,
        name="first_message",
    )(counts, mark)
    two, ends = pl.pallas_call(
        functools.partial(second_kernel, basis, tile, overall),
        in_specs=[ANYWHERE, ANYWHERE],
        out_specs=[VMEM, VMEM],
        out_shape=[
            jax.ShapeDtypeStruct((half * bins + 2 * carry_rows(half, basis), tile), jnp.bfloat16),
            jax.ShapeDtypeStruct((basis, types), jnp.float32),
        ],
        scratch_shapes=[
            pltpu.VMEM((bins, types), jnp.int32),
            pltpu.VMEM((bins, types), jnp.bfloat16),
            pltpu.SemaphoreType.DMA((2, 2)),
        ],
        compiler_params=params,
        name="second_message",
    )(counts, mark)
    return one, two, ends


def carry_kernel(basis, bins, enter_ref, _, out_ref, held, sem):
    rows, tile = out_ref.shape
    half = enter_ref.shape[1] // tile // 2
    each = carry_rows(half, basis)
    carry = []
    for d in range(2):
        for q in range(half):
            carry.append(enter_ref[:, (d * half + q) * tile : (d * half + q + 1) * tile])
        if each > half * basis:
            carry.append(jnp.zeros((each - half * basis, tile), jnp.float32))
    held[...] = jnp.concatenate(carry, axis=0).astype(jnp.bfloat16)
    copy = pltpu.make_async_copy(held, out_ref.at[pl.ds(half * bins, 2 * each)], sem)
    copy.start()
    copy.wait()


def add_carry(enter, two, basis, bins):
    rows, tile = two.shape
    return pl.pallas_call(
        functools.partial(carry_kernel, basis, bins),
        in_specs=[VMEM, ANYWHERE],
        out_specs=ANYWHERE,
        out_shape=jax.ShapeDtypeStruct(two.shape, two.dtype),
        scratch_shapes=[
            pltpu.VMEM((rows % bins, tile), jnp.bfloat16),
            pltpu.SemaphoreType.DMA,
        ],
        input_output_aliases={1: 0},
        compiler_params=PARAMS,
        name="carry_rows",
    )(enter, two)


def ring_place(index, n):
    return jnp.where((index & 1) == 0, index >> 1, n - 1 - (index >> 1))


def code_of(row, slot, block):
    return (row * 256 + slot) * 256 + block


def plan_kernel(shape, col_ref, fill_ref, plan_ref):
    brows, slots, width, n, most = shape
    own = lax.axis_index("types")
    calls = n // 2 + 1
    tail = calls * (most + 1)
    plan_ref[tail] = lax.axis_index("tm")
    for step in range(calls):
        plan_ref[step * (most + 1)] = 0

    @pl.loop(0, brows)
    def _(row):
        fill = fill_ref[own * brows + row]
        plan_ref[tail + 1 + row] = fill

        @pl.loop(0, fill)
        def _(slot):
            column = col_ref[own * brows + row, slot]
            shift = width.bit_length() - 1
            even = width == 1 << shift
            source = column >> shift if even else lax.div(column, width)
            block = column & (width - 1) if even else lax.rem(column, width)
            ahead = ring_place(source, n) - ring_place(own, n)
            ahead = jnp.where(ahead < 0, ahead + n, ahead)
            call = jnp.minimum(ahead, n - ahead)
            down = (ahead > 0) & (ahead < n // 2)
            base = call * (most + 1)
            count = plan_ref[base] + 1
            plan_ref[base] = count
            plan_ref[base + count] = code_of(row, slot, jnp.where(down, width + block, block))

    for step in range(calls):
        base = step * (most + 1)
        count = plan_ref[base]

        @pl.when(lax.rem(count, 2) == 1)
        def _(base=base, count=count):
            plan_ref[base + count + 1] = code_of(brows, 0, 0)


def make_plan(cols, fill, dims, width, n):
    _, brows, slots, _ = dims
    most = 2 * max(2, brows * slots // n)
    return pl.pallas_call(
        functools.partial(plan_kernel, (brows, slots, width, n, most)),
        in_specs=[SMEM] * 2,
        out_specs=SMEM,
        out_shape=jax.ShapeDtypeStruct(((n // 2 + 1) * (most + 1) + 1 + brows,), jnp.int32),
        compiler_params=PARAMS,
        name="plan",
    )(cols, fill)


def start_kernel(tile, counts_ref, base_ref, total_ref):
    for row in range(total_ref.shape[0] - 1):
        at = slice(row * tile, (row + 1) * tile)
        total_ref[row] = base_ref[:, at] - counts_ref[:, at].astype(jnp.float32)
    total_ref[total_ref.shape[0] - 1] = jnp.zeros(total_ref.shape[1:], jnp.float32)


def start_total(counts, base_rate, dims):
    _, brows, _, tile = dims
    return pl.pallas_call(
        functools.partial(start_kernel, tile),
        in_specs=[VMEM, VMEM],
        out_specs=VMEM,
        out_shape=jax.ShapeDtypeStruct((brows + 1, counts.shape[0], tile), jnp.float32),
        compiler_params=PARAMS,
        name="base_less_counts",
    )(counts, base_rate)


def step_kernel(dims, n, call, groups, plan_ref, *refs):
    basis, brows, slots, tile = dims
    lag_ref, power_ref, excite_ref = refs[len(groups) : len(groups) + 3]
    total_in, states_ref, total_ref, built_ref, held, weights, sems = refs[-7:]
    bins = lag_ref.shape[1]
    half = held.shape[0] // len(groups)
    each = carry_rows(half, basis)
    most = (plan_ref.shape[0] - 1 - brows) // (n // 2 + 1) - 1
    built_ref[...] = jnp.zeros_like(built_ref)
    pairs = (plan_ref[call * (most + 1)] + 1) // 2

    def entry_at(place):
        code = plan_ref[call * (most + 1) + 1 + place]
        return code >> 16, (code >> 8) & 255, code & 255

    def weight_at(place):
        row, slot, _ = entry_at(place)
        return pltpu.make_async_copy(
            excite_ref.at[:, jnp.minimum(row, brows - 1), slot],
            weights.at[place],
            sems.at[0, place],
        )

    def copy_at(place):
        row, slot, block = entry_at(place)
        return pltpu.make_async_copy(
            held.at[block], states_ref.at[row * slots + slot], sems.at[1, place]
        )

    @pl.loop(0, 2 * pairs)
    def _(place):
        weight_at(place).start()

    total_ref[...] = total_in[...]
    for d, (carried_by, second) in enumerate(groups):
        impact_ref, carry_ref = refs[d], refs[carried_by]
        first = half * bins + second * each
        carry = carry_ref[first : first + each].astype(jnp.float32)
        for q in range(0, half, 2):
            both = jnp.concatenate(
                [impact_ref[(q + i) * bins : (q + i + 1) * bins] for i in range(2)], axis=1
            )
            for b in range(basis):
                state = jnp.dot(lag_ref[b], both, preferred_element_type=jnp.float32)
                for i in range(2):
                    row = (q + i) * basis + b
                    held[d * half + q + i, :, b * tile : (b + 1) * tile] = (
                        state[:, i * tile : (i + 1) * tile] + power_ref[b] * carry[row : row + 1]
                    ).astype(jnp.bfloat16)

    @pl.loop(0, 2 * pairs)
    def _(place):
        copy_at(place).start()

    @pl.loop(0, pairs)
    def _(k):
        terms = []
        for i in range(2):
            row, _, block = entry_at(2 * k + i)
            weight_at(2 * k + i).wait()
            weight = jnp.concatenate([weights[2 * k + i, b] for b in range(basis)], axis=1)
            term = lax.dot_general(
                held[block], weight, (((1,), (1,)), ((), ())), preferred_element_type=jnp.float32
            )
            terms.append((row, term))
        for row, term in terms:
            total_ref[row] += term

    @pl.loop(0, 2 * pairs)
    def _(place):
        copy_at(place).wait()


def take_step(call, groups, plan, arrived, lag, power, excite, states, total, dims, n):
    basis, brows, slots, tile = dims
    bins = lag.shape[1]
    half = arrived[0].shape[0] // bins
    most = (plan.shape[0] - 1 - brows) // (n // 2 + 1) - 1
    given = [total] if states is None else [states, total]
    return pl.pallas_call(
        functools.partial(step_kernel, dims, n, call, groups),
        in_specs=[SMEM] + [VMEM] * (len(groups) + 2) + [ANYWHERE] * len(given) + [VMEM],
        out_specs=[ANYWHERE, VMEM, VMEM],
        out_shape=[
            jax.ShapeDtypeStruct((brows * slots + 1, bins, basis * tile), jnp.bfloat16),
            jax.ShapeDtypeStruct(total.shape, total.dtype),
            jax.ShapeDtypeStruct((8, tile), jnp.float32),
        ],
        scratch_shapes=[
            pltpu.VMEM((len(groups) * half, bins, basis * tile), jnp.bfloat16),
            pltpu.VMEM((most, basis, tile, tile), jnp.bfloat16),
            pltpu.SemaphoreType.DMA((2, most)),
        ],
        input_output_aliases={} if states is None else {len(groups) + 4: 0},
        compiler_params=PARAMS,
        cost_estimate=pl.CostEstimate(
            flops=8 * basis * bins * bins * tile * 4,
            bytes_accessed=4 * 1024 * 1024,
            transcendentals=0,
        ),
        name="ring_step",
    )(plan, *arrived, lag, power, excite, *given)


def products(turned_ref, states_ref, plan_ref, group, dims, sent_ref, kept_ref):
    basis, brows, slots, tile = dims
    tail = plan_ref.shape[0] - 1 - brows
    part = tile // 2
    for r, row in enumerate(rows_of(group, dims)):
        fill = plan_ref[tail + 1 + row]
        for s in range(slots):
            grad = jnp.dot(
                turned_ref[row], states_ref[row * slots + s], preferred_element_type=jnp.float32
            )
            grad = jnp.where(s < fill, grad, jnp.zeros_like(grad))
            for b in range(basis):
                at = slice(b * tile, (b + 1) * tile)
                kept_ref[b, r, s] = grad[:part, at]
                sent_ref[b, r, s] = grad[part:, at].astype(sent_ref.dtype)


def rows_of(group, dims):
    count = dims[1] // GROUPS
    return range(group * count, (group + 1) * count)


def weighted_kernel(dims, overall, plan_ref, total_ref, states_ref, sent_ref, kept_ref, *refs):
    _, brows, _, tile = dims
    turned_ref, rate_sent_ref, rate_kept_ref = refs
    half = plan_ref[plan_ref.shape[0] - 1 - brows]
    part = tile // 2
    rates = []
    for row in range(brows):
        weighted = (2.0 / overall) * total_ref[row]
        rates.append(jnp.sum(weighted, axis=0, keepdims=True))
        weighted = weighted.T.astype(jnp.bfloat16)
        upper, lower = weighted[:part], weighted[part:]
        turned_ref[row, :part] = jnp.where(half == 0, upper, lower)
        turned_ref[row, part:] = jnp.where(half == 0, lower, upper)
    first_half = jnp.concatenate(rates[: brows // 2], axis=0)
    second_half = jnp.concatenate(rates[brows // 2 :], axis=0)
    rate_kept_ref[...] = jnp.where(half == 0, first_half, second_half)
    rate_sent_ref[...] = jnp.where(half == 0, second_half, first_half)
    products(turned_ref, states_ref, plan_ref, 0, dims, sent_ref, kept_ref)


def later_kernel(dims, group, plan_ref, turned_ref, states_ref, sent_ref, kept_ref):
    products(turned_ref, states_ref, plan_ref, group, dims, sent_ref, kept_ref)


def group_shape(dims, dtype):
    basis, brows, slots, tile = dims
    return jax.ShapeDtypeStruct((basis, brows // GROUPS, slots, tile // 2, tile), dtype)


def first_products(plan, total, states, dims, overall):
    _, brows, _, tile = dims
    turned = jax.ShapeDtypeStruct((brows, tile, total.shape[1]), jnp.bfloat16)
    rate = jax.ShapeDtypeStruct((brows // 2, tile), jnp.float32)
    return pl.pallas_call(
        functools.partial(weighted_kernel, dims, overall),
        in_specs=[SMEM, VMEM, VMEM],
        out_specs=[VMEM] * 5,
        out_shape=[
            group_shape(dims, jnp.bfloat16),
            group_shape(dims, jnp.float32),
            turned,
            rate,
            rate,
        ],
        compiler_params=PARAMS,
        name="weighted_products",
    )(plan, total, states)


def later_products(group, plan, turned, states, dims):
    return pl.pallas_call(
        functools.partial(later_kernel, dims, group),
        in_specs=[SMEM, VMEM, VMEM],
        out_specs=[VMEM, VMEM],
        out_shape=[group_shape(dims, jnp.bfloat16), group_shape(dims, jnp.float32)],
        compiler_params=PARAMS,
        name="products",
    )(plan, turned, states)


def add_kernel(dims, group, kept_ref, got_ref, *refs):
    basis, brows, _, _ = dims
    out_ref, held, sems = refs[-3:]
    if group == GROUPS - 1:
        rate_ref, rate_got_ref, rate_out_ref = refs[0], refs[1], refs[-4]
        out_ref, rate_out_ref = rate_out_ref, out_ref
        rate_out_ref[...] = rate_ref[...] + rate_got_ref[...]
    copies = []
    for r, row in enumerate(rows_of(group, dims)):
        for b in range(basis):
            held[b, r] = (kept_ref[b, r] + got_ref[b, r].astype(jnp.float32)).astype(jnp.bfloat16)
            copies.append(
                pltpu.make_async_copy(held.at[b, r], out_ref.at[b, row], sems.at[b, r])
            )
            copies[-1].start()
    for copy in copies:
        copy.wait()


def add_received(group, kept, got, rates, grad, dims):
    basis, brows, slots, tile = dims
    whole = jax.ShapeDtypeStruct((basis, brows, slots, tile // 2, tile), jnp.bfloat16)
    given = [] if grad is None else [grad]
    last = group == GROUPS - 1
    return pl.pallas_call(
        functools.partial(add_kernel, dims, group),
        in_specs=[VMEM] * (2 + len(rates)) + [ANYWHERE] * len(given),
        out_specs=[ANYWHERE, VMEM] if last else [ANYWHERE],
        out_shape=[whole] + ([jax.ShapeDtypeStruct(rates[0].shape, jnp.float32)] if last else []),
        scratch_shapes=[
            pltpu.VMEM(group_shape(dims, jnp.bfloat16).shape, jnp.bfloat16),
            pltpu.SemaphoreType.DMA((basis, brows // GROUPS)),
        ],
        input_output_aliases={2 + len(rates): 0} if given else {},
        compiler_params=PARAMS,
        name="add_received",
    )(kept, got, *rates, *given)


def shards(counts, mark_value, base_rate, excite, block_col, row_fill):
    dims = excite.shape[:4]
    basis, _, _, tile = dims
    bins = counts.shape[0]
    overall = bins * lax.axis_size("tm")
    n = lax.axis_size("types")
    order = list(range(0, n, 2)) + list(range(1, n, 2))[::-1]
    up = [(order[i], order[(i + 1) % n]) for i in range(n)]
    down = [(b, a) for a, b in up]
    swap = [(0, 1), (1, 0)]

    one, two, ends = impact_messages(counts, mark_value, dims, overall)
    enter = lax.ppermute(ends, "tm", [(0, 1)])
    two = add_carry(enter, two, basis, bins)
    lag, power = lag_tables(bins, basis, overall, tile)

    states = None
    built = []

    def after(value, message):
        return lax.optimization_barrier((value, message))[0]

    def step(groups, arrived):
        nonlocal states, total
        states, total, done = take_step(
            len(built), groups, plan, arrived, lag, power, excite, states, total, dims, n
        )
        built.append(done)

    def send(message, way, hop):
        if hop > 2:
            message = after(message, built[hop - 3])
        return lax.ppermute(message, "types", way)

    two_groups = ((1, 0), (1, 1))
    hops = n // 2
    at_up, at_down = [one, two], [one, two]
    for hop in range(1, hops + 1):
        if hop == 2:
            ready = (at_up[0], at_down[0], plan)
            at_up = [at_up[0], after(at_up[1], ready)]
            at_down = [at_down[0], after(at_down[1], ready)]
        if hop < hops:
            next_up, next_down = [None, None], [None, None]
            for second in range(2):
                next_up[second] = send(at_up[second], up, hop)
                next_down[second] = send(at_down[second], down, hop)
        else:
            next_up = [send(at_up[0], up, hop), None]
            next_down = [None, send(at_down[1], down, hop)]
        if hop == 1:
            cols = after(block_col, (next_up[0], next_down[0]))
            plan = make_plan(cols, row_fill, dims, counts.shape[1] // tile, n)
            total = start_total(counts, base_rate.reshape(1, -1), dims)
            total = after(total, next_up[1])
            step(two_groups, [one, two])
        else:
            step(((1, 0), (1, 1), (3, 0), (3, 1)), [*at_up, *at_down])
        at_up, at_down = next_up, next_down
    step(two_groups, [at_up[0], at_down[1]])

    out, kept, turned, rate_sent, rate_kept = first_products(plan, total, states, dims, overall)
    kept = [kept]
    got = [lax.ppermute(out, "tm", swap)]
    rate_got = lax.ppermute(rate_sent, "tm", swap)
    for group in range(1, GROUPS):
        out, more = later_products(group, plan, turned, states, dims)
        kept.append(more)
        got.append(lax.ppermute(out, "tm", swap))
    grad = None
    for group in range(GROUPS):
        rates = [rate_kept, rate_got] if group == GROUPS - 1 else []
        grad, *rate = add_received(group, kept[group], got[group], rates, grad, dims)
    return grad, rate[0].reshape(-1)


def solution(mesh):
    return jax.shard_map(
        shards,
        mesh=mesh,
        in_specs=(
            P(("parts", "tm"), "types"),
            P(("parts", "tm"), "types"),
            P("types"),
            P(None, "types", None, None, None),
            P(),
            P(),
        ),
        out_specs=(P("parts", "types", None, "tm", None), P(("parts", "types", "tm"))),
        check_vma=False,
    )
```
